32 devices in a mesh: dp: 8 (over z, y), seq: 4 (over x, core).
Axes of the slice: x: 2, y: 2, z: 4, core: 2. Of those that a mesh axis runs over, the one named last changes fastest.
Arguments:
- tokens: bfloat16 [16, 576, 768], P('dp', 'seq'), may hold values from -6 to 6
- image_lengths: int32 [16, 4], P('dp'), may hold values from 1 to 573, as said below
- grid_widths: int32 [16, 4], P('dp'), may hold values from 8 to 24
- qkv_weight: bfloat16 [768, 2304], P(('dp', 'seq')), may hold values from -0.21875 to 0.21875
- q_bias: bfloat16 [768], P(('dp', 'seq')), may hold values from -3 to 3
- v_bias: bfloat16 [768], P(('dp', 'seq')), may hold values from -3 to 3
- proj_weight: bfloat16 [768, 768], P(('dp', 'seq')), may hold values from -0.4375 to 0.4375
- proj_bias: bfloat16 [768], P(('dp', 'seq')), may hold values from -2 to 2
- fc1_weight: bfloat16 [768, 3072], P(('dp', 'seq')), may hold values from -0.21875 to 0.21875
- fc1_bias: bfloat16 [3072], P(('dp', 'seq')), may hold values from -3 to 3
- fc2_weight: bfloat16 [3072, 768], P(('dp', 'seq')), may hold values from -0.15625 to 0.15625
- fc2_bias: bfloat16 [768], P(('dp', 'seq')), may hold values from -2 to 2
- norm1_gain: bfloat16 [768], P(('dp', 'seq')), may hold values from 0.099609375 to 1.8984375
- norm1_bias: bfloat16 [768], P(('dp', 'seq')), may hold values from -2 to 2
- norm2_gain: bfloat16 [768], P(('dp', 'seq')), may hold values from 0.099609375 to 1.8984375
- norm2_bias: bfloat16 [768], P(('dp', 'seq')), may hold values from -2 to 2
- scale1: bfloat16 [768], P(('dp', 'seq')), may hold values from 0.099609375 to 1.8984375
- scale2: bfloat16 [768], P(('dp', 'seq')), may hold values from 0.099609375 to 1.8984375
- bias_table: bfloat16 [2209, 12], replicated, may hold values from -5 to 5
- out_grad: bfloat16 [16, 576, 768], P('dp', 'seq'), may hold values from -6 to 6
Outputs:
- mixed: bfloat16 [16, 576, 768], P('dp', 'seq')
- tokens_grad: bfloat16 [16, 576, 768], P('dp', 'seq')
- qkv_weight_grad: float32 [768, 2304], P(('dp', 'seq'))
- q_bias_grad: float32 [768], P(('dp', 'seq'))
- v_bias_grad: float32 [768], P(('dp', 'seq'))
- proj_weight_grad: float32 [768, 768], P(('dp', 'seq'))
- proj_bias_grad: float32 [768], P(('dp', 'seq'))
- fc1_weight_grad: float32 [768, 3072], P(('dp', 'seq'))
- fc1_bias_grad: float32 [3072], P(('dp', 'seq'))
- fc2_weight_grad: float32 [3072, 768], P(('dp', 'seq'))
- fc2_bias_grad: float32 [768], P(('dp', 'seq'))
- norm1_gain_grad: float32 [768], P(('dp', 'seq'))
- norm1_bias_grad: float32 [768], P(('dp', 'seq'))
- norm2_gain_grad: float32 [768], P(('dp', 'seq'))
- norm2_bias_grad: float32 [768], P(('dp', 'seq'))
- scale1_grad: float32 [768], P(('dp', 'seq'))
- scale2_grad: float32 [768], P(('dp', 'seq'))
- table_grad: float32 [2209, 12], replicated
The draws below stay inside these ranges and needn't reach their ends.
Inputs may be any that keep to these rules, and one draw needn't show every extreme that they name: `image_lengths`: in each row the 4 image lengths sum to at most 576; the rest of the row is padding.
All inputs are finite; a program needn't handle non-finite values.
Results may differ from the reference program's by a relative error of at most 0.014.
Values may be sent and summed in bfloat16 or wider, within the bound.
No kernel may reach another device: no remote copies, remote signals or barrier semaphores. Data moves between devices by JAX's collectives and lax.ppermute only.
A program may use at most 384 MiB of HBM per device.

```python
import math
import jax
import jax.numpy as jnp
from jax import lax

D = 768
HEADS = 12
FF = 3072
GRID = 24
ROW_LEN = 576
IMGS = 4
ROWS = 16
TABLE = 2209


def draw_image_lengths(key, part):
    key = jax.random.fold_in(key, 11)
    pick_key, small_key, pad_key, full_key = jax.random.split(key, 4)
    small = jax.random.randint(small_key, (ROWS, IMGS), 1, ROW_LEN // (6 * IMGS) + 1)
    padding = jax.random.randint(pad_key, (ROWS, 1), 0, ROW_LEN // 16 + 1)
    full_row = jax.random.randint(full_key, (), 0, ROWS)
    is_full = jnp.arange(ROWS, dtype=jnp.int32)[:, None] == full_row
    small = jnp.where(is_full, 1, small)
    padding = jnp.where(is_full, 0, padding)
    chosen = jax.random.randint(pick_key, (ROWS, 1), 0, IMGS)
    slot = jnp.arange(IMGS, dtype=jnp.int32)[None, :] == chosen
    others = jnp.sum(jnp.where(slot, 0, small), axis=1, keepdims=True)
    long_len = ROW_LEN - padding - others
    return jnp.where(slot, long_len, small).astype(jnp.int32)


def set_ends(result, own_key, smallest, top_value):
    longest = result.shape.index(max(result.shape))
    spots = []
    for shift in (0, 1):
        where = [jax.random.randint(jax.random.fold_in(own_key, axis), (), 0, length) for axis, length in enumerate(result.shape)]
        where[longest] = (where[longest] + shift) % result.shape[longest]
        spots.append(tuple(where))
    return result.at[spots[0]].set(smallest).at[spots[1]].set(top_value)


def steps_of(rng, shape, pieces, least, high):
    loudness = 1.0
    for position, blocks in pieces:
        heights = jax.random.uniform(jax.random.fold_in(jax.random.fold_in(rng, 6), position), (blocks,), jnp.float32, least / len(pieces), high / len(pieces))
        loudness = loudness * jnp.repeat(jnp.exp(heights), shape[position] // blocks).reshape((-1,) + (1,) * (len(shape) - 1 - position))
    return loudness


def gaussian(key, shape, deviation, bound, shards=(), kind=jnp.bfloat16):
    entries = deviation * jax.random.normal(key, shape, jnp.float32)
    if shards:
        entries = entries * steps_of(key, shape, shards, -0.22, 0.18)
    return jnp.clip(entries, -bound, bound).astype(kind)


def setup_inputs(seed: int = 0) -> dict:
    seeds = jax.random.split(jax.random.key(seed), 21)
    tokens = gaussian(seeds[0], (ROWS, ROW_LEN, D), 1.0, 6.0, ((0, 8), (1, 4)))
    image_lengths = draw_image_lengths(jax.random.fold_in(seeds[20], 71), 0)
    grid_widths = set_ends(jax.random.randint(seeds[2], (ROWS, IMGS), 8, GRID + 1), jax.random.fold_in(seeds[2], 1), 8, GRID).astype(jnp.int32)
    qkv_weight = gaussian(seeds[3], (D, 3 * D), D ** -0.5, 0.21875, ((0, 32),))
    q_bias = gaussian(seeds[4], (D,), 0.5, 3.0, ((0, 32),))
    v_bias = gaussian(seeds[5], (D,), 0.5, 3.0, ((0, 32),))
    proj_weight = gaussian(seeds[6], (D, D), (D // 4) ** -0.5, 0.4375, ((0, 32),))
    proj_bias = gaussian(seeds[7], (D,), 0.3, 2.0, ((0, 32),))
    fc1_weight = gaussian(seeds[8], (D, FF), D ** -0.5, 0.21875, ((0, 32),))
    fc1_bias = gaussian(seeds[9], (FF,), 0.5, 3.0, ((0, 32),))
    fc2_weight = gaussian(seeds[10], (FF, D), (FF // 2) ** -0.5, 0.15625, ((0, 32),))
    fc2_bias = gaussian(seeds[11], (D,), 0.3, 2.0, ((0, 32),))
    norm1_gain = jnp.clip(1.0 + 0.18 * jax.random.normal(seeds[12], (D,), jnp.float32), 0.099609375, 1.8984375).astype(jnp.bfloat16)
    norm1_bias = gaussian(seeds[13], (D,), 0.3, 2.0, ((0, 32),))
    norm2_gain = jnp.clip(1.0 + 0.18 * jax.random.normal(seeds[14], (D,), jnp.float32), 0.099609375, 1.8984375).astype(jnp.bfloat16)
    norm2_bias = gaussian(seeds[15], (D,), 0.3, 2.0, ((0, 32),))
    scale1 = jnp.clip(1.0 + 0.18 * jax.random.normal(seeds[16], (D,), jnp.float32), 0.099609375, 1.8984375).astype(jnp.bfloat16)
    scale2 = jnp.clip(1.0 + 0.18 * jax.random.normal(seeds[17], (D,), jnp.float32), 0.099609375, 1.8984375).astype(jnp.bfloat16)
    bias_table = gaussian(seeds[18], (TABLE, HEADS), 1.0, 5.0)
    out_grad = gaussian(seeds[19], (ROWS, ROW_LEN, D), 1.0, 6.0, ((0, 8), (1, 4)))
    return {"tokens": tokens, "image_lengths": image_lengths, "grid_widths": grid_widths, "qkv_weight": qkv_weight, "q_bias": q_bias, "v_bias": v_bias, "proj_weight": proj_weight, "proj_bias": proj_bias, "fc1_weight": fc1_weight, "fc1_bias": fc1_bias, "fc2_weight": fc2_weight, "fc2_bias": fc2_bias, "norm1_gain": norm1_gain, "norm1_bias": norm1_bias, "norm2_gain": norm2_gain, "norm2_bias": norm2_bias, "scale1": scale1, "scale2": scale2, "bias_table": bias_table, "out_grad": out_grad}


@jax.custom_vjp
def low(v):
    return lax.optimization_barrier(v.astype(jnp.bfloat16)).astype(jnp.float32)

@jax.custom_vjp
def low_back(v):
    return v

def low_keep(v):
    return (low(v), None)

def low_pass(kept, grad):
    return (grad,)

def back_keep(v):
    return (v, None)

def back_low(kept, grad):
    return (low(grad),)
low.defvjp(low_keep, low_pass)
low_back.defvjp(back_keep, back_low)
EPS = 1e-06
HIGH = lax.Precision.HIGHEST

def norm_rows(values, gain_vec, offset_vec):
    center = values - lax.optimization_barrier(jnp.mean(values, axis=-1, keepdims=True))
    spread = lax.optimization_barrier(jnp.mean(center * center, axis=-1, keepdims=True))
    return center * lax.rsqrt(spread + EPS) * gain_vec + offset_vec

def layout(lengths, widths, row_len):
    lengths = lengths.astype(jnp.int32)
    widths = widths.astype(jnp.int32)
    end_points = jnp.cumsum(lengths).astype(jnp.int32)
    starts = (end_points - lengths).astype(jnp.int32)
    places = jnp.arange(row_len, dtype=jnp.int32)
    segment = lax.optimization_barrier(jnp.sum((places[:, None] >= end_points[None, :]).astype(jnp.int32), axis=1)).astype(jnp.int32)
    member = (segment[:, None] == jnp.arange(lengths.shape[0], dtype=jnp.int32)[None, :]).astype(jnp.int32)
    offset = (places - lax.optimization_barrier(jnp.sum(member * starts[None, :], axis=1))).astype(jnp.int32)
    across = (lax.optimization_barrier(jnp.sum(member * widths[None, :], axis=1)) + (1 - lax.optimization_barrier(jnp.sum(member, axis=1))) * GRID).astype(jnp.int32)
    return (segment, (offset // across).astype(jnp.int32), (offset % across).astype(jnp.int32))

def pairs(query_side, key_side):
    segment_query, row_query, column_query = query_side
    segment_key, row_key, column_key = key_side
    allowed = segment_query[:, None] == segment_key[None, :]
    row_diff = jnp.clip(row_query[:, None] - row_key[None, :], -(GRID - 1), GRID - 1)
    table_index = (row_diff + GRID - 1) * (2 * GRID - 1) + (column_query[:, None] - column_key[None, :] + GRID - 1)
    return (allowed, table_index.astype(jnp.int32))

def forward_rows(inputs, params, allowed, table_index):
    w_qkv, b_query, b_value, w_proj, b_proj, w_up, b_up, w_down, b_down, gain_one, shift_one, gain_two, shift_two, layer_one, layer_two, rel_table = params
    row_count, row_len, model_width = inputs.shape
    head_size = model_width // HEADS
    normed = low(norm_rows(inputs, gain_one, shift_one))
    joint_qkv = jnp.einsum('rtd,de->rte', normed, w_qkv, precision=HIGH)
    queries = low_back(low((joint_qkv[..., :model_width] + b_query) * head_size ** (-0.5)))
    key_rows = low_back(low(joint_qkv[..., model_width:2 * model_width]))
    valued = low_back(low(joint_qkv[..., 2 * model_width:] + b_value))
    shape_heads = (row_count, row_len, HEADS, head_size)
    product = jnp.einsum('rqhd,rkhd->rhqk', queries.reshape(shape_heads), key_rows.reshape(shape_heads), precision=HIGH)
    offsets = jnp.moveaxis(jnp.take(rel_table.T, table_index, axis=1), 0, 1)
    scores = low_back(jnp.where(allowed[:, None], product + offsets, -1e+30))
    attention = low(jax.nn.softmax(scores, axis=-1))
    heads_out = jnp.einsum('rhqk,rkhd->rqhd', attention, valued.reshape(shape_heads), precision=HIGH)
    joined = low_back(low(heads_out.reshape(inputs.shape)))
    branch = low_back(jnp.einsum('rtd,de->rte', joined, w_proj, precision=HIGH) + b_proj)
    middle = inputs + layer_one * branch
    normed_two = low(norm_rows(middle, gain_two, shift_two))
    before = low_back(jnp.einsum('rtd,df->rtf', normed_two, w_up, precision=HIGH) + b_up)
    activated = low(jax.nn.gelu(before, approximate=False))
    down_out = low_back(jnp.einsum('rtf,fd->rtd', activated, w_down, precision=HIGH) + b_down)
    return middle + layer_two * down_out

def reference(tokens, image_lengths, grid_widths, qkv_weight, q_bias, v_bias, proj_weight, proj_bias, fc1_weight, fc1_bias, fc2_weight, fc2_bias, norm1_gain, norm1_bias, norm2_gain, norm2_bias, scale1, scale2, bias_table, out_grad):
    params = tuple((weight.astype(jnp.float32) for weight in (qkv_weight, q_bias, v_bias, proj_weight, proj_bias, fc1_weight, fc1_bias, fc2_weight, fc2_bias, norm1_gain, norm1_bias, norm2_gain, norm2_bias, scale1, scale2, bias_table)))
    group_size = math.gcd(ROWS, 4)
    blocks = ROWS // group_size

    def grouped(array):
        return array.reshape((blocks, group_size) + array.shape[1:])

    def one_block(totals, block_in):
        token_rows, grad_rows, length_rows, width_rows = block_in
        sides = jax.vmap(lambda lengths, widths: layout(lengths, widths, ROW_LEN))(length_rows, width_rows)
        allowed, table_index = jax.vmap(pairs)(sides, sides)
        outputs, pullback = jax.vjp(lambda inputs, weights: forward_rows(inputs, weights, allowed, table_index), token_rows.astype(jnp.float32), params)
        grad_inputs, grad_weights = pullback(grad_rows.astype(jnp.float32))
        totals = jax.tree.map(jnp.add, totals, grad_weights)
        return (totals, (outputs.astype(jnp.bfloat16), grad_inputs.astype(jnp.bfloat16)))
    zero_grads = jax.tree.map(jnp.zeros_like, params)
    totals, (mixed, tokens_grad) = lax.scan(one_block, zero_grads, (grouped(tokens), grouped(out_grad), grouped(image_lengths), grouped(grid_widths)))
    shape_all = (ROWS, ROW_LEN, D)
    return (mixed.reshape(shape_all), tokens_grad.reshape(shape_all), totals[0], totals[1], totals[2], totals[3], totals[4], totals[5], totals[6], totals[7], totals[8], totals[9], totals[10], totals[11], totals[12], totals[13], totals[14], totals[15])
```

```python
import functools

import jax
import jax.numpy as jnp
from jax import lax
from jax.experimental import pallas as pl
from jax.experimental.pallas import tpu as pltpu
from jax.sharding import PartitionSpec as P

GRID = 24
SIDE = 2 * GRID - 1
ROW_LEN = 576
IMGS = 4
EPS = 1e-06
STRIP = 640
BLOCKS = 11
BF = jnp.bfloat16
F32 = jnp.float32
BOTH = ("dp", "seq")


def norm_rows(values, gain_vec, offset_vec):
    center = values - jnp.mean(values, axis=-1, keepdims=True)
    spread = jnp.mean(center * center, axis=-1, keepdims=True)
    return center * lax.rsqrt(spread + EPS) * gain_vec + offset_vec


def layout(lengths, widths):
    ends = jnp.cumsum(lengths).astype(jnp.int32)
    starts = ends - lengths
    total = ends[-1]
    full = jnp.full((1,), ROW_LEN, jnp.int32)
    meta = jnp.stack(
        [
            jnp.concatenate([starts, total[None]]),
            jnp.concatenate([ends, full]),
            jnp.concatenate([starts, jnp.zeros((1,), jnp.int32)]),
            jnp.concatenate([widths, jnp.full((1,), GRID, jnp.int32)]),
        ]
    ).astype(jnp.int32)
    places = jnp.arange(ROW_LEN, dtype=jnp.int32)
    segment = jnp.sum((places[:, None] >= ends[None, :]).astype(jnp.int32), axis=1)
    return meta, segment


def strip_range(b, e):
    length = e - b
    return (STRIP - length) // 128, jnp.minimum((STRIP + length + GRID) // 128, BLOCKS - 1)


def strip_onehot(block, w, depth):
    lane = lax.broadcasted_iota(jnp.int32, (1, 128), 1) + (block * 128 - STRIP + 80 * w)
    line = jnp.floor((lane.astype(F32) + 0.5) / jnp.full((1, 128), w, jnp.int32).astype(F32)).astype(jnp.int32)
    column = lane - line * w
    level = jnp.clip(80 - line, 1 - GRID, GRID - 1) + (GRID - 1)
    code = level * GRID + column
    return (lax.broadcasted_iota(jnp.int32, (depth, 128), 0) == code).astype(F32).astype(BF)


def attn_fwd_kernel(meta, tab, q, k, v, seg_col, seg_row, p_out, o_out, strip, bias):
    heads = p_out.shape[0]
    depth = tab.shape[1]
    lane = lax.broadcasted_iota(jnp.int32, (1, 128), 1)
    for g in range(IMGS + 1):
        b, e, s, w = meta[0, g], meta[1, g], meta[2, g], meta[3, g]
        low, high = strip_range(b, e)

        def build(block, carry, w=w):
            strip[block] = jnp.dot(tab[...], strip_onehot(block, w, depth), preferred_element_type=F32)
            return carry

        lax.fori_loop(low, jnp.where(e > b, high + 1, low), build, 0)

        def line(y, carry, b=b, e=e, s=s, w=w, g=g):
            p0 = s + y * w
            off = STRIP - p0
            j0 = off // 128
            r = off - j0 * 128
            shift = (128 - r) % 128

            def part(kb, inner):
                mixed = jnp.where(lane >= r, strip[j0 + kb], strip[j0 + kb + 1])
                moved = pltpu.roll(mixed, shift, 1)
                for h in range(heads):
                    piece = moved[h * GRID : (h + 1) * GRID]
                    if g == IMGS:
                        piece = jnp.where(lane + kb * 128 >= b, piece, bias[h, kb, pl.ds(p0, GRID), :])
                    bias[h, kb, pl.ds(p0, GRID), :] = piece
                return inner

            lax.fori_loop(b // 128, (e - 1) // 128 + 1, part, 0)
            return carry

        lax.fori_loop((b - s) // w, jnp.where(e > b, (e - 1 - s) // w + 1, 0), line, 0)

    rows = 144
    half = lax.broadcasted_iota(jnp.int32, (1, 128), 1) < 64
    for t in range(heads // 2):
        cols = slice(128 * t, 128 * t + 128)

        def chunk(i, carry, t=t, cols=cols):
            r0 = pl.multiple_of(i * rows, 16)
            here = pl.ds(r0, rows)
            q_tile = q[here, cols]
            outs = []
            for sub in range(2):
                h = 2 * t + sub
                q_own = jnp.where(half if sub == 0 else ~half, q_tile, jnp.zeros_like(q_tile))
                score = lax.dot_general(q_own, k[:, cols], (((1,), (1,)), ((), ())), preferred_element_type=F32)
                offs = jnp.concatenate([bias[h, kb, here, :] for kb in range(5)], axis=1)[:, :ROW_LEN]
                score = jnp.where(seg_col[here, :] == seg_row[...], score + offs, -1e30)
                top = jnp.max(score, axis=1, keepdims=True)
                raised = jnp.exp(score - top)
                prob = (raised / jnp.sum(raised, axis=1, keepdims=True)).astype(BF)
                p_out[h, here, :] = prob
                outs.append(jnp.dot(prob, v[:, cols], preferred_element_type=F32))
            o_out[here, cols] = jnp.where(half, outs[0], outs[1]).astype(BF)
            return carry

        lax.fori_loop(0, ROW_LEN // rows, chunk, 0)


def attn_bwd_kernel(meta, q, k, v, do, p, dq_out, dk_out, dv_out, grid_out, strip, dscore, ds_low, dkt, dvt):
    heads = p.shape[0]
    depth = grid_out.shape[1]
    rows = 144
    lane = lax.broadcasted_iota(jnp.int32, (1, 128), 1)
    half = lane < 64
    for t in range(heads // 2):
        cols = slice(128 * t, 128 * t + 128)
        q_turn = jnp.transpose(q[:, cols].astype(F32)).astype(BF)
        do_turn = jnp.transpose(do[:, cols].astype(F32)).astype(BF)
        for sub in range(2):
            h = 2 * t + sub

            def chunk(i, carry, h=h, sub=sub, cols=cols):
                here = pl.ds(pl.multiple_of(i * rows, 16), rows)
                do_tile = do[here, cols]
                do_own = jnp.where(half if sub == 0 else ~half, do_tile, jnp.zeros_like(do_tile))
                d_prob = lax.dot_general(do_own, v[:, cols], (((1,), (1,)), ((), ())), preferred_element_type=F32)
                prob = p[h, here, :].astype(F32)
                weighted = prob * d_prob
                delta = jnp.sum(weighted, axis=1, keepdims=True)
                low = (weighted - prob * delta).astype(BF)
                ds_low[sub, here, :] = low
                wide = low.astype(F32)
                for kb in range(4):
                    dscore[h, kb, here, :] = wide[:, 128 * kb : 128 * kb + 128]
                dscore[h, 4, here, 0:64] = wide[:, 512:576]
                return carry

            lax.fori_loop(0, ROW_LEN // rows, chunk, 0)
            feats = slice(64 * sub, 64 * sub + 64)
            own = slice(64 * h, 64 * h + 64)
            dkt[own, :] = jnp.dot(q_turn[feats], ds_low[sub], preferred_element_type=F32)
            dvt[own, :] = jnp.dot(do_turn[feats], p[h], preferred_element_type=F32)

        def query(i, carry, cols=cols):
            here = pl.ds(pl.multiple_of(i * rows, 16), rows)
            even = jnp.dot(ds_low[0, here, :], k[:, cols], preferred_element_type=F32)
            odd = jnp.dot(ds_low[1, here, :], k[:, cols], preferred_element_type=F32)
            dq_out[here, cols] = jnp.where(half, even, odd).astype(BF)
            return carry

        lax.fori_loop(0, ROW_LEN // rows, query, 0)
        dk_out[:, cols] = jnp.transpose(dkt[128 * t : 128 * t + 128, :]).astype(BF)
        dv_out[:, cols] = jnp.transpose(dvt[128 * t : 128 * t + 128, :]).astype(BF)

    grid_out[...] = jnp.zeros_like(grid_out)
    dscore[:, :, ROW_LEN:, :] = jnp.zeros(dscore.shape[:2] + (dscore.shape[2] - ROW_LEN, 128), F32)
    column = lax.broadcasted_iota(jnp.int32, (GRID, 128), 0)
    for g in range(IMGS + 1):
        b, e, s, w = meta[0, g], meta[1, g], meta[2, g], meta[3, g]
        low, high = strip_range(b, e)
        stop = jnp.where(e > b, high + 1, low)

        def clear(block, carry):
            strip[block] = jnp.zeros(strip.shape[1:], F32)
            return carry

        lax.fori_loop(low, stop, clear, 0)

        def line(y, carry, b=b, e=e, s=s, w=w):
            p0 = s + y * w
            off = STRIP - p0
            j0 = off // 128
            r = off - j0 * 128

            def part(kb, inner):
                place = lane + kb * 128
                keep = (column < w) & (place >= b) & (place < e)
                for h in range(heads):
                    rows_h = slice(h * GRID, (h + 1) * GRID)
                    piece = jnp.where(keep, dscore[h, kb, pl.ds(p0, GRID), :], 0.0)
                    moved = pltpu.roll(piece, r, 1)
                    strip[j0 + kb, rows_h, :] += jnp.where(lane >= r, moved, 0.0)
                    strip[j0 + kb + 1, rows_h, :] += jnp.where(lane >= r, 0.0, moved)
                return inner

            lax.fori_loop(b // 128, (e - 1) // 128 + 1, part, 0)
            return carry

        lax.fori_loop((b - s) // w, jnp.where(e > b, (e - 1 - s) // w + 1, 0), line, 0)

        def fold(block, carry, w=w):
            grid_out[...] += lax.dot_general(
                strip[block].astype(BF),
                strip_onehot(block, w, depth),
                (((1,), (1,)), ((), ())),
                preferred_element_type=F32,
            )
            return carry

        lax.fori_loop(low, stop, fold, 0)


def vmem():
    return pl.BlockSpec(memory_space=pltpu.VMEM)


def attn_fwd(meta, tab, q, k, v, segment):
    heads = tab.shape[0] // GRID
    return pl.pallas_call(
        attn_fwd_kernel,
        out_shape=(
            jax.ShapeDtypeStruct((heads, ROW_LEN, ROW_LEN), BF),
            jax.ShapeDtypeStruct(q.shape, BF),
        ),
        in_specs=[pl.BlockSpec(memory_space=pltpu.SMEM)] + [vmem()] * 6,
        out_specs=(vmem(), vmem()),
        scratch_shapes=[
            pltpu.VMEM((BLOCKS, heads * GRID, 128), F32),
            pltpu.VMEM((heads, 5, ROW_LEN + 32, 128), F32),
        ],
        compiler_params=pltpu.CompilerParams(vmem_limit_bytes=48 * 1024 * 1024),
        cost_estimate=pl.CostEstimate(flops=2_000_000_000, bytes_accessed=8_000_000, transcendentals=2_000_000),
        name="attn_fwd",
    )(meta, tab, q, k, v, segment[:, None], segment[None, :])


def attn_bwd(meta, q, k, v, do, p, depth):
    heads = p.shape[0]
    low = jax.ShapeDtypeStruct(q.shape, BF)
    return pl.pallas_call(
        attn_bwd_kernel,
        out_shape=(low, low, low, jax.ShapeDtypeStruct((heads * GRID, depth), F32)),
        in_specs=[pl.BlockSpec(memory_space=pltpu.SMEM)] + [vmem()] * 5,
        out_specs=(vmem(),) * 4,
        scratch_shapes=[
            pltpu.VMEM((BLOCKS, heads * GRID, 128), F32),
            pltpu.VMEM((heads, 5, ROW_LEN + 32, 128), F32),
            pltpu.VMEM((2, ROW_LEN, ROW_LEN), BF),
            pltpu.VMEM((heads * 64, ROW_LEN), F32),
            pltpu.VMEM((heads * 64, ROW_LEN), F32),
        ],
        compiler_params=pltpu.CompilerParams(vmem_limit_bytes=48 * 1024 * 1024),
        cost_estimate=pl.CostEstimate(flops=5_000_000_000, bytes_accessed=8_000_000, transcendentals=0),
        name="attn_bwd",
    )(meta, q, k, v, do, p)


def reorder_kernel(to_out, places, src, dst):
    for i in range(16):
        j = places[i]
        if to_out:
            dst[j] = src[i]
        else:
            dst[i] = src[j]


def reorder(blocks, places, to_out):
    size = blocks.size * 2
    return pl.pallas_call(
        functools.partial(reorder_kernel, to_out),
        out_shape=jax.ShapeDtypeStruct(blocks.shape, blocks.dtype),
        in_specs=[pl.BlockSpec(memory_space=pltpu.SMEM), vmem()],
        out_specs=vmem(),
        compiler_params=pltpu.CompilerParams(vmem_limit_bytes=16 * 1024 * 1024),
        cost_estimate=pl.CostEstimate(flops=0, bytes_accessed=2 * size, transcendentals=0),
        name="reorder",
    )(places, blocks)


class Net:
    def __init__(self, dp, seq):
        self.dp, self.seq = dp, seq
        self.fast = dp == 8
        at_seq = lax.axis_index("seq")
        self.core = at_seq % 2
        self.x = at_seq // 2
        at_dp = lax.axis_index("dp")

        def table(fn):
            pairs = []
            for d in range(dp):
                for s in range(seq):
                    d2, s2 = fn(d, s)
                    pairs.append((d * seq + s, d2 * seq + s2))
            return pairs

        self.to_core = table(lambda d, s: (d, s ^ 1))
        self.to_x = table(lambda d, s: (d, s ^ 2))
        if self.fast:
            self.phases = (
                table(lambda d, s: (d ^ 4, s)),
                table(lambda d, s: (d ^ 2, s)),
                table(lambda d, s: (d, s ^ 2) if s % 2 == 0 else (d ^ 1, s)),
                table(lambda d, s: (d ^ 1, s) if s % 2 == 0 else (d, s ^ 2)),
            )
            rel = jnp.arange(16, dtype=jnp.int32)
            d1, d2, d3, d4 = rel % 2, (rel // 2) % 2, (rel // 4) % 2, rel // 8
            by_x = jnp.where(self.core == 0, d3, d4)
            by_y = jnp.where(self.core == 0, d4, d3)
            self.places = ((at_dp * 2 + self.x) ^ (d1 * 8 + d2 * 4 + by_y * 2 + by_x)).astype(jnp.int32)

    def send(self, array, pairs):
        return lax.ppermute(array, BOTH, pairs)

    def by_core(self, own, other, axis):
        first = self.core == 0
        return jnp.stack([jnp.where(first, own, other), jnp.where(first, other, own)], axis=axis)

    def pick(self, array, index, axis):
        return lax.dynamic_index_in_dim(array, index, axis, keepdims=False)

    def gather(self, block):
        if self.fast:
            for pairs in self.phases:
                block = jnp.stack([block, self.send(block, pairs)])
            shape = block.shape[4:]
            return reorder(block.reshape((16,) + shape), self.places, True).reshape((self.dp, 2) + shape)
        block = lax.all_gather(block, "dp", axis=0)
        other = self.send(block, self.to_x)
        first = self.x == 0
        return jnp.stack([jnp.where(first, block, other), jnp.where(first, other, block)], axis=1)

    def reduce(self, blocks):
        shape = blocks.shape[2:]
        if self.fast:
            blocks = reorder(blocks.reshape((16,) + shape), self.places, False)
            for step in (3, 2, 1, 0):
                blocks = blocks.reshape((2, 2**step) + shape)
                came = self.send(blocks[1], self.phases[step])
                blocks = blocks[0].astype(F32) + came.astype(F32)
                if step:
                    blocks = blocks.astype(BF)
            return blocks.reshape(shape)
        came = self.send(self.pick(blocks, 1 - self.x, 1), self.to_x)
        summed = self.pick(blocks, self.x, 1).astype(F32) + came.astype(F32)
        return lax.psum_scatter(summed, "dp", scatter_dimension=0, tiled=False)

    def total(self, array):
        if self.fast:
            for pairs in self.phases:
                array = array + self.send(array, pairs)
            return array
        array = array + self.send(array, self.to_x)
        return lax.psum(array, "dp")


def wide(array):
    return array.astype(F32)


def dot(a, b):
    return jnp.dot(a, b, preferred_element_type=F32)


def dot_t(a, b):
    return lax.dot_general(a, b, (((0,), (0,)), ((), ())), preferred_element_type=F32)


def dot_r(a, b):
    return lax.dot_general(a, b, (((1,), (1,)), ((), ())), preferred_element_type=F32)


def local(
    dp,
    seq,
    tokens,
    image_lengths,
    grid_widths,
    qkv_weight,
    q_bias,
    v_bias,
    proj_weight,
    proj_bias,
    fc1_weight,
    fc1_bias,
    fc2_weight,
    fc2_bias,
    norm1_gain,
    norm1_bias,
    norm2_gain,
    norm2_bias,
    scale1,
    scale2,
    bias_table,
    out_grad,
):
    net = Net(dp, seq)
    core, at_x = net.core, net.x
    row_count, shard, width = tokens.shape
    heads = bias_table.shape[1]
    own_heads = heads // 2
    own_feats = width // 2
    scale = (width // heads) ** (-0.5)
    n_dev = dp * seq
    rows_w = width // n_dev
    ff = fc2_weight.shape[0] * n_dev
    rows_f = ff // n_dev
    chips = n_dev // 2

    small = [q_bias, v_bias, proj_bias, fc2_bias, norm1_gain, norm1_bias, norm2_gain, norm2_bias, scale1, scale2, fc1_bias]
    small = jnp.concatenate(small)
    n_small = small.shape[0]
    pack_rows = -(-(rows_w + 1) // 16) * 16
    pack = jnp.concatenate(
        [proj_weight, jnp.pad(small, (0, width - n_small))[None], jnp.zeros((pack_rows - rows_w - 1, width), BF)]
    )
    qkv_view = qkv_weight.reshape(rows_w, 3, 2, own_feats)
    qkv_block = net.by_core(
        net.pick(qkv_view, core, 2), net.send(net.pick(qkv_view, 1 - core, 2), net.to_core), 0
    ).reshape(2 * rows_w, 3 * own_feats)
    fc1_view = fc1_weight.reshape(rows_w, chips, 2, rows_f)
    fc1_block = net.by_core(
        net.pick(fc1_view, core, 2), net.send(net.pick(fc1_view, 1 - core, 2), net.to_core), 0
    ).reshape(2 * rows_w, ff // 2)

    pack_all = net.gather(pack)
    w_qkv = net.gather(qkv_block).reshape(width, 3 * own_feats)
    pack_all = net.by_core(pack_all, net.send(pack_all, net.to_core), 2)
    w_proj = pack_all[:, :, :, :rows_w].reshape(width, width)
    vectors = pack_all[:, :, :, rows_w, :n_small]
    whole = [vectors[..., j * rows_w : (j + 1) * rows_w].reshape(width) for j in range(10)]
    b_query, b_value, b_proj, b_down, gain_one, shift_one, gain_two, shift_two, layer_one, layer_two = [wide(a) for a in whole]
    b_up = wide(net.pick(vectors[..., 10 * rows_w :], core, 2).reshape(ff // 2))
    b_query = lax.dynamic_slice_in_dim(b_query, core * own_feats, own_feats)
    b_value = lax.dynamic_slice_in_dim(b_value, core * own_feats, own_feats)
    w_up = net.gather(fc1_block).reshape(width, ff // 2)
    w_down = net.gather(fc2_weight).reshape(ff // 2, width)

    def to_own(array):
        mine, theirs = net.pick(array, at_x, 0), net.pick(array, 1 - at_x, 0)
        came = net.send(theirs, net.to_x)
        first = at_x == 0
        return jnp.stack([jnp.where(first, mine, came), jnp.where(first, came, mine)])

    def to_home(array):
        mine = net.pick(array, at_x, 0)
        came = net.send(net.pick(array, 1 - at_x, 0), net.to_x)
        first = at_x == 0
        return jnp.stack([jnp.where(first, mine, came), jnp.where(first, came, mine)])

    def whole_row(array):
        other = net.send(array, net.to_core)
        return net.by_core(array, other, 1).reshape(ROW_LEN, array.shape[-1])

    def own_sum(array):
        view = array.reshape(2, 2, shard, array.shape[-1])
        came = net.send(net.pick(view, 1 - core, 1).astype(BF), net.to_core)
        return net.pick(view, core, 1) + came.astype(F32)

    lengths = net.pick(image_lengths, at_x, 0)
    widths = net.pick(grid_widths, at_x, 0)
    meta, segment = layout(lengths, widths)

    steps = jnp.arange(GRID)
    spread = (steps[:, None, None] - steps[None, :, None] + GRID - 1 == jnp.arange(SIDE)[None, None, :]).astype(BF)
    depth = -(-SIDE * GRID // 128) * 128
    cube = lax.dynamic_slice_in_dim(bias_table.reshape(SIDE, SIDE, heads), core * own_heads, own_heads, 2)
    tab = jnp.einsum("abh,ckb->hcak", cube, spread, preferred_element_type=F32).astype(BF)
    tab = jnp.pad(tab.reshape(own_heads * GRID, SIDE * GRID), ((0, 0), (0, depth - SIDE * GRID)))

    inputs = wide(to_own(tokens))
    upstream = wide(to_own(out_grad))

    normed, norm_one_pull = jax.vjp(norm_rows, inputs, gain_one, shift_one)
    h1 = whole_row(normed.astype(BF))
    joint = dot(h1, w_qkv)
    q = ((joint[:, :own_feats] + b_query) * scale).astype(BF)
    k = joint[:, own_feats : 2 * own_feats].astype(BF)
    v = (joint[:, 2 * own_feats :] + b_value).astype(BF)
    prob, mixed_heads = attn_fwd(meta, tab, q, k, v, segment)

    view = mixed_heads.reshape(2, 2, shard, own_feats)
    came = net.send(net.pick(view, 1 - core, 1), net.to_core)
    joined = net.by_core(net.pick(view, core, 1), came, 2).reshape(2 * shard, width)
    branch = (dot(joined, w_proj) + b_proj).reshape(2, shard, width)
    middle = inputs + layer_one * branch
    normed_two, norm_two_pull = jax.vjp(norm_rows, middle, gain_two, shift_two)
    h2 = whole_row(normed_two.astype(BF))
    before = dot(h2, w_up) + b_up
    activated, gelu_pull = jax.vjp(lambda hidden: jax.nn.gelu(hidden, approximate=False), before)
    act_low = activated.astype(BF)
    after = own_sum(dot(act_low, w_down)) + b_down
    mixed = to_home((middle + layer_two * after).astype(BF))

    d_layer_two = jnp.sum(upstream * after, axis=(0, 1))
    d_after_own = (layer_two * upstream).astype(BF)
    d_b_down = jnp.sum(wide(d_after_own), axis=(0, 1))
    d_after = whole_row(d_after_own)
    d_w_down = dot_t(act_low, d_after).astype(BF)
    g_down = net.reduce(d_w_down.reshape(dp, 2, rows_f, width))
    d_before = gelu_pull(dot_r(d_after, w_down))[0].astype(BF)
    d_b_up = jnp.sum(wide(d_before), axis=0)
    d_w_up = dot_t(h2, d_before).astype(BF)
    g_up = net.reduce(d_w_up.reshape(dp, 2, 2 * rows_w, ff // 2))
    d_h2 = own_sum(dot_r(d_before, w_up))
    d_middle_in, d_gain_two, d_shift_two = norm_two_pull(d_h2)
    d_middle = upstream + d_middle_in
    d_layer_one = jnp.sum(d_middle * branch, axis=(0, 1))
    d_branch = (layer_one * d_middle).astype(BF).reshape(2 * shard, width)
    d_b_proj = jnp.sum(wide(d_branch), axis=0)
    d_w_proj = dot_t(joined, d_branch).astype(BF)
    d_joined = dot_r(d_branch, w_proj).astype(BF).reshape(2, shard, 2, own_feats)
    came = net.send(net.pick(d_joined, 1 - core, 2), net.to_core)
    d_heads = net.by_core(net.pick(d_joined, core, 2), came, 1).reshape(ROW_LEN, own_feats)

    dq, dk, dv, grid = attn_bwd(meta, q, k, v, d_heads, prob, depth)
    grid = grid[:, : SIDE * GRID].reshape(own_heads, GRID, SIDE, GRID)
    table = jnp.einsum("hcak,ckb->hab", grid, wide(spread), precision=lax.Precision.HIGHEST)
    table = table.reshape(own_heads * SIDE * SIDE)
    pad = -table.shape[0] % 1024
    table_sum = net.total(jnp.pad(table, (0, pad)).reshape(-1, 128)).reshape(-1)[: table.shape[0]]
    table_sum = table_sum.reshape(own_heads, SIDE * SIDE)
    table_sum = net.by_core(table_sum, net.send(table_sum, net.to_core), 0).reshape(heads, SIDE * SIDE)
    table_grad = jnp.transpose(table_sum)

    dq_scaled = wide(dq) * scale
    d_b_query = jnp.sum(dq_scaled, axis=0)
    d_b_value = jnp.sum(wide(dv), axis=0)
    d_joint = jnp.concatenate([dq_scaled.astype(BF), dk, dv], axis=1)
    d_w_qkv = dot_t(h1, d_joint).astype(BF)
    g_qkv = net.reduce(d_w_qkv.reshape(dp, 2, 2 * rows_w, 3 * own_feats))
    d_h1 = own_sum(dot_r(d_joint, w_qkv))
    d_inputs_in, d_gain_one, d_shift_one = norm_one_pull(d_h1)
    tokens_grad = to_home((d_middle + d_inputs_in).astype(BF))

    def placed(part):
        return lax.dynamic_update_slice_in_dim(jnp.zeros((width,), F32), part, core * own_feats, 0)

    parts = [placed(d_b_query), placed(d_b_value), d_b_proj, d_b_down, d_gain_one, d_shift_one, d_gain_two, d_shift_two, d_layer_one, d_layer_two]
    parts = [a.reshape(dp, 2, 2, rows_w) for a in parts]
    up = d_b_up.reshape(dp, 2, 1, rows_f)
    mine = (jnp.arange(2) == core)[None, None, :, None]
    parts.append(jnp.where(mine, up, 0.0))
    parts = jnp.concatenate(parts, axis=-1).astype(BF)
    parts = jnp.pad(parts, ((0, 0), (0, 0), (0, 0), (0, width - n_small)))[:, :, :, None]
    fill = jnp.zeros((dp, 2, 2, pack_rows - rows_w - 1, width), BF)
    d_pack = jnp.concatenate([d_w_proj.reshape(dp, 2, 2, rows_w, width), parts, fill], axis=3)
    came = net.send(net.pick(d_pack, 1 - core, 2), net.to_core)
    g_pack = net.reduce((wide(net.pick(d_pack, core, 2)) + wide(came)).astype(BF))
    g_proj = g_pack[:rows_w]
    g_small = g_pack[rows_w, :n_small]
    smalls = [g_small[j * rows_w : (j + 1) * rows_w] for j in range(10)] + [g_small[10 * rows_w :]]

    def home(block, groups, cols):
        view = block.reshape(2, rows_w, groups, cols)
        came = net.send(net.pick(view, 1 - core, 0), net.to_core)
        return net.by_core(net.pick(view, core, 0), came, 2).reshape(rows_w, groups * 2 * cols)

    g_qkv = home(g_qkv, 3, own_feats)
    g_up = home(g_up, chips, rows_f)
    g_query, g_value, g_bproj, g_bdown, g_gain1, g_shift1, g_gain2, g_shift2, g_layer1, g_layer2, g_bup = smalls
    return (
        mixed,
        tokens_grad,
        g_qkv,
        g_query,
        g_value,
        g_proj,
        g_bproj,
        g_up,
        g_bup,
        g_down,
        g_bdown,
        g_gain1,
        g_shift1,
        g_gain2,
        g_shift2,
        g_layer1,
        g_layer2,
        table_grad,
    )


def solution(mesh):
    both = P(BOTH)
    both2 = P(BOTH, None)
    act = P("dp", "seq", None)
    in_specs = (act, P("dp", None), P("dp", None), both2, both, both, both2, both, both2, both, both2)
    in_specs += (both,) * 7 + (P(), act)
    out_specs = (act, act, both2, both, both, both2, both, both2, both, both2) + (both,) * 7 + (P(),)
    body = functools.partial(local, mesh.shape["dp"], mesh.shape["seq"])
    return jax.shard_map(body, mesh=mesh, in_specs=in_specs, out_specs=out_specs, check_vma=False)
```

```python
import functools

import jax
import jax.numpy as jnp
from jax import lax
from jax.experimental import pallas as pl
from jax.experimental.pallas import tpu as pltpu
from jax.sharding import PartitionSpec as P

GRID = 24
SIDE = 2 * GRID - 1
ROW_LEN = 576
IMGS = 4
EPS = 1e-06
STRIP = 640
BLOCKS = 12
DEPTH = 1152
FLAT = 2304
BF = jnp.bfloat16
F32 = jnp.float32
BOTH = ("dp", "seq")
VECS = ("q", "v", "b_proj", "b_down", "gain1", "shift1", "gain2", "shift2", "scale1", "scale2")


def layout(lengths, widths):
    ends = jnp.cumsum(lengths).astype(jnp.int32)
    starts = ends - lengths
    total = ends[-1]
    full = jnp.full((1,), ROW_LEN, jnp.int32)
    meta = jnp.stack(
        [
            jnp.concatenate([starts, total[None]]),
            jnp.concatenate([ends, full]),
            jnp.concatenate([starts, jnp.zeros((1,), jnp.int32)]),
            jnp.concatenate([widths, jnp.full((1,), GRID, jnp.int32)]),
        ]
    ).astype(jnp.int32)
    places = jnp.arange(ROW_LEN, dtype=jnp.int32)
    segment = jnp.sum((places[:, None] >= ends[None, :]).astype(jnp.int32), axis=1)
    return meta, segment


def strip_range(b, e):
    length = e - b
    return (STRIP - length) // 256, jnp.minimum((STRIP + length + GRID) // 256, BLOCKS // 2 - 1)


def strip_onehot(pair, w, depth):
    lane = lax.broadcasted_iota(jnp.int32, (1, 256), 1) + (pair * 256 - STRIP + 80 * w)
    line = jnp.floor((lane.astype(F32) + 0.5) / jnp.full((1, 256), w, jnp.int32).astype(F32)).astype(jnp.int32)
    column = lane - line * w
    level = jnp.clip(80 - line, 1 - GRID, GRID - 1) + (GRID - 1)
    code = (GRID - 1 - column) * SIDE + level
    return (lax.broadcasted_iota(jnp.int32, (depth, 256), 0) == code).astype(F32).astype(BF)


def segment_loops(meta, g):
    b, e, s, w = meta[0, g], meta[1, g], meta[2, g], meta[3, g]
    low, high = strip_range(b, e)
    stop = jnp.where(e > b, high + 1, low)
    first, last = (b - s) // w, jnp.where(e > b, (e - 1 - s) // w + 1, 0)
    return b, e, s, w, low, stop, first, last, (w + 7) // 8


def bias_kernel(meta, flat, seg_col, seg_row, *refs):
    outs, (tab, strip, bias) = refs[:-3], refs[-3:]
    heads = bias.shape[0]
    depth = tab.shape[1]
    lane = lax.broadcasted_iota(jnp.int32, (1, 128), 1)
    for c in range(GRID):
        moved = flat[:, SIDE * c : SIDE * c + depth]
        for h in range(heads):
            row = (c // 8 * heads + h) * 8 + c % 8
            tab[row : row + 1, :] = moved[h : h + 1]
    low_tab = tab[...].astype(BF)
    for g in range(IMGS + 1):
        b, e, s, w, low, stop, first, last, groups = segment_loops(meta, g)

        def build(pair, carry, w=w):
            made = jnp.dot(low_tab, strip_onehot(pair, w, depth), preferred_element_type=F32)
            for n in range(3):
                rows_n = slice(n * heads * 8, (n + 1) * heads * 8)
                strip[n, 2 * pair] = made[rows_n, :128]
                strip[n, 2 * pair + 1] = made[rows_n, 128:]
            return carry

        lax.fori_loop(low, stop, build, 0)

        for size in range(1, 4):

            def line(y, carry, b=b, s=s, w=w, g=g, size=size):
                p0 = s + y * w
                off = STRIP - p0
                j0 = off // 128
                r = off - j0 * 128
                shift = (128 - r) % 128
                for n in range(size):
                    here = pl.ds(p0 + 8 * n, 8)
                    parts = [strip[n, j0 + kb] for kb in range(6)]
                    for kb in range(5):
                        moved = pltpu.roll(jnp.where(lane >= r, parts[kb], parts[kb + 1]), shift, 1)
                        for h in range(heads):
                            piece = moved[h * 8 : (h + 1) * 8]
                            if g == IMGS:
                                piece = jnp.where(lane + kb * 128 >= b, piece, bias[h, kb, here, :])
                            bias[h, kb, here, :] = piece
                return carry

            lax.fori_loop(first, jnp.where(groups == size, last, first), line, 0)

    rows = 144

    def mask(i, carry):
        here = pl.ds(pl.multiple_of(i * rows, 16), rows)
        allowed = seg_col[here, :] == seg_row[...]
        for h in range(heads):
            offs = jnp.concatenate([bias[h, kb, here, :] for kb in range(5)], axis=1)[:, :ROW_LEN]
            outs[h // 2][h % 2, here, :] = jnp.where(allowed, offs, -1e30).astype(BF)
        return carry

    lax.fori_loop(0, ROW_LEN // rows, mask, 0)


def norm_parts(x):
    center = x - jnp.mean(x, axis=-1, keepdims=True)
    inverse = lax.rsqrt(jnp.mean(center * center, axis=-1, keepdims=True) + EPS)
    return center * inverse, inverse


def norm_back(normed, inverse, grad, gain):
    pulled = grad * gain
    mean = jnp.mean(pulled, axis=-1, keepdims=True)
    along = jnp.mean(pulled * normed, axis=-1, keepdims=True)
    return (pulled - mean - normed * along) * inverse


def vec(vecs, name):
    return vecs[VECS.index(name) : VECS.index(name) + 1, :].astype(F32)


def own_half(core, row):
    n = row.shape[1] // 2
    return jnp.where(core == 0, row[:, :n], row[:, n:])


def split_kernel(flags, w, keep, give):
    core = flags[0]
    n = w.shape[1] // 6
    for j in range(3):
        low, high = w[:, 2 * n * j : 2 * n * j + n], w[:, 2 * n * j + n : 2 * n * j + 2 * n]
        keep[:, n * j : n * j + n] = jnp.where(core == 0, low, high)
        give[:, n * j : n * j + n] = jnp.where(core == 0, high, low)


def stack_kernel(flags, own, came, out):
    core = flags[0]
    rows = own.shape[0]
    first = core == 0
    out[:rows] = jnp.where(first, own[...], came[...])
    out[rows:] = jnp.where(first, came[...], own[...])


def start_kernel(flags, tokens, out_grad, came, both):
    x = flags[1]
    both[0, x] = tokens[x]
    both[1, x] = out_grad[x]
    both[0, 1 - x] = came[0]
    both[1, 1 - x] = came[1]


def attn_fwd_kernel(first, t, flags, *refs):
    core = flags[0]
    if first:
        own, came, w, vecs, bias, q, k, v, p_out, keep, give, h1, joined = refs
        shard = own.shape[2]
        for a in range(2):
            for side, part in ((core, own), (1 - core, came)):
                normed, _ = norm_parts(part[0, a].astype(F32))
                normed = normed * vec(vecs, "gain1") + vec(vecs, "shift1")
                h1[pl.ds(pl.multiple_of((2 * a + side) * shard, 16), shard), :] = normed.astype(BF)
    else:
        h1, w, vecs, bias, q, k, v, p_out, keep, give, joined = refs
        shard = keep.shape[1]
    feats = w.shape[2] // 3
    cols = slice(128 * t, 128 * t + 128)

    def weight(j):
        return w[:, :, feats * j + 128 * t : feats * j + 128 * t + 128].reshape(h1.shape[1], 128)

    q_row, v_row = own_half(core, vec(vecs, "q"))[:, cols], own_half(core, vec(vecs, "v"))[:, cols]
    q[...] = ((jnp.dot(h1[...], weight(0), preferred_element_type=F32) + q_row) * 64**-0.5).astype(BF)
    k[...] = jnp.dot(h1[...], weight(1), preferred_element_type=F32).astype(BF)
    v[...] = (jnp.dot(h1[...], weight(2), preferred_element_type=F32) + v_row).astype(BF)
    rows = 144
    half = lax.broadcasted_iota(jnp.int32, (1, 128), 1) < 64

    def chunk(i, carry):
        here = pl.ds(pl.multiple_of(i * rows, 16), rows)
        q_tile = q[here, :]
        outs = []
        for sub in range(2):
            q_own = jnp.where(half if sub == 0 else ~half, q_tile, jnp.zeros_like(q_tile))
            score = lax.dot_general(q_own, k[...], (((1,), (1,)), ((), ())), preferred_element_type=F32)
            score = score + bias[sub, here, :].astype(F32)
            raised = jnp.exp(score - jnp.max(score, axis=1, keepdims=True))
            prob = (raised * (1.0 / jnp.sum(raised, axis=1, keepdims=True))).astype(BF)
            p_out[sub, here, :] = prob
            outs.append(jnp.dot(prob, v[...], preferred_element_type=F32))
        joined[here, :] = jnp.where(half, outs[0], outs[1]).astype(BF)
        return carry

    lax.fori_loop(0, ROW_LEN // rows, chunk, 0)
    for a in range(2):
        keep[a] = joined[pl.ds(pl.multiple_of((2 * a + core) * shard, 16), shard), :]
        give[a] = joined[pl.ds(pl.multiple_of((2 * a + 1 - core) * shard, 16), shard), :]


def by_core_in(core, own, came):
    return jnp.concatenate([jnp.where(core == 0, own, came), jnp.where(core == 0, came, own)], axis=-1)


def proj_kernel(flags, *refs):
    keeps, cames = refs[:3], refs[3:6]
    w_own, w_came, own, grads_came, vecs, joined, branch, middle, h2, d_after = refs[6:]
    core = flags[0]
    width = own.shape[-1]
    shard = own.shape[2]
    feats = width // 2
    for a in range(2):
        keep = jnp.concatenate([part[a] for part in keeps], axis=-1)
        came = jnp.concatenate([part[a] for part in cames], axis=-1)
        joined[a] = by_core_in(core, keep, came)
    weight = by_core_in(core, w_own[...].reshape(width, feats), w_came[...].reshape(width, feats))
    for a in range(2):
        out = jnp.dot(joined[a], weight, preferred_element_type=F32) + vec(vecs, "b_proj")
        branch[a] = out.astype(BF)
        mid = own[0, a].astype(F32) + vec(vecs, "scale1") * out
        middle[a] = mid
        for j, part in enumerate((own, grads_came)):
            here = slice((2 * j + a) * shard, (2 * j + a + 1) * shard)
            d_after[here, :] = (vec(vecs, "scale2") * part[1, a].astype(F32)).astype(BF)
        normed, _ = norm_parts(mid)
        h2[a] = (normed * vec(vecs, "gain2") + vec(vecs, "shift2")).astype(BF)


def after_kernel(flags, act, w, keep, give):
    n = keep.shape[0]
    keep[...] = jnp.dot(act[:n], w[...], preferred_element_type=F32)
    give[...] = jnp.dot(act[n:], w[...], preferred_element_type=F32).astype(BF)


def mixed_kernel(flags, keep, came, middle, own, d_after, vecs, mixed, sums):
    rows = middle.shape[0] * middle.shape[1]
    width = middle.shape[2]
    out = keep[...] + came[...].astype(F32) + vec(vecs, "b_down")
    mid = middle[...].reshape(rows, width)
    mixed[...] = (mid + vec(vecs, "scale2") * out).astype(BF).reshape(mixed.shape)
    g = own[1].reshape(rows, width).astype(F32)
    sums[0:1, :] = jnp.sum(g * out, axis=0, keepdims=True)
    sums[1:2, :] = jnp.sum(d_after[:rows].astype(F32), axis=0, keepdims=True)


def hidden_back_kernel(flags, d_after, w_down, slope, w_up, d_before, b_sum, keep, give, total):
    i = pl.program_id(0)
    width = w_up.shape[0]
    d_act = lax.dot_general(d_after[...], w_down[...], (((1,), (1,)), ((), ())), preferred_element_type=F32)
    low = (d_act * slope[...].astype(F32)).astype(BF)
    d_before[...] = low
    b_sum[...] = jnp.sum(low.astype(F32), axis=0, keepdims=True)
    d_h2 = lax.dot_general(low, w_up[...], (((1,), (1,)), ((), ())), preferred_element_type=F32)

    @pl.when(i == 0)
    def _():
        total[...] = d_h2

    @pl.when(i > 0)
    def _():
        total[...] += d_h2

    @pl.when(i == pl.num_programs(0) - 1)
    def _():
        n = keep.shape[0]
        keep[...] = total[:n]
        give[...] = total[n:].astype(BF)


def middle_back_kernel(flags, keep_in, came, middle, own, branch, w_own, w_came, vecs, d_middle, d_branch, keep, give, sums):
    core = flags[0]
    width = middle.shape[-1]
    shard = middle.shape[1]
    weight = by_core_in(core, w_own[...].reshape(width, width // 2), w_came[...].reshape(width, width // 2))
    total = [jnp.zeros((1, width), F32)] * 4
    for a in range(2):
        here = slice(a * shard, a * shard + shard)
        normed, inverse = norm_parts(middle[a])
        d_h2 = keep_in[here, :] + came[here, :].astype(F32)
        d_mid = own[1, a].astype(F32) + norm_back(normed, inverse, d_h2, vec(vecs, "gain2"))
        d_middle[a] = d_mid
        low = (vec(vecs, "scale1") * d_mid).astype(BF)
        d_branch[here, :] = low
        back = lax.dot_general(low, weight, (((1,), (1,)), ((), ())), preferred_element_type=F32).astype(BF)
        feats = width // 2
        keep[a] = jnp.where(core == 0, back[:, :feats], back[:, feats:])
        give[a] = jnp.where(core == 0, back[:, feats:], back[:, :feats])
        parts = (d_h2 * normed, d_h2, d_mid * branch[a].astype(F32), low.astype(F32))
        total = [t + jnp.sum(p, axis=0, keepdims=True) for t, p in zip(total, parts)]
    for j in range(4):
        sums[j : j + 1, :] = total[j]


def attn_bwd_kernel(t, flags, q, k, v, keep, came, p, d_joint, ds_out, sums, do, dkt, dvt):
    core = flags[0]
    shard = keep.shape[1]
    cols = slice(128 * t, 128 * t + 128)
    for a in range(2):
        do[pl.ds(pl.multiple_of((2 * a + core) * shard, 16), shard), :] = keep[a, :, cols]
        do[pl.ds(pl.multiple_of((2 * a + 1 - core) * shard, 16), shard), :] = came[a, :, cols]
    rows = 144
    half = lax.broadcasted_iota(jnp.int32, (1, 128), 1) < 64
    q_turn = jnp.transpose(q[...].astype(F32)).astype(BF)
    do_turn = jnp.transpose(do[...].astype(F32)).astype(BF)

    def chunk(i, carry):
        here = pl.ds(pl.multiple_of(i * rows, 16), rows)
        do_tile = do[here, :]
        outs = []
        for sub in range(2):
            do_own = jnp.where(half if sub == 0 else ~half, do_tile, jnp.zeros_like(do_tile))
            d_prob = lax.dot_general(do_own, v[...], (((1,), (1,)), ((), ())), preferred_element_type=F32)
            prob = p[sub, here, :].astype(F32)
            weighted = prob * d_prob
            delta = jnp.sum(weighted, axis=1, keepdims=True)
            low = (weighted - prob * delta).astype(BF)
            ds_out[sub, here, :] = low
            outs.append(jnp.dot(low, k[...], preferred_element_type=F32))
        dq = jnp.where(half, outs[0], outs[1]).astype(BF).astype(F32) * 64**-0.5
        d_joint[here, 0:128] = dq.astype(BF)
        return carry + jnp.sum(dq, axis=0, keepdims=True)

    sums[0:1, :] = lax.fori_loop(0, ROW_LEN // rows, chunk, jnp.zeros((1, 128), F32))
    for sub in range(2):
        part = slice(64 * sub, 64 * sub + 64)
        dkt[part, :] = jnp.dot(q_turn[part], ds_out[sub], preferred_element_type=F32)
        dvt[part, :] = jnp.dot(do_turn[part], p[sub], preferred_element_type=F32)
    dv = jnp.transpose(dvt[...]).astype(BF)
    d_joint[:, 128:256] = jnp.transpose(dkt[...]).astype(BF)
    d_joint[:, 256:384] = dv
    sums[1:2, :] = jnp.sum(dv.astype(F32), axis=0, keepdims=True)


def h1_back_kernel(flags, first, second, third, w, keep, give):
    core = flags[0]
    width = keep.shape[-1]
    shard = keep.shape[1]
    feats = w.shape[2] // 3
    parts = []
    for t in range(3):
        for j in range(3):
            parts.append(w[:, :, feats * j + 128 * t : feats * j + 128 * t + 128])
    weight = jnp.concatenate(parts, axis=2).reshape(width, 3 * feats)
    for a in range(2):
        for mine in range(2):
            side = core if mine else 1 - core
            here = pl.ds(pl.multiple_of((2 * a + side) * shard, 16), shard)
            part = jnp.concatenate([d_joint[here, :] for d_joint in (first, second, third)], axis=1)
            out = lax.dot_general(part, weight, (((1,), (1,)), ((), ())), preferred_element_type=F32)
            if mine:
                keep[a] = out
            else:
                give[a] = out.astype(BF)


def end_kernel(flags, keep_in, came, own, d_middle, mixed, vecs, *refs):
    sums_attn, (sums_mid, sums_out, d_b_up, keep, give, sums) = refs[:-6], refs[-6:]
    core, x = flags[0], flags[1]
    width = own.shape[-1]
    total = [jnp.zeros((1, width), F32)] * 2
    for a in range(2):
        side = x if a == 0 else 1 - x
        d_h1 = keep_in[side] + came[side].astype(F32)
        normed, inverse = norm_parts(own[0, side].astype(F32))
        out = d_middle[side] + norm_back(normed, inverse, d_h1, vec(vecs, "gain1"))
        to = keep if a == 0 else give
        to[0] = mixed[side]
        to[1] = out.astype(BF)
        parts = (d_h1 * normed, d_h1)
        total = [t + jnp.sum(p, axis=0, keepdims=True) for t, p in zip(total, parts)]
    attn = jnp.concatenate([part[...] for part in sums_attn], axis=1)
    none = jnp.zeros_like(attn)
    attn = jnp.concatenate([jnp.where(core == 0, attn, none), jnp.where(core == 0, none, attn)], axis=1)
    mid, out = sums_mid[...], sums_out[...]
    rows = [attn, mid[3:4], out[1:2], *total, mid[0:3], out[0:1]]
    n_up = d_b_up.shape[1] // width
    for c in range(2):
        for j in range(n_up):
            rows.append(jnp.where(core == c, d_b_up[:, j * width : (j + 1) * width], 0.0))
    rows = jnp.concatenate(rows, axis=0)
    sums[: rows.shape[0], :] = rows
    sums[rows.shape[0] :, :] = jnp.zeros((sums.shape[0] - rows.shape[0], width), F32)


def home_kernel(flags, keep, came, mixed, d_tokens):
    x = flags[1]
    for j, out in enumerate((mixed, d_tokens)):
        out[x] = keep[j]
        out[1 - x] = came[j]


def table_kernel(meta, *refs):
    scores, (out, grid_out, strip, wide_ds) = refs[:-4], refs[-4:]
    heads = wide_ds.shape[0]
    depth = grid_out.shape[1]
    rows = 144
    lane = lax.broadcasted_iota(jnp.int32, (1, 128), 1)
    column = lax.broadcasted_iota(jnp.int32, (8, 128), 0)
    wide_ds[:, :, ROW_LEN:, :] = jnp.zeros(wide_ds.shape[:2] + (wide_ds.shape[2] - ROW_LEN, 128), F32)

    def widen(i, carry):
        here = pl.ds(pl.multiple_of(i * rows, 16), rows)
        for h in range(heads):
            part = scores[h // 2][h % 2, here, :].astype(F32)
            for kb in range(4):
                wide_ds[h, kb, here, :] = part[:, 128 * kb : 128 * kb + 128]
            wide_ds[h, 4, here, 0:64] = part[:, 512:576]
        return carry

    lax.fori_loop(0, ROW_LEN // rows, widen, 0)
    grid_out[...] = jnp.zeros_like(grid_out)
    for g in range(IMGS + 1):
        b, e, s, w, low, stop, first, last, groups = segment_loops(meta, g)

        def clear(pair, carry):
            for n in range(3):
                strip[n, 2 * pair] = jnp.zeros(strip.shape[2:], F32)
                strip[n, 2 * pair + 1] = jnp.zeros(strip.shape[2:], F32)
            return carry

        lax.fori_loop(low, stop, clear, 0)

        for size in range(1, 4):

            def line(y, carry, b=b, e=e, s=s, w=w, size=size):
                p0 = s + y * w
                off = STRIP - p0
                j0 = off // 128
                r = off - j0 * 128
                for n in range(size):
                    here = pl.ds(p0 + 8 * n, 8)
                    inside = column < w - 8 * n
                    moved = []
                    for kb in range(5):
                        place = lane + kb * 128
                        keep = inside & (place >= b) & (place < e)
                        piece = [jnp.where(keep, wide_ds[h, kb, here, :], 0.0) for h in range(heads)]
                        moved.append(pltpu.roll(jnp.concatenate(piece, axis=0), r, 1))
                    zero = jnp.zeros_like(moved[0])
                    moved = [zero] + moved + [zero]
                    for kb in range(6):
                        strip[n, j0 + kb] += jnp.where(lane >= r, moved[kb + 1], moved[kb])
                return carry

            lax.fori_loop(first, jnp.where(groups == size, last, first), line, 0)

        def fold(pair, carry, w=w):
            sides = [jnp.concatenate([strip[n, 2 * pair + j] for n in range(3)], axis=0) for j in range(2)]
            whole = jnp.concatenate(sides, axis=1)
            grid_out[...] += lax.dot_general(
                whole.astype(BF), strip_onehot(pair, w, depth), (((1,), (1,)), ((), ())), preferred_element_type=F32
            )
            return carry

        lax.fori_loop(low, stop, fold, 0)

    total = jnp.zeros((heads, FLAT), F32)
    for c in range(GRID):
        rows_c = [(c // 8 * heads + h) * 8 + c % 8 for h in range(heads)]
        part = jnp.concatenate([grid_out[i : i + 1, :] for i in rows_c], axis=0)
        pieces = [part, jnp.zeros((heads, FLAT - depth - SIDE * c), F32)]
        if c:
            pieces.insert(0, jnp.zeros((heads, SIDE * c), F32))
        total = total + jnp.concatenate(pieces, axis=1)
    out[...] = total


def vmem():
    return pl.BlockSpec(memory_space=pltpu.VMEM)


def smem():
    return pl.BlockSpec(memory_space=pltpu.SMEM)


def params(mib):
    return pltpu.CompilerParams(vmem_limit_bytes=mib * 1024 * 1024)


def cost(us):
    return pl.CostEstimate(flops=int(us * 600_000_000), bytes_accessed=1_000, transcendentals=0)


def strip_scratch(heads):
    return [
        pltpu.VMEM((3, BLOCKS, heads * 8, 128), F32),
        pltpu.VMEM((heads, 5, ROW_LEN + 32, 128), F32),
    ]


def hidden_kernel(flags, own, came, w, b, act, slope, h2):
    width = w.shape[0]
    n = h2.shape[0] // 2

    @pl.when(pl.program_id(0) == 0)
    def _():
        h2[:n] = own[...].reshape(n, width)
        h2[n:] = came[...].reshape(n, width)

    x = jnp.dot(h2[...], w[...], preferred_element_type=F32) + b[...].astype(F32)
    size = jnp.abs(x)
    t = 1.0 / (1.0 + (0.3275911 * 0.7071067811865476) * size)
    bell = jnp.exp(-0.5 * x * x)
    tail = t * (0.254829592 + t * (-0.284496736 + t * (1.421413741 + t * (-1.453152027 + t * 1.061405429))))
    tail = 0.5 * tail * bell
    phi = jnp.where(x >= 0, 1.0 - tail, tail)
    act[...] = (x * phi).astype(BF)
    slope[...] = (phi + x * (bell * 0.3989422804014327)).astype(BF)


def fixed(array, part=None):
    if part is None:
        return pl.BlockSpec(array.shape, lambda i: (0,) * array.ndim)
    return pl.BlockSpec((1,) + array.shape[1:], lambda i: (part,) + (0,) * (array.ndim - 1))


def join_kernel(places, own, came, *outs):
    n = own.shape[0]
    rows = own.shape[1]
    at = 0
    for out in outs:
        for high in range(out.shape[1] // rows):
            cols = slice(at, at + out.shape[2])
            at += out.shape[2]
            for i in range(n):
                out[places[i], high * rows : (high + 1) * rows, :] = own[i, :, cols]
                out[places[n + i], high * rows : (high + 1) * rows, :] = came[i, :, cols]


def first_join_kernel(places, own, came, w, vecs):
    n = own.shape[0]
    cols = w.shape[2]
    total = jnp.zeros((own.shape[1], own.shape[2] - cols), F32)
    for i in range(n):
        w[places[i]] = own[i, :, :cols]
        w[places[n + i]] = came[i, :, :cols]
        total = total + own[i, :, cols:].astype(F32) + came[i, :, cols:].astype(F32)
    for v in range(vecs.shape[0]):
        vecs[v : v + 1, :] = jnp.concatenate([total[3 * v + j : 3 * v + j + 1] for j in range(3)], axis=1)


def cat_kernel(flags, *refs):
    out, at = refs[-1], 0
    for part in refs[:-1]:
        out[at : at + part.shape[0]] = part[...]
        at += part.shape[0]


def add_kernel(flags, a, b, *outs):
    at = 0
    for out in outs:
        n = out.shape[0]
        out[...] = (a[at : at + n].astype(F32) + b[at : at + n].astype(F32)).astype(BF)
        at += n


def sum_kernel(flags, *refs):
    total = refs[0][...].astype(F32)
    for part in refs[1:-1]:
        total = total + part[...].astype(F32)
    refs[-1][...] = total


def grad_kernel(places, *refs):
    keep, give, full = refs[-3:]
    at = 0
    for a, b in zip(refs[:-3:2], refs[1:-3:2]):
        cols = slice(at, at + b.shape[1])
        at += b.shape[1]
        if a.shape[0] == full.shape[0]:
            full[:, cols] = (a[...].astype(F32) + b[...].astype(F32)).astype(BF)
            continue
        step = 256
        for t in range(full.shape[0] // step):
            here = slice(t * step, t * step + step)
            made = lax.dot_general(a[:, here], b[...], (((0,), (0,)), ((), ())), preferred_element_type=F32)
            full[here, cols] = made.astype(BF)
    n, rows, _ = keep.shape
    width = full.shape[1]
    block = full.shape[0] // (2 * n)
    for high in range(block // rows):
        there = slice(high * width, (high + 1) * width)
        for i in range(n):
            for out, j in ((keep, places[i]), (give, places[n + i])):
                out[i, :, there] = full[pl.ds(pl.multiple_of(j * block + high * rows, 16), rows), :]


def proj_grad_kernel(flags, joined, d_branch, keep, give):
    core = flags[0]
    n = keep.shape[1]
    width = joined.shape[-1]
    made = lax.dot_general(
        joined[...].reshape(-1, width), d_branch[...], (((0,), (0,)), ((), ())), preferred_element_type=F32
    )
    low, high = made[:, :n], made[:, n:]
    keep[...] = jnp.where(core == 0, low, high).astype(BF)
    give[...] = jnp.where(core == 0, high, low).astype(BF)


def after(array, *others):
    others = tuple(other for other in others if other is not None)
    return lax.optimization_barrier((array,) + others)[0] if others else array


class Net:
    def __init__(self, dp, seq):
        self.dp, self.seq = dp, seq
        self.fast = dp == 8
        self.last = None
        at_seq = lax.axis_index("seq")
        self.core = at_seq % 2
        self.x = at_seq // 2
        at_dp = lax.axis_index("dp")

        def table(fn):
            pairs = []
            for d in range(dp):
                for s in range(seq):
                    d2, s2 = fn(d, s)
                    pairs.append((d * seq + s, d2 * seq + s2))
            return pairs

        self.to_core = table(lambda d, s: (d, s ^ 1))
        self.to_x = table(lambda d, s: (d, s ^ 2))
        self.flags = jnp.stack([self.core, self.x]).astype(jnp.int32)
        if self.fast:
            self.phases = (
                table(lambda d, s: (d ^ 4, s)),
                table(lambda d, s: (d ^ 2, s)),
                table(lambda d, s: (d, s ^ 2) if s % 2 == 0 else (d ^ 1, s)),
                table(lambda d, s: (d ^ 1, s) if s % 2 == 0 else (d, s ^ 2)),
            )
            rel = jnp.arange(16, dtype=jnp.int32)
            d1, d2, d3, d4 = rel % 2, (rel // 2) % 2, (rel // 4) % 2, rel // 8
            by_x = jnp.where(self.core == 0, d3, d4)
            by_y = jnp.where(self.core == 0, d4, d3)
            self.places = ((at_dp * 2 + self.x) ^ (d1 * 8 + d2 * 4 + by_y * 2 + by_x)).astype(jnp.int32)

    def pin(self, array):
        return array if self.last is None else after(array, self.last)

    def call(self, kernel, us, outs, args, scratch=(), mib=8):
        got = pl.pallas_call(
            kernel,
            out_shape=tuple(jax.ShapeDtypeStruct(shape, kind) for shape, kind in outs),
            in_specs=[smem()] + [vmem()] * (len(args) - 1),
            out_specs=(vmem(),) * len(outs),
            scratch_shapes=list(scratch),
            compiler_params=params(mib),
            cost_estimate=cost(us),
            name=getattr(kernel, "func", kernel).__name__,
        )(self.pin(args[0]), *args[1:])
        self.last = got[0]
        return got

    def send(self, array, pairs):
        return lax.ppermute(array, BOTH, pairs)

    def by_core(self, own, other, axis):
        first = self.core == 0
        return jnp.stack([jnp.where(first, own, other), jnp.where(first, other, own)], axis=axis)

    def pick(self, array, index, axis):
        return lax.dynamic_index_in_dim(array, index, axis, keepdims=False)

    def bias_of(self, meta, flat, segment):
        heads = flat.shape[0]
        return self.call(
            bias_kernel,
            12,
            (((2, ROW_LEN, ROW_LEN), BF),) * (heads // 2),
            (meta, flat, segment[:, None], segment[None, :]),
            scratch=[pltpu.VMEM((heads * GRID, DEPTH), F32)] + strip_scratch(heads),
            mib=16,
        )

    def table_of(self, meta, scores):
        heads = 2 * len(scores)
        return self.call(
            table_kernel,
            12,
            (((heads, FLAT), F32),),
            (meta, *scores),
            scratch=[pltpu.VMEM((heads * GRID, DEPTH), F32)] + strip_scratch(heads),
            mib=16,
        )[0]

    def hidden(self, own, came, w, b):
        rows = 2 * own.size // w.shape[0]
        depth, cols = w.shape
        tile = 256
        out = jax.ShapeDtypeStruct((rows, cols), BF)
        got = pl.pallas_call(
            hidden_kernel,
            grid=(cols // tile,),
            out_shape=(out, out, jax.ShapeDtypeStruct((rows, depth), BF)),
            in_specs=[
                smem(),
                fixed(own),
                fixed(came),
                pl.BlockSpec((depth, tile), lambda i: (0, i)),
                pl.BlockSpec((1, tile), lambda i: (0, i)),
            ],
            out_specs=(pl.BlockSpec((rows, tile), lambda i: (0, i)),) * 2 + (pl.BlockSpec((rows, depth), lambda i: (0, 0)),),
            compiler_params=params(8),
            cost_estimate=cost(6),
            name="hidden",
        )(self.pin(self.flags), own, came, w, b)
        self.last = got[0]
        return got

    def hidden_back(self, d_after, w_down, slope, w_up):
        rows, cols = slope.shape
        width = w_up.shape[0]
        tile = cols // 2
        got = pl.pallas_call(
            hidden_back_kernel,
            grid=(cols // tile,),
            out_shape=(
                jax.ShapeDtypeStruct((rows, cols), BF),
                jax.ShapeDtypeStruct((1, cols), F32),
                jax.ShapeDtypeStruct((rows // 2, width), F32),
                jax.ShapeDtypeStruct((rows // 2, width), BF),
            ),
            in_specs=[
                smem(),
                fixed(d_after),
                pl.BlockSpec((tile, width), lambda i: (i, 0)),
                pl.BlockSpec((rows, tile), lambda i: (0, i)),
                pl.BlockSpec((width, tile), lambda i: (0, i)),
            ],
            out_specs=(
                pl.BlockSpec((rows, tile), lambda i: (0, i)),
                pl.BlockSpec((1, tile), lambda i: (0, i)),
                pl.BlockSpec((rows // 2, width), lambda i: (0, 0)),
                pl.BlockSpec((rows // 2, width), lambda i: (0, 0)),
            ),
            scratch_shapes=[pltpu.VMEM((rows, width), F32)],
            compiler_params=params(14),
            cost_estimate=cost(5),
            name="hidden_back",
        )(self.pin(self.flags), d_after, w_down, slope, w_up)
        self.last = got[0]
        return got

    def gather(self, block):
        return Gather(self, block) if self.fast else WholeGather(self, block)

    def library_gather(self, block):
        if not self.fast:
            return WholeGather(self, block).got
        groups = [[(d * 2 + x) * 2 + c for d in range(self.dp) for x in range(2)] for c in range(2)]
        return lax.all_gather(block, BOTH, axis=0, axis_index_groups=groups)

    def reduce(self, shape, *pairs):
        if self.fast:
            return Reduce(self, shape, pairs)
        made = []
        for a, b in pairs:
            made.append((wide(a) + wide(b) if a.shape == b.shape else dot_t(a, b)).astype(BF))
        return WholeReduce(self, jnp.concatenate(made, axis=1))


class Gather:
    def __init__(self, net, block):
        self.net, self.got, self.step = net, block[None], 0
        self.go()

    def go(self):
        self.came = self.net.send(self.got, self.net.phases[self.step])

    def next(self):
        out = ((2 * self.got.shape[0],) + self.got.shape[1:], BF)
        self.got = self.net.call(cat_kernel, 0.6, (out,), (self.net.flags, self.got, self.came))[0]
        self.step += 1
        self.go()

    def join(self, *shapes):
        outs = [((2 * self.got.shape[0],) + shape, BF) for shape in shapes]
        return self.net.call(join_kernel, 0.7, outs, (self.net.places, self.got, self.came))

    def first_join(self, cols):
        _, rows, width = self.got.shape
        outs = (((2 * self.got.shape[0], rows, cols), BF), ((rows // 3, 3 * (width - cols)), F32))
        return self.net.call(first_join_kernel, 0.7, outs, (self.net.places, self.got, self.came))


class WholeGather:
    def __init__(self, net, block):
        block = lax.all_gather(block, "dp", axis=0)
        other = net.send(block, net.to_x)
        first = net.x == 0
        block = jnp.stack([jnp.where(first, block, other), jnp.where(first, other, block)], axis=1)
        self.got = block.reshape((2 * net.dp,) + block.shape[2:])

    def next(self):
        pass

    def join(self, *shapes):
        cut = shapes[0][1]
        return (self.got,) if len(shapes) == 1 else (self.got[:, :, :cut], self.got[:, :, cut:])


class Reduce:
    def __init__(self, net, shape, pairs):
        self.net, self.step = net, 3
        arrays = [array for pair in pairs for array in pair]
        depth = pairs[0][0].shape[0] if pairs[0][0].shape == pairs[0][1].shape else pairs[0][0].shape[1]
        width = sum(b.shape[1] for _, b in pairs)
        out = ((8,) + shape, BF)
        self.keep, self.give = net.call(
            grad_kernel, 3, (out, out), (net.places, *arrays), scratch=[pltpu.VMEM((depth, width), BF)]
        )
        self.go()

    def go(self):
        self.came = self.net.send(self.give, self.net.phases[self.step])

    def next(self):
        out = ((self.keep.shape[0] // 2,) + self.keep.shape[1:], BF)
        self.keep, self.give = self.net.call(add_kernel, 1, (out, out), (self.net.flags, self.keep, self.came))
        self.step -= 1
        self.go()

    def end(self):
        out = ((1,) + self.keep.shape[1:], F32)
        return self.net.call(sum_kernel, 0.6, (out,), (self.net.flags, self.keep, self.came))[0][0]


class WholeReduce:
    def __init__(self, net, full):
        blocks = full.reshape((net.dp, 2, -1) + full.shape[1:])
        came = net.send(net.pick(blocks, 1 - net.x, 1), net.to_x)
        summed = net.pick(blocks, net.x, 1).astype(F32) + came.astype(F32)
        self.sum = lax.psum_scatter(summed, "dp", scatter_dimension=0, tiled=False)

    def next(self):
        pass

    def end(self):
        return self.sum


class Total:
    def __init__(self, net, array):
        self.net, self.sum, self.step = net, array, 0
        if net.fast:
            self.came = net.send(array, net.phases[0])
        else:
            self.sum = lax.psum(array + net.send(array, net.to_x), "dp")

    def next(self):
        if self.net.fast:
            out = (self.sum.shape, F32)
            self.sum = self.net.call(sum_kernel, 0.6, (out,), (self.net.flags, self.sum, self.came))[0]
            self.step += 1
            if self.step < 4:
                self.came = self.net.send(self.sum, self.net.phases[self.step])


def wide(array):
    return array.astype(F32)


def dot(a, b):
    return jnp.dot(a, b, preferred_element_type=F32)


def dot_t(a, b):
    return lax.dot_general(a, b, (((0,), (0,)), ((), ())), preferred_element_type=F32)


def local(
    dp,
    seq,
    tokens,
    image_lengths,
    grid_widths,
    qkv_weight,
    q_bias,
    v_bias,
    proj_weight,
    proj_bias,
    fc1_weight,
    fc1_bias,
    fc2_weight,
    fc2_bias,
    norm1_gain,
    norm1_bias,
    norm2_gain,
    norm2_bias,
    scale1,
    scale2,
    bias_table,
    out_grad,
):
    net = Net(dp, seq)
    call, flags, core, at_x = net.call, net.flags, net.core, net.x
    row_count, shard, width = tokens.shape
    heads = bias_table.shape[1]
    own_heads = heads // 2
    own_feats = width // 2
    n_dev = dp * seq
    chips = n_dev // 2
    rows_w = width // n_dev
    ff = fc2_weight.shape[0] * n_dev
    rows_f = ff // n_dev
    at = lax.axis_index("dp") * seq + lax.axis_index("seq")
    at_chip = lax.axis_index("dp") * 2 + at_x

    lanes = jnp.arange(width, dtype=jnp.int32)
    spots = (lanes[None] // rows_w == at) & (lanes[None] % rows_w == jnp.arange(rows_w, dtype=jnp.int32)[:, None])
    vecs = [q_bias, v_bias, proj_bias, fc2_bias, norm1_gain, norm1_bias, norm2_gain, norm2_bias, scale1, scale2]
    n_vec = len(vecs)
    placed = dot(jnp.stack(vecs), spots.astype(BF)).astype(BF)
    n_up = ff // 2 // width
    lanes_up = jnp.arange(ff // 2, dtype=jnp.int32)
    spots_up = (lanes_up[None] // rows_f == at_chip) & (lanes_up[None] % rows_f == jnp.arange(rows_f, dtype=jnp.int32)[:, None])
    placed_up = dot(fc1_bias[None], spots_up.astype(BF)).astype(BF).reshape(n_up, width)
    mine = (jnp.arange(2) == core)[:, None, None]
    placed_up = jnp.where(mine, placed_up[None], jnp.zeros((), BF)).reshape(2 * n_up, width)
    placed = jnp.concatenate([placed, placed_up, jnp.zeros((16 - n_vec - 2 * n_up, width), BF)])

    low = ((rows_w, 3 * own_feats), BF)
    keep, give = call(split_kernel, 0.5, (low, low), (flags, qkv_weight))
    attn_block = net.by_core(keep, net.send(give, net.to_core), 0).reshape(2 * rows_w, 3 * own_feats)
    placed = placed + net.send(placed, net.to_core)
    if net.fast:
        attn_block = jnp.concatenate([attn_block, placed.reshape(48, 256)], axis=1)
    attn_chain = net.gather(attn_block)

    their_tokens, their_grad = after(tokens, attn_block), after(out_grad, attn_block)
    theirs = jnp.stack([net.pick(their_tokens, 1 - at_x, 0), net.pick(their_grad, 1 - at_x, 0)])
    token_came = net.send(theirs, net.to_x)
    proj_view = after(proj_weight, attn_block).reshape(rows_w, 2, own_feats)
    fc1_view = after(fc1_weight, attn_block).reshape(rows_w, chips, 2, rows_f)
    views = []
    for index in (core, 1 - core):
        up = net.pick(fc1_view, index, 2).reshape(rows_w, ff // 2)
        views.append(jnp.concatenate([up, net.pick(proj_view, index, 1)], axis=1))
    up_came = net.send(views[1], net.to_core)

    lengths = net.pick(image_lengths, at_x, 0)
    widths = net.pick(grid_widths, at_x, 0)
    meta, segment = layout(after(lengths, attn_block), after(widths, attn_block))
    flat = jnp.transpose(after(bias_table, attn_block).reshape(SIDE, SIDE, heads), (2, 1, 0)).reshape(heads, SIDE * SIDE)
    flat = jnp.pad(wide(lax.dynamic_slice_in_dim(flat, core * own_heads, own_heads)), ((0, 0), (0, FLAT - SIDE * SIDE)))

    chunk = (2, shard, width)
    attn_chain.next()
    (up_block,) = call(stack_kernel, 0.5, (((2 * rows_w, ff // 2 + own_feats), BF),), (flags, views[0], up_came))
    up_chain = net.gather(up_block)
    biases = net.bias_of(meta, after(flat, token_came), segment)
    up_chain.next()
    attn_chain.next()
    down_block = fc2_weight if not net.fast else jnp.concatenate([fc2_weight[: 2 * rows_w], fc2_weight[2 * rows_w :]], axis=1)
    down_chain = net.gather(net.pin(down_block))
    (both,) = call(start_kernel, 0.5, (((2,) + chunk, BF),), (flags, tokens, out_grad, token_came))
    both_came = net.send(both, net.to_core)
    attn_chain.next()
    up_chain.next()
    down_chain.next()
    if net.fast:
        w_qkv, vectors = attn_chain.first_join(3 * own_feats)
    else:
        (w_qkv,) = attn_chain.join((2 * rows_w, 3 * own_feats))
        vectors = Total(net, wide(placed)).sum
    up_chain.next()
    b_up = net.pick(vectors[n_vec : n_vec + 2 * n_up].reshape(2, 1, ff // 2), core, 0)

    row = (ROW_LEN, 128)
    part_heads = (2, shard, 128)
    square = (2, ROW_LEN, ROW_LEN)
    pairs, keeps, cames = [], [], []
    for t, bias in enumerate(biases):
        outs = ((row, BF),) * 3 + ((square, BF), (part_heads, BF), (part_heads, BF))
        if t == 0:
            outs = outs + (((ROW_LEN, width), BF),)
            args = (flags, both, both_came, w_qkv, vectors, bias)
        else:
            args = (flags, h1, w_qkv, vectors, bias)
        got = call(functools.partial(attn_fwd_kernel, t == 0, t), 5, outs, args, scratch=[pltpu.VMEM(row, BF)])
        if t == 0:
            h1 = got[6]
        pairs.append(got[:4])
        keeps.append(got[4])
        cames.append(net.send(got[5], net.to_core))
        if t == 0:
            down_chain.next()
    down_chain.next()
    fc1_all, pj_own = up_chain.join((2 * rows_w, ff // 2), (2 * rows_w, own_feats))
    pj_came = net.send(pj_own, net.to_core)
    joined, branch, middle, h2, d_after = call(
        proj_kernel,
        3,
        ((chunk, BF), (chunk, BF), (chunk, F32), (chunk, BF), ((ROW_LEN, width), BF)),
        (flags, *keeps, *cames, pj_own, pj_came, both, both_came, vectors),
    )
    h2_came = net.send(h2, net.to_core)
    w_up = fc1_all.reshape(width, ff // 2)
    act, slope, h2_all = net.hidden(h2, h2_came, w_up, b_up)
    down_sum = net.reduce((rows_f, width), (act, d_after))
    w_down = down_chain.join((rows_f, width))[0].reshape(ff // 2, width)
    d_before, d_b_up, keep, give = net.hidden_back(d_after, w_down, slope, w_up)
    mid_came = net.send(give, net.to_core)
    own = 2 * shard
    after_keep, after_give = call(after_kernel, 2, (((own, width), F32), ((own, width), BF)), (flags, act, w_down))
    after_came = net.send(after_give, net.to_core)
    half = (2, shard, own_feats)
    d_middle, d_branch, keep, give, sums_mid = call(
        middle_back_kernel,
        3,
        ((chunk, F32), ((own, width), BF), (half, BF), (half, BF), ((4, width), F32)),
        (flags, keep, mid_came, middle, both, branch, pj_own, pj_came, vectors),
    )
    heads_came = net.send(give, net.to_core)
    out = ((width, own_feats), BF)
    proj_keep, proj_give = call(proj_grad_kernel, 2, (out, out), (flags, joined, d_branch))
    proj_came = net.send(proj_give, net.to_core)

    d_joints, scores, sums_attn = [], [], []
    for t, (q, k, v, prob) in enumerate(pairs):
        d_joint, ds, sums = call(
            functools.partial(attn_bwd_kernel, t),
            5,
            (((ROW_LEN, 384), BF), (square, BF), ((2, 128), F32)),
            (flags, q, k, v, keep, heads_came, prob),
            scratch=[pltpu.VMEM(row, BF), pltpu.VMEM((128, ROW_LEN), F32), pltpu.VMEM((128, ROW_LEN), F32)],
        )
        d_joints.append(d_joint)
        scores.append(ds)
        sums_attn.append(sums)
        if t == 0:
            up_sum = net.reduce((2 * rows_w, ff // 2 + own_feats), (h2_all, d_before), (proj_keep, proj_came))
            down_sum.next()
        if t == 1:
            mixed, sums_out = call(
                mixed_kernel,
                2,
                ((chunk, BF), ((2, width), F32)),
                (flags, after_keep, after_came, middle, both, d_after, vectors),
            )
    attn_sum = net.reduce((2 * rows_w, 3 * own_feats), *[(h1, d_joint) for d_joint in d_joints])
    keep, give = call(h1_back_kernel, 3, ((chunk, F32), (chunk, BF)), (flags, *d_joints, w_qkv))
    h1_came = net.send(give, net.to_core)
    down_sum.next()
    up_sum.next()
    table = net.table_of(meta, scores)
    down_sum.next()
    up_sum.next()

    keep, give, smalls = call(
        end_kernel,
        2,
        ((chunk, BF), (chunk, BF), ((16, width), F32)),
        (flags, keep, h1_came, both, d_middle, mixed, vectors, *sums_attn, sums_mid, sums_out, d_b_up),
    )
    smalls_came = net.send(smalls, net.to_core)
    out_came = net.send(give, net.to_x)
    attn_sum.next()
    (smalls,) = call(sum_kernel, 0.6, (((16, width), F32),), (flags, smalls, smalls_came))
    total = Total(net, jnp.concatenate([smalls.reshape(-1, 128), table.reshape(-1, 128)]))
    total.next()
    g_down = down_sum.end()
    up_sum.next()
    total.next()
    attn_sum.next()
    total.next()
    g_up = up_sum.end()
    attn_sum.next()
    total.next()
    mixed, tokens_grad = call(home_kernel, 1, ((chunk, BF), (chunk, BF)), (flags, keep, out_came))
    g_attn = attn_sum.end()

    def home(block, groups, cols):
        view = block.reshape(2, rows_w, groups, cols)
        came = net.send(net.pick(view, 1 - core, 0), net.to_core)
        return net.by_core(net.pick(view, core, 0), came, 2).reshape(rows_w, groups * 2 * cols)

    g_proj = home(g_up[:, ff // 2 :], 1, own_feats)
    g_up = home(g_up[:, : ff // 2], chips, rows_f)
    packed = total.sum
    sums = packed[: smalls.size // 128].reshape(smalls.shape)
    table = packed[smalls.size // 128 :].reshape(own_heads, FLAT)
    table = net.by_core(table, net.send(table, net.to_core), 0).reshape(heads, FLAT)[:, : SIDE * SIDE]
    table_grad = jnp.transpose(table.reshape(heads, SIDE, SIDE), (2, 1, 0)).reshape(SIDE * SIDE, heads)
    g_small = lax.dynamic_slice_in_dim(sums[:n_vec], at * rows_w, rows_w, 1)
    g_up_small = net.pick(sums[n_vec : n_vec + 2 * n_up].reshape(2, ff // 2), core, 0)
    g_up_small = lax.dynamic_slice_in_dim(g_up_small, at_chip * rows_f, rows_f)
    smalls = [g_small[j] for j in range(n_vec)] + [g_up_small]

    g_attn = g_attn.reshape(2 * rows_w, 3, 3, 128).transpose(0, 2, 1, 3).reshape(2 * rows_w, 3 * own_feats)
    g_qkv = home(g_attn, 3, own_feats)
    g_query, g_value, g_bproj, g_bdown, g_gain1, g_shift1, g_gain2, g_shift2, g_layer1, g_layer2, g_bup = smalls
    return (
        mixed,
        tokens_grad,
        g_qkv,
        g_query,
        g_value,
        g_proj,
        g_bproj,
        g_up,
        g_bup,
        g_down,
        g_bdown,
        g_gain1,
        g_shift1,
        g_gain2,
        g_shift2,
        g_layer1,
        g_layer2,
        table_grad,
    )


def solution(mesh):
    both = P(BOTH)
    both2 = P(BOTH, None)
    act = P("dp", "seq", None)
    in_specs = (act, P("dp", None), P("dp", None), both2, both, both, both2, both, both2, both, both2)
    in_specs += (both,) * 7 + (P(), act)
    out_specs = (act, act, both2, both, both, both2, both, both2, both, both2) + (both,) * 7 + (P(),)
    body = functools.partial(local, mesh.shape["dp"], mesh.shape["seq"])
    return jax.shard_map(body, mesh=mesh, in_specs=in_specs, out_specs=out_specs, check_vma=False)
```

```python
import functools

import jax
import jax.numpy as jnp
from jax import lax
from jax.experimental import pallas as pl
from jax.experimental.pallas import tpu as pltpu
from jax.sharding import PartitionSpec as P

GRID = 24
SIDE = 2 * GRID - 1
ROW_LEN = 576
IMGS = 4
EPS = 1e-06
STRIP = 640
BLOCKS = 12
DEPTH = 1152
FLAT = 2304
BF = jnp.bfloat16
F32 = jnp.float32
BOTH = ("dp", "seq")
VECS = ("q", "v", "b_proj", "b_down", "gain1", "shift1", "gain2", "shift2", "scale1", "scale2")


def layout(lengths, widths):
    ends = jnp.cumsum(lengths).astype(jnp.int32)
    starts = ends - lengths
    total = ends[-1]
    full = jnp.full((1,), ROW_LEN, jnp.int32)
    meta = jnp.stack(
        [
            jnp.concatenate([starts, total[None]]),
            jnp.concatenate([ends, full]),
            jnp.concatenate([starts, jnp.zeros((1,), jnp.int32)]),
            jnp.concatenate([widths, jnp.full((1,), GRID, jnp.int32)]),
        ]
    ).astype(jnp.int32)
    places = jnp.arange(ROW_LEN, dtype=jnp.int32)
    segment = jnp.sum((places[:, None] >= ends[None, :]).astype(jnp.int32), axis=1)
    return meta, segment


def strip_range(b, e):
    length = e - b
    return (STRIP - length) // 256, jnp.minimum((STRIP + length + GRID) // 256, BLOCKS // 2 - 1)


def strip_onehot(pair, w, depth):
    lane = lax.broadcasted_iota(jnp.int32, (1, 256), 1) + (pair * 256 - STRIP + 80 * w)
    line = jnp.floor((lane.astype(F32) + 0.5) / jnp.full((1, 256), w, jnp.int32).astype(F32)).astype(jnp.int32)
    column = lane - line * w
    level = jnp.clip(80 - line, 1 - GRID, GRID - 1) + (GRID - 1)
    code = (GRID - 1 - column) * SIDE + level
    return (lax.broadcasted_iota(jnp.int32, (depth, 256), 0) == code).astype(F32).astype(BF)


def segment_loops(meta, g):
    b, e, s, w = meta[0, g], meta[1, g], meta[2, g], meta[3, g]
    low, high = strip_range(b, e)
    stop = jnp.where(e > b, high + 1, low)
    first, last = (b - s) // w, jnp.where(e > b, (e - 1 - s) // w + 1, 0)
    return b, e, s, w, low, stop, first, last, (w + 7) // 8


def bias_kernel(meta, flat, seg_col, seg_row, *refs):
    outs, (tab, strip, bias) = refs[:-3], refs[-3:]
    heads = bias.shape[0]
    depth = tab.shape[1]
    lane = lax.broadcasted_iota(jnp.int32, (1, 128), 1)
    for c in range(GRID):
        moved = flat[:, SIDE * c : SIDE * c + depth]
        for h in range(heads):
            row = (c // 8 * heads + h) * 8 + c % 8
            tab[row : row + 1, :] = moved[h : h + 1]
    low_tab = tab[...].astype(BF)
    for g in range(IMGS + 1):
        b, e, s, w, low, stop, first, last, groups = segment_loops(meta, g)

        def build(pair, carry, w=w):
            made = jnp.dot(low_tab, strip_onehot(pair, w, depth), preferred_element_type=F32)
            for n in range(3):
                rows_n = slice(n * heads * 8, (n + 1) * heads * 8)
                strip[n, 2 * pair] = made[rows_n, :128]
                strip[n, 2 * pair + 1] = made[rows_n, 128:]
            return carry

        lax.fori_loop(low, stop, build, 0)

        for size in range(1, 4):

            def lines(turn, carry, b=b, s=s, w=w, g=g, size=size, first=first, last=last):
                found = []
                for y in (first + 2 * turn, jnp.minimum(first + 2 * turn + 1, last - 1)):
                    p0 = s + y * w
                    off = STRIP - p0
                    j0 = off // 128
                    r = off - j0 * 128
                    for n in range(size):
                        parts = [strip[n, j0 + kb] for kb in range(6)]
                        for kb in range(5):
                            moved = pltpu.roll(jnp.where(lane >= r, parts[kb], parts[kb + 1]), (128 - r) % 128, 1)
                            found.append((kb, pl.ds(p0 + 8 * n, 8), moved))
                for kb, here, moved in found:
                    for h in range(heads):
                        piece = moved[h * 8 : (h + 1) * 8]
                        if g == IMGS:
                            piece = jnp.where(lane + kb * 128 >= b, piece, bias[h, kb, here, :])
                        bias[h, kb, here, :] = piece
                return carry

            lax.fori_loop(0, jnp.where(groups == size, (last - first + 1) // 2, 0), lines, 0)

    rows = 144

    def mask(i, carry):
        here = pl.ds(pl.multiple_of(i * rows, 16), rows)
        allowed = seg_col[here, :] == seg_row[...]
        for h in range(heads):
            offs = jnp.concatenate([bias[h, kb, here, :] for kb in range(5)], axis=1)[:, :ROW_LEN]
            outs[h // 2][h % 2, here, :] = jnp.where(allowed, offs, -1e30).astype(BF)
        return carry

    lax.fori_loop(0, ROW_LEN // rows, mask, 0)


def norm_parts(x):
    center = x - jnp.mean(x, axis=-1, keepdims=True)
    inverse = lax.rsqrt(jnp.mean(center * center, axis=-1, keepdims=True) + EPS)
    return center * inverse, inverse


def norm_back(normed, inverse, grad, gain):
    pulled = grad * gain
    mean = jnp.mean(pulled, axis=-1, keepdims=True)
    along = jnp.mean(pulled * normed, axis=-1, keepdims=True)
    return (pulled - mean - normed * along) * inverse


def vec(vecs, name):
    return vecs[VECS.index(name) : VECS.index(name) + 1, :].astype(F32)


def own_half(core, row):
    n = row.shape[1] // 2
    return jnp.where(core == 0, row[:, :n], row[:, n:])


def split_kernel(flags, w, keep, give):
    core = flags[0]
    n = w.shape[1] // 6
    for j in range(3):
        low, high = w[:, 2 * n * j : 2 * n * j + n], w[:, 2 * n * j + n : 2 * n * j + 2 * n]
        keep[:, n * j : n * j + n] = jnp.where(core == 0, low, high)
        give[:, n * j : n * j + n] = jnp.where(core == 0, high, low)


def stack_kernel(flags, own, came, out):
    core = flags[0]
    rows = own.shape[0]
    first = core == 0
    out[:rows] = jnp.where(first, own[...], came[...])
    out[rows:] = jnp.where(first, came[...], own[...])


def start_kernel(flags, tokens, out_grad, came, both):
    x = flags[1]
    both[0, x] = tokens[x]
    both[1, x] = out_grad[x]
    both[0, 1 - x] = came[0]
    both[1, 1 - x] = came[1]


def attn_fwd_kernel(first, t, flags, *refs):
    core = flags[0]
    if first:
        own, came, w, vecs, bias, q, k, v, p_out, keep, give, h1, joined = refs
        shard = own.shape[2]
        for a in range(2):
            for side, part in ((core, own), (1 - core, came)):
                normed, _ = norm_parts(part[0, a].astype(F32))
                normed = normed * vec(vecs, "gain1") + vec(vecs, "shift1")
                h1[pl.ds(pl.multiple_of((2 * a + side) * shard, 16), shard), :] = normed.astype(BF)
    else:
        h1, w, vecs, bias, q, k, v, p_out, keep, give, joined = refs
        shard = keep.shape[1]
    feats = w.shape[2] // 3
    cols = slice(128 * t, 128 * t + 128)

    def weight(j):
        return w[:, :, feats * j + 128 * t : feats * j + 128 * t + 128].reshape(h1.shape[1], 128)

    q_row, v_row = own_half(core, vec(vecs, "q"))[:, cols], own_half(core, vec(vecs, "v"))[:, cols]
    q[...] = ((jnp.dot(h1[...], weight(0), preferred_element_type=F32) + q_row) * 64**-0.5).astype(BF)
    k[...] = jnp.dot(h1[...], weight(1), preferred_element_type=F32).astype(BF)
    v[...] = (jnp.dot(h1[...], weight(2), preferred_element_type=F32) + v_row).astype(BF)
    rows = 144
    half = lax.broadcasted_iota(jnp.int32, (1, 128), 1) < 64

    def chunk(i, carry):
        here = pl.ds(pl.multiple_of(i * rows, 16), rows)
        q_tile = q[here, :]
        outs = []
        for sub in range(2):
            q_own = jnp.where(half if sub == 0 else ~half, q_tile, jnp.zeros_like(q_tile))
            score = lax.dot_general(q_own, k[...], (((1,), (1,)), ((), ())), preferred_element_type=F32)
            score = score + bias[sub, here, :].astype(F32)
            raised = jnp.exp(score - jnp.max(score, axis=1, keepdims=True))
            prob = (raised * (1.0 / jnp.sum(raised, axis=1, keepdims=True))).astype(BF)
            p_out[sub, here, :] = prob
            outs.append(jnp.dot(prob, v[...], preferred_element_type=F32))
        joined[here, :] = jnp.where(half, outs[0], outs[1]).astype(BF)
        return carry

    lax.fori_loop(0, ROW_LEN // rows, chunk, 0)
    for a in range(2):
        keep[a] = joined[pl.ds(pl.multiple_of((2 * a + core) * shard, 16), shard), :]
        give[a] = joined[pl.ds(pl.multiple_of((2 * a + 1 - core) * shard, 16), shard), :]


def by_core_in(core, own, came):
    return jnp.concatenate([jnp.where(core == 0, own, came), jnp.where(core == 0, came, own)], axis=-1)


def proj_kernel(flags, *refs):
    keeps, cames = refs[:3], refs[3:6]
    w_own, w_came, own, grads_came, vecs, joined, branch, middle, h2, d_after = refs[6:]
    core = flags[0]
    width = own.shape[-1]
    shard = own.shape[2]
    feats = width // 2
    for a in range(2):
        keep = jnp.concatenate([part[a] for part in keeps], axis=-1)
        came = jnp.concatenate([part[a] for part in cames], axis=-1)
        joined[a] = by_core_in(core, keep, came)
    weight = by_core_in(core, w_own[...].reshape(width, feats), w_came[...].reshape(width, feats))
    for a in range(2):
        out = jnp.dot(joined[a], weight, preferred_element_type=F32) + vec(vecs, "b_proj")
        branch[a] = out.astype(BF)
        mid = own[0, a].astype(F32) + vec(vecs, "scale1") * out
        middle[a] = mid
        for j, part in enumerate((own, grads_came)):
            here = slice((2 * j + a) * shard, (2 * j + a + 1) * shard)
            d_after[here, :] = (vec(vecs, "scale2") * part[1, a].astype(F32)).astype(BF)
        normed, _ = norm_parts(mid)
        h2[a] = (normed * vec(vecs, "gain2") + vec(vecs, "shift2")).astype(BF)


def after_kernel(flags, act, w, keep, give):
    n = keep.shape[0]
    keep[...] = jnp.dot(act[:n], w[...], preferred_element_type=F32)
    give[...] = jnp.dot(act[n:], w[...], preferred_element_type=F32).astype(BF)


def mixed_kernel(flags, keep, came, middle, own, d_after, vecs, mixed, sums):
    rows = middle.shape[0] * middle.shape[1]
    width = middle.shape[2]
    out = keep[...] + came[...].astype(F32) + vec(vecs, "b_down")
    mid = middle[...].reshape(rows, width)
    mixed[...] = (mid + vec(vecs, "scale2") * out).astype(BF).reshape(mixed.shape)
    g = own[1].reshape(rows, width).astype(F32)
    sums[0:1, :] = jnp.sum(g * out, axis=0, keepdims=True)
    sums[1:2, :] = jnp.sum(d_after[:rows].astype(F32), axis=0, keepdims=True)


def hidden_back_kernel(flags, d_after, w_down, slope, w_up, d_before, b_sum, keep, give, total):
    i = pl.program_id(0)
    width = w_up.shape[0]
    d_act = lax.dot_general(d_after[...], w_down[...], (((1,), (1,)), ((), ())), preferred_element_type=F32)
    low = (d_act * slope[...].astype(F32)).astype(BF)
    d_before[...] = low
    b_sum[...] = jnp.sum(low.astype(F32), axis=0, keepdims=True)
    d_h2 = lax.dot_general(low, w_up[...], (((1,), (1,)), ((), ())), preferred_element_type=F32)

    @pl.when(i == 0)
    def _():
        total[...] = d_h2

    @pl.when(i > 0)
    def _():
        total[...] += d_h2

    @pl.when(i == pl.num_programs(0) - 1)
    def _():
        n = keep.shape[0]
        keep[...] = total[:n]
        give[...] = total[n:].astype(BF)


def middle_back_kernel(flags, keep_in, came, middle, own, branch, w_own, w_came, vecs, d_middle, d_branch, keep, give, sums):
    core = flags[0]
    width = middle.shape[-1]
    shard = middle.shape[1]
    weight = by_core_in(core, w_own[...].reshape(width, width // 2), w_came[...].reshape(width, width // 2))
    total = [jnp.zeros((1, width), F32)] * 4
    for a in range(2):
        here = slice(a * shard, a * shard + shard)
        normed, inverse = norm_parts(middle[a])
        d_h2 = keep_in[here, :] + came[here, :].astype(F32)
        d_mid = own[1, a].astype(F32) + norm_back(normed, inverse, d_h2, vec(vecs, "gain2"))
        d_middle[a] = d_mid
        low = (vec(vecs, "scale1") * d_mid).astype(BF)
        d_branch[here, :] = low
        back = lax.dot_general(low, weight, (((1,), (1,)), ((), ())), preferred_element_type=F32).astype(BF)
        feats = width // 2
        keep[a] = jnp.where(core == 0, back[:, :feats], back[:, feats:])
        give[a] = jnp.where(core == 0, back[:, feats:], back[:, :feats])
        parts = (d_h2 * normed, d_h2, d_mid * branch[a].astype(F32), low.astype(F32))
        total = [t + jnp.sum(p, axis=0, keepdims=True) for t, p in zip(total, parts)]
    for j in range(4):
        sums[j : j + 1, :] = total[j]


def attn_bwd_kernel(t, flags, q, k, v, keep, came, p, d_joint, ds_out, sums, do, dkt, dvt):
    core = flags[0]
    shard = keep.shape[1]
    cols = slice(128 * t, 128 * t + 128)
    for a in range(2):
        do[pl.ds(pl.multiple_of((2 * a + core) * shard, 16), shard), :] = keep[a, :, cols]
        do[pl.ds(pl.multiple_of((2 * a + 1 - core) * shard, 16), shard), :] = came[a, :, cols]
    rows = 144
    half = lax.broadcasted_iota(jnp.int32, (1, 128), 1) < 64
    q_turn = jnp.transpose(q[...].astype(F32)).astype(BF)
    do_turn = jnp.transpose(do[...].astype(F32)).astype(BF)

    def chunk(i, carry):
        here = pl.ds(pl.multiple_of(i * rows, 16), rows)
        do_tile = do[here, :]
        outs = []
        for sub in range(2):
            do_own = jnp.where(half if sub == 0 else ~half, do_tile, jnp.zeros_like(do_tile))
            d_prob = lax.dot_general(do_own, v[...], (((1,), (1,)), ((), ())), preferred_element_type=F32)
            prob = p[sub, here, :].astype(F32)
            weighted = prob * d_prob
            delta = jnp.sum(weighted, axis=1, keepdims=True)
            low = (weighted - prob * delta).astype(BF)
            ds_out[sub, here, :] = low
            outs.append(jnp.dot(low, k[...], preferred_element_type=F32))
        dq = jnp.where(half, outs[0], outs[1]).astype(BF).astype(F32) * 64**-0.5
        d_joint[here, 0:128] = dq.astype(BF)
        return carry + jnp.sum(dq, axis=0, keepdims=True)

    sums[0:1, :] = lax.fori_loop(0, ROW_LEN // rows, chunk, jnp.zeros((1, 128), F32))
    for sub in range(2):
        part = slice(64 * sub, 64 * sub + 64)
        dkt[part, :] = jnp.dot(q_turn[part], ds_out[sub], preferred_element_type=F32)
        dvt[part, :] = jnp.dot(do_turn[part], p[sub], preferred_element_type=F32)
    dv = jnp.transpose(dvt[...]).astype(BF)
    d_joint[:, 128:256] = jnp.transpose(dkt[...]).astype(BF)
    d_joint[:, 256:384] = dv
    sums[1:2, :] = jnp.sum(dv.astype(F32), axis=0, keepdims=True)


def h1_back_kernel(flags, first, second, third, w, keep, give):
    core = flags[0]
    width = keep.shape[-1]
    shard = keep.shape[1]
    feats = w.shape[2] // 3
    parts = []
    for t in range(3):
        for j in range(3):
            parts.append(w[:, :, feats * j + 128 * t : feats * j + 128 * t + 128])
    weight = jnp.concatenate(parts, axis=2).reshape(width, 3 * feats)
    for a in range(2):
        for mine in range(2):
            side = core if mine else 1 - core
            here = pl.ds(pl.multiple_of((2 * a + side) * shard, 16), shard)
            part = jnp.concatenate([d_joint[here, :] for d_joint in (first, second, third)], axis=1)
            out = lax.dot_general(part, weight, (((1,), (1,)), ((), ())), preferred_element_type=F32)
            if mine:
                keep[a] = out
            else:
                give[a] = out.astype(BF)


def end_kernel(flags, keep_in, came, own, d_middle, mixed, vecs, *refs):
    sums_attn, (sums_mid, sums_out, d_b_up, keep, give, sums) = refs[:-6], refs[-6:]
    core, x = flags[0], flags[1]
    width = own.shape[-1]
    total = [jnp.zeros((1, width), F32)] * 2
    for a in range(2):
        side = x if a == 0 else 1 - x
        d_h1 = keep_in[side] + came[side].astype(F32)
        normed, inverse = norm_parts(own[0, side].astype(F32))
        out = d_middle[side] + norm_back(normed, inverse, d_h1, vec(vecs, "gain1"))
        to = keep if a == 0 else give
        to[0] = mixed[side]
        to[1] = out.astype(BF)
        parts = (d_h1 * normed, d_h1)
        total = [t + jnp.sum(p, axis=0, keepdims=True) for t, p in zip(total, parts)]
    attn = jnp.concatenate([part[...] for part in sums_attn], axis=1)
    none = jnp.zeros_like(attn)
    attn = jnp.concatenate([jnp.where(core == 0, attn, none), jnp.where(core == 0, none, attn)], axis=1)
    mid, out = sums_mid[...], sums_out[...]
    rows = [attn, mid[3:4], out[1:2], *total, mid[0:3], out[0:1]]
    n_up = d_b_up.shape[1] // width
    for c in range(2):
        for j in range(n_up):
            rows.append(jnp.where(core == c, d_b_up[:, j * width : (j + 1) * width], 0.0))
    rows = jnp.concatenate(rows, axis=0)
    sums[: rows.shape[0], :] = rows
    sums[rows.shape[0] :, :] = jnp.zeros((sums.shape[0] - rows.shape[0], width), F32)


def home_kernel(flags, keep, came, mixed, d_tokens):
    x = flags[1]
    for j, out in enumerate((mixed, d_tokens)):
        out[x] = keep[j]
        out[1 - x] = came[j]


def table_kernel(meta, *refs):
    scores, (out, grid_out, strip, wide_ds) = refs[:-4], refs[-4:]
    heads = wide_ds.shape[0]
    depth = grid_out.shape[1]
    rows = 144
    lane = lax.broadcasted_iota(jnp.int32, (1, 128), 1)
    column = lax.broadcasted_iota(jnp.int32, (8, 128), 0)
    wide_ds[:, :, ROW_LEN:, :] = jnp.zeros(wide_ds.shape[:2] + (wide_ds.shape[2] - ROW_LEN, 128), F32)

    def widen(i, carry):
        here = pl.ds(pl.multiple_of(i * rows, 16), rows)
        for h in range(heads):
            part = scores[h // 2][h % 2, here, :].astype(F32)
            for kb in range(4):
                wide_ds[h, kb, here, :] = part[:, 128 * kb : 128 * kb + 128]
            wide_ds[h, 4, here, 0:64] = part[:, 512:576]
        return carry

    lax.fori_loop(0, ROW_LEN // rows, widen, 0)
    grid_out[...] = jnp.zeros_like(grid_out)
    for g in range(IMGS + 1):
        b, e, s, w, low, stop, first, last, groups = segment_loops(meta, g)

        def clear(pair, carry):
            for n in range(3):
                strip[n, 2 * pair] = jnp.zeros(strip.shape[2:], F32)
                strip[n, 2 * pair + 1] = jnp.zeros(strip.shape[2:], F32)
            return carry

        lax.fori_loop(low, stop, clear, 0)

        for size in range(1, 4):

            def lines(turn, carry, b=b, e=e, s=s, w=w, size=size, first=first, last=last):
                found = []
                for extra in range(2):
                    y = first + 2 * turn + extra
                    stop_column = jnp.where(y < last, w, 0)
                    p0 = s + jnp.minimum(y, last - 1) * w
                    off = STRIP - p0
                    j0 = off // 128
                    r = off - j0 * 128
                    for n in range(size):
                        here = pl.ds(p0 + 8 * n, 8)
                        inside = column < stop_column - 8 * n
                        moved = []
                        for kb in range(5):
                            place = lane + kb * 128
                            keep = inside & (place >= b) & (place < e)
                            piece = [jnp.where(keep, wide_ds[h, kb, here, :], 0.0) for h in range(heads)]
                            moved.append(pltpu.roll(jnp.concatenate(piece, axis=0), r, 1))
                        zero = jnp.zeros_like(moved[0])
                        moved = [zero] + moved + [zero]
                        for kb in range(6):
                            found.append((n, j0 + kb, jnp.where(lane >= r, moved[kb + 1], moved[kb])))
                for n, block, part in found:
                    strip[n, block] += part
                return carry

            lax.fori_loop(0, jnp.where(groups == size, (last - first + 1) // 2, 0), lines, 0)

        def fold(pair, carry, w=w):
            sides = [jnp.concatenate([strip[n, 2 * pair + j] for n in range(3)], axis=0) for j in range(2)]
            whole = jnp.concatenate(sides, axis=1)
            grid_out[...] += lax.dot_general(
                whole.astype(BF), strip_onehot(pair, w, depth), (((1,), (1,)), ((), ())), preferred_element_type=F32
            )
            return carry

        lax.fori_loop(low, stop, fold, 0)

    total = jnp.zeros((heads, FLAT), F32)
    for c in range(GRID):
        rows_c = [(c // 8 * heads + h) * 8 + c % 8 for h in range(heads)]
        part = jnp.concatenate([grid_out[i : i + 1, :] for i in rows_c], axis=0)
        pieces = [part, jnp.zeros((heads, FLAT - depth - SIDE * c), F32)]
        if c:
            pieces.insert(0, jnp.zeros((heads, SIDE * c), F32))
        total = total + jnp.concatenate(pieces, axis=1)
    out[...] = total


def vmem():
    return pl.BlockSpec(memory_space=pltpu.VMEM)


def smem():
    return pl.BlockSpec(memory_space=pltpu.SMEM)


def params(mib):
    return pltpu.CompilerParams(vmem_limit_bytes=mib * 1024 * 1024)


def cost(us):
    return pl.CostEstimate(flops=int(us * 600_000_000), bytes_accessed=1_000, transcendentals=0)


def strip_scratch(heads):
    return [
        pltpu.VMEM((3, BLOCKS, heads * 8, 128), F32),
        pltpu.VMEM((heads, 5, ROW_LEN + 32, 128), F32),
    ]


def hidden_kernel(flags, own, came, w, b, act, slope, h2):
    width = w.shape[0]
    n = h2.shape[0] // 2

    @pl.when(pl.program_id(0) == 0)
    def _():
        h2[:n] = own[...].reshape(n, width)
        h2[n:] = came[...].reshape(n, width)

    x = jnp.dot(h2[...], w[...], preferred_element_type=F32) + b[...].astype(F32)
    size = jnp.abs(x)
    t = 1.0 / (1.0 + (0.3275911 * 0.7071067811865476) * size)
    bell = jnp.exp(-0.5 * x * x)
    tail = t * (0.254829592 + t * (-0.284496736 + t * (1.421413741 + t * (-1.453152027 + t * 1.061405429))))
    tail = 0.5 * tail * bell
    phi = jnp.where(x >= 0, 1.0 - tail, tail)
    act[...] = (x * phi).astype(BF)
    slope[...] = (phi + x * (bell * 0.3989422804014327)).astype(BF)


def fixed(array, part=None):
    if part is None:
        return pl.BlockSpec(array.shape, lambda i: (0,) * array.ndim)
    return pl.BlockSpec((1,) + array.shape[1:], lambda i: (part,) + (0,) * (array.ndim - 1))


def join_kernel(places, own, came, *outs):
    n = own.shape[0]
    rows = own.shape[1]
    at = 0
    for out in outs:
        for high in range(out.shape[1] // rows):
            cols = slice(at, at + out.shape[2])
            at += out.shape[2]
            for i in range(n):
                out[places[i], high * rows : (high + 1) * rows, :] = own[i, :, cols]
                out[places[n + i], high * rows : (high + 1) * rows, :] = came[i, :, cols]


def first_join_kernel(places, own, came, w, vecs):
    n = own.shape[0]
    cols = w.shape[2]
    total = jnp.zeros((own.shape[1], own.shape[2] - cols), F32)
    for i in range(n):
        w[places[i]] = own[i, :, :cols]
        w[places[n + i]] = came[i, :, :cols]
        total = total + own[i, :, cols:].astype(F32) + came[i, :, cols:].astype(F32)
    for v in range(vecs.shape[0]):
        vecs[v : v + 1, :] = jnp.concatenate([total[3 * v + j : 3 * v + j + 1] for j in range(3)], axis=1)


def cat_kernel(flags, *refs):
    out, at = refs[-1], 0
    for part in refs[:-1]:
        out[at : at + part.shape[0]] = part[...]
        at += part.shape[0]


def add_kernel(flags, a, b, *outs):
    at = 0
    for out in outs:
        n = out.shape[0]
        out[...] = (a[at : at + n].astype(F32) + b[at : at + n].astype(F32)).astype(BF)
        at += n


def sum_kernel(flags, *refs):
    total = refs[0][...].astype(F32)
    for part in refs[1:-1]:
        total = total + part[...].astype(F32)
    refs[-1][...] = total.astype(refs[-1].dtype)


def grad_kernel(places, *refs):
    keep, give, full = refs[-3:]
    at = 0
    for a, b in zip(refs[:-3:2], refs[1:-3:2]):
        cols = slice(at, at + b.shape[1])
        at += b.shape[1]
        if a.shape[0] == full.shape[0]:
            full[:, cols] = (a[...].astype(F32) + b[...].astype(F32)).astype(BF)
            continue
        step = 256
        for t in range(full.shape[0] // step):
            here = slice(t * step, t * step + step)
            made = lax.dot_general(a[:, here], b[...], (((0,), (0,)), ((), ())), preferred_element_type=F32)
            full[here, cols] = made.astype(BF)
    n, rows, _ = keep.shape
    width = full.shape[1]
    block = full.shape[0] // (2 * n)
    for high in range(block // rows):
        there = slice(high * width, (high + 1) * width)
        for i in range(n):
            for out, j in ((keep, places[i]), (give, places[n + i])):
                out[i, :, there] = full[pl.ds(pl.multiple_of(j * block + high * rows, 16), rows), :]


def proj_grad_kernel(flags, joined, d_branch, keep, give):
    core = flags[0]
    n = keep.shape[1]
    width = joined.shape[-1]
    made = lax.dot_general(
        joined[...].reshape(-1, width), d_branch[...], (((0,), (0,)), ((), ())), preferred_element_type=F32
    )
    low, high = made[:, :n], made[:, n:]
    keep[...] = jnp.where(core == 0, low, high).astype(BF)
    give[...] = jnp.where(core == 0, high, low).astype(BF)


def after(array, *others):
    others = tuple(other for other in others if other is not None)
    return lax.optimization_barrier((array,) + others)[0] if others else array


class Net:
    def __init__(self, dp, seq):
        self.dp, self.seq = dp, seq
        self.fast = dp == 8
        self.last = None
        at_seq = lax.axis_index("seq")
        self.core = at_seq % 2
        self.x = at_seq // 2
        at_dp = lax.axis_index("dp")

        def table(fn):
            pairs = []
            for d in range(dp):
                for s in range(seq):
                    d2, s2 = fn(d, s)
                    pairs.append((d * seq + s, d2 * seq + s2))
            return pairs

        self.to_core = table(lambda d, s: (d, s ^ 1))
        self.to_x = table(lambda d, s: (d, s ^ 2))
        self.flags = jnp.stack([self.core, self.x]).astype(jnp.int32)
        if self.fast:
            self.phases = (
                table(lambda d, s: (d ^ 4, s)),
                table(lambda d, s: (d ^ 2, s)),
                table(lambda d, s: (d, s ^ 2) if s % 2 == 0 else (d ^ 1, s)),
                table(lambda d, s: (d ^ 1, s) if s % 2 == 0 else (d, s ^ 2)),
            )
            rel = jnp.arange(16, dtype=jnp.int32)
            d1, d2, d3, d4 = rel % 2, (rel // 2) % 2, (rel // 4) % 2, rel // 8
            by_x = jnp.where(self.core == 0, d3, d4)
            by_y = jnp.where(self.core == 0, d4, d3)
            self.places = ((at_dp * 2 + self.x) ^ (d1 * 8 + d2 * 4 + by_y * 2 + by_x)).astype(jnp.int32)

    def pin(self, array):
        return array if self.last is None else after(array, self.last)

    def call(self, kernel, us, outs, args, scratch=(), mib=8):
        got = pl.pallas_call(
            kernel,
            out_shape=tuple(jax.ShapeDtypeStruct(shape, kind) for shape, kind in outs),
            in_specs=[smem()] + [vmem()] * (len(args) - 1),
            out_specs=(vmem(),) * len(outs),
            scratch_shapes=list(scratch),
            compiler_params=params(mib),
            cost_estimate=cost(us),
            name=getattr(kernel, "func", kernel).__name__,
        )(self.pin(args[0]), *args[1:])
        self.last = got[0]
        return got

    def send(self, array, pairs):
        return lax.ppermute(array, BOTH, pairs)

    def by_core(self, own, other, axis):
        first = self.core == 0
        return jnp.stack([jnp.where(first, own, other), jnp.where(first, other, own)], axis=axis)

    def pick(self, array, index, axis):
        return lax.dynamic_index_in_dim(array, index, axis, keepdims=False)

    def bias_of(self, meta, flat, segment):
        heads = flat.shape[0]
        return self.call(
            bias_kernel,
            12,
            (((2, ROW_LEN, ROW_LEN), BF),) * (heads // 2),
            (meta, flat, segment[:, None], segment[None, :]),
            scratch=[pltpu.VMEM((heads * GRID, DEPTH), F32)] + strip_scratch(heads),
            mib=16,
        )

    def table_of(self, meta, scores):
        heads = 2 * len(scores)
        return self.call(
            table_kernel,
            12,
            (((heads, FLAT), F32),),
            (meta, *scores),
            scratch=[pltpu.VMEM((heads * GRID, DEPTH), F32)] + strip_scratch(heads),
            mib=16,
        )[0]

    def hidden(self, own, came, w, b):
        rows = 2 * own.size // w.shape[0]
        depth, cols = w.shape
        tile = 256
        out = jax.ShapeDtypeStruct((rows, cols), BF)
        got = pl.pallas_call(
            hidden_kernel,
            grid=(cols // tile,),
            out_shape=(out, out, jax.ShapeDtypeStruct((rows, depth), BF)),
            in_specs=[
                smem(),
                fixed(own),
                fixed(came),
                pl.BlockSpec((depth, tile), lambda i: (0, i)),
                pl.BlockSpec((1, tile), lambda i: (0, i)),
            ],
            out_specs=(pl.BlockSpec((rows, tile), lambda i: (0, i)),) * 2 + (pl.BlockSpec((rows, depth), lambda i: (0, 0)),),
            compiler_params=params(8),
            cost_estimate=cost(6),
            name="hidden",
        )(self.pin(self.flags), own, came, w, b)
        self.last = got[0]
        return got

    def hidden_back(self, d_after, w_down, slope, w_up):
        rows, cols = slope.shape
        width = w_up.shape[0]
        tile = cols // 2
        got = pl.pallas_call(
            hidden_back_kernel,
            grid=(cols // tile,),
            out_shape=(
                jax.ShapeDtypeStruct((rows, cols), BF),
                jax.ShapeDtypeStruct((1, cols), F32),
                jax.ShapeDtypeStruct((rows // 2, width), F32),
                jax.ShapeDtypeStruct((rows // 2, width), BF),
            ),
            in_specs=[
                smem(),
                fixed(d_after),
                pl.BlockSpec((tile, width), lambda i: (i, 0)),
                pl.BlockSpec((rows, tile), lambda i: (0, i)),
                pl.BlockSpec((width, tile), lambda i: (0, i)),
            ],
            out_specs=(
                pl.BlockSpec((rows, tile), lambda i: (0, i)),
                pl.BlockSpec((1, tile), lambda i: (0, i)),
                pl.BlockSpec((rows // 2, width), lambda i: (0, 0)),
                pl.BlockSpec((rows // 2, width), lambda i: (0, 0)),
            ),
            scratch_shapes=[pltpu.VMEM((rows, width), F32)],
            compiler_params=params(14),
            cost_estimate=cost(5),
            name="hidden_back",
        )(self.pin(self.flags), d_after, w_down, slope, w_up)
        self.last = got[0]
        return got

    def gather(self, block):
        return Gather(self, block) if self.fast else WholeGather(self, block)

    def library_gather(self, block):
        if not self.fast:
            return WholeGather(self, block).got
        groups = [[(d * 2 + x) * 2 + c for d in range(self.dp) for x in range(2)] for c in range(2)]
        return lax.all_gather(block, BOTH, axis=0, axis_index_groups=groups)

    def reduce(self, shape, *pairs):
        if self.fast:
            return Reduce(self, shape, pairs)
        made = []
        for a, b in pairs:
            made.append((wide(a) + wide(b) if a.shape == b.shape else dot_t(a, b)).astype(BF))
        return WholeReduce(self, jnp.concatenate(made, axis=1))


class Gather:
    def __init__(self, net, block):
        self.net, self.got, self.step = net, block[None], 0
        self.go()

    def go(self):
        self.came = self.net.send(self.got, self.net.phases[self.step])

    def next(self):
        out = ((2 * self.got.shape[0],) + self.got.shape[1:], BF)
        self.got = self.net.call(cat_kernel, 0.6, (out,), (self.net.flags, self.got, self.came))[0]
        self.step += 1
        self.go()

    def join(self, *shapes):
        outs = [((2 * self.got.shape[0],) + shape, BF) for shape in shapes]
        return self.net.call(join_kernel, 0.7, outs, (self.net.places, self.got, self.came))

    def first_join(self, cols):
        _, rows, width = self.got.shape
        outs = (((2 * self.got.shape[0], rows, cols), BF), ((rows // 3, 3 * (width - cols)), F32))
        return self.net.call(first_join_kernel, 0.7, outs, (self.net.places, self.got, self.came))


class WholeGather:
    def __init__(self, net, block):
        block = lax.all_gather(block, "dp", axis=0)
        other = net.send(block, net.to_x)
        first = net.x == 0
        block = jnp.stack([jnp.where(first, block, other), jnp.where(first, other, block)], axis=1)
        self.got = block.reshape((2 * net.dp,) + block.shape[2:])

    def next(self):
        pass

    def join(self, *shapes):
        cut = shapes[0][1]
        return (self.got,) if len(shapes) == 1 else (self.got[:, :, :cut], self.got[:, :, cut:])


class Reduce:
    def __init__(self, net, shape, pairs):
        self.net, self.step = net, 3
        arrays = [array for pair in pairs for array in pair]
        depth = pairs[0][0].shape[0] if pairs[0][0].shape == pairs[0][1].shape else pairs[0][0].shape[1]
        width = sum(b.shape[1] for _, b in pairs)
        out = ((8,) + shape, BF)
        self.keep, self.give = net.call(
            grad_kernel, 3, (out, out), (net.places, *arrays), scratch=[pltpu.VMEM((depth, width), BF)]
        )
        self.go()

    def go(self):
        self.came = self.net.send(self.give, self.net.phases[self.step])

    def next(self):
        out = ((self.keep.shape[0] // 2,) + self.keep.shape[1:], BF)
        self.keep, self.give = self.net.call(add_kernel, 1, (out, out), (self.net.flags, self.keep, self.came))
        self.step -= 1
        self.go()

    def end(self):
        out = ((1,) + self.keep.shape[1:], F32)
        return self.net.call(sum_kernel, 0.6, (out,), (self.net.flags, self.keep, self.came))[0][0]


class WholeReduce:
    def __init__(self, net, full):
        blocks = full.reshape((net.dp, 2, -1) + full.shape[1:])
        came = net.send(net.pick(blocks, 1 - net.x, 1), net.to_x)
        summed = net.pick(blocks, net.x, 1).astype(F32) + came.astype(F32)
        self.sum = lax.psum_scatter(summed, "dp", scatter_dimension=0, tiled=False)

    def next(self):
        pass

    def end(self):
        return self.sum


class Total:
    def __init__(self, net, array):
        self.net, self.sum, self.step = net, array, 0
        if net.fast:
            self.came = net.send(array, net.phases[0])
        else:
            self.sum = lax.psum(array + net.send(array, net.to_x), "dp")

    def next(self):
        if self.net.fast:
            out = (self.sum.shape, F32)
            self.sum = self.net.call(sum_kernel, 0.6, (out,), (self.net.flags, self.sum, self.came))[0]
            self.step += 1
            if self.step < 4:
                self.came = self.net.send(self.sum, self.net.phases[self.step])


def wide(array):
    return array.astype(F32)


def dot(a, b):
    return jnp.dot(a, b, preferred_element_type=F32)


def dot_t(a, b):
    return lax.dot_general(a, b, (((0,), (0,)), ((), ())), preferred_element_type=F32)


def local(
    dp,
    seq,
    tokens,
    image_lengths,
    grid_widths,
    qkv_weight,
    q_bias,
    v_bias,
    proj_weight,
    proj_bias,
    fc1_weight,
    fc1_bias,
    fc2_weight,
    fc2_bias,
    norm1_gain,
    norm1_bias,
    norm2_gain,
    norm2_bias,
    scale1,
    scale2,
    bias_table,
    out_grad,
):
    net = Net(dp, seq)
    call, flags, core, at_x = net.call, net.flags, net.core, net.x
    row_count, shard, width = tokens.shape
    heads = bias_table.shape[1]
    own_heads = heads // 2
    own_feats = width // 2
    n_dev = dp * seq
    chips = n_dev // 2
    rows_w = width // n_dev
    ff = fc2_weight.shape[0] * n_dev
    rows_f = ff // n_dev
    at = lax.axis_index("dp") * seq + lax.axis_index("seq")
    at_chip = lax.axis_index("dp") * 2 + at_x

    lanes = jnp.arange(width, dtype=jnp.int32)
    spots = (lanes[None] // rows_w == at) & (lanes[None] % rows_w == jnp.arange(rows_w, dtype=jnp.int32)[:, None])
    vecs = [q_bias, v_bias, proj_bias, fc2_bias, norm1_gain, norm1_bias, norm2_gain, norm2_bias, scale1, scale2]
    n_vec = len(vecs)
    placed = dot(jnp.stack(vecs), spots.astype(BF)).astype(BF)
    n_up = ff // 2 // width
    lanes_up = jnp.arange(ff // 2, dtype=jnp.int32)
    spots_up = (lanes_up[None] // rows_f == at_chip) & (lanes_up[None] % rows_f == jnp.arange(rows_f, dtype=jnp.int32)[:, None])
    placed_up = dot(fc1_bias[None], spots_up.astype(BF)).astype(BF).reshape(n_up, width)
    mine = (jnp.arange(2) == core)[:, None, None]
    placed_up = jnp.where(mine, placed_up[None], jnp.zeros((), BF)).reshape(2 * n_up, width)
    placed = jnp.concatenate([placed, placed_up, jnp.zeros((16 - n_vec - 2 * n_up, width), BF)])

    low = ((rows_w, 3 * own_feats), BF)
    keep, give = call(split_kernel, 0.5, (low, low), (flags, qkv_weight))
    attn_block = net.by_core(keep, net.send(give, net.to_core), 0).reshape(2 * rows_w, 3 * own_feats)
    placed = placed + net.send(placed, net.to_core)
    if net.fast:
        attn_block = jnp.concatenate([attn_block, placed.reshape(48, 256)], axis=1)
    attn_chain = net.gather(attn_block)

    their_tokens, their_grad = after(tokens, attn_block), after(out_grad, attn_block)
    theirs = jnp.stack([net.pick(their_tokens, 1 - at_x, 0), net.pick(their_grad, 1 - at_x, 0)])
    token_came = net.send(theirs, net.to_x)
    proj_view = after(proj_weight, attn_block).reshape(rows_w, 2, own_feats)
    fc1_view = after(fc1_weight, attn_block).reshape(rows_w, chips, 2, rows_f)
    views = []
    for index in (core, 1 - core):
        up = net.pick(fc1_view, index, 2).reshape(rows_w, ff // 2)
        views.append(jnp.concatenate([up, net.pick(proj_view, index, 1)], axis=1))
    up_came = net.send(views[1], net.to_core)

    lengths = net.pick(image_lengths, at_x, 0)
    widths = net.pick(grid_widths, at_x, 0)
    meta, segment = layout(after(lengths, attn_block), after(widths, attn_block))
    flat = jnp.transpose(after(bias_table, attn_block).reshape(SIDE, SIDE, heads), (2, 1, 0)).reshape(heads, SIDE * SIDE)
    flat = jnp.pad(wide(lax.dynamic_slice_in_dim(flat, core * own_heads, own_heads)), ((0, 0), (0, FLAT - SIDE * SIDE)))

    chunk = (2, shard, width)
    attn_chain.next()
    (up_block,) = call(stack_kernel, 0.5, (((2 * rows_w, ff // 2 + own_feats), BF),), (flags, views[0], up_came))
    up_chain = net.gather(up_block)
    attn_chain.next()
    (both,) = call(start_kernel, 0.5, (((2,) + chunk, BF),), (flags, tokens, out_grad, token_came))
    both_came = net.send(both, net.to_core)
    attn_chain.next()
    up_chain.next()
    down_block = fc2_weight if not net.fast else jnp.concatenate([fc2_weight[: 2 * rows_w], fc2_weight[2 * rows_w :]], axis=1)
    down_chain = net.gather(net.pin(down_block))
    biases = net.bias_of(meta, flat, segment)
    up_chain.next()
    if net.fast:
        w_qkv, vectors = attn_chain.first_join(3 * own_feats)
    else:
        (w_qkv,) = attn_chain.join((2 * rows_w, 3 * own_feats))
        vectors = Total(net, wide(placed)).sum
    b_up = net.pick(vectors[n_vec : n_vec + 2 * n_up].reshape(2, 1, ff // 2), core, 0)

    row = (ROW_LEN, 128)
    part_heads = (2, shard, 128)
    square = (2, ROW_LEN, ROW_LEN)
    pairs, keeps, cames = [], [], []
    for t, bias in enumerate(biases):
        outs = ((row, BF),) * 3 + ((square, BF), (part_heads, BF), (part_heads, BF))
        if t == 0:
            outs = outs + (((ROW_LEN, width), BF),)
            args = (flags, both, both_came, w_qkv, vectors, bias)
        else:
            args = (flags, h1, w_qkv, vectors, bias)
        got = call(functools.partial(attn_fwd_kernel, t == 0, t), 5, outs, args, scratch=[pltpu.VMEM(row, BF)])
        if t == 0:
            h1 = got[6]
        pairs.append(got[:4])
        keeps.append(got[4])
        cames.append(net.send(got[5], net.to_core))
        if t == 0:
            down_chain.next()
            up_chain.next()
        if t == 1:
            down_chain.next()
    fc1_all, pj_own = up_chain.join((2 * rows_w, ff // 2), (2 * rows_w, own_feats))
    pj_came = net.send(pj_own, net.to_core)
    joined, branch, middle, h2, d_after = call(
        proj_kernel,
        3,
        ((chunk, BF), (chunk, BF), (chunk, F32), (chunk, BF), ((ROW_LEN, width), BF)),
        (flags, *keeps, *cames, pj_own, pj_came, both, both_came, vectors),
    )
    h2_came = net.send(h2, net.to_core)
    down_chain.next()
    w_up = fc1_all.reshape(width, ff // 2)
    act, slope, h2_all = net.hidden(h2, h2_came, w_up, b_up)
    down_sum = net.reduce((rows_f, width), (act, d_after))
    w_down = down_chain.join((rows_f, width))[0].reshape(ff // 2, width)
    d_before, d_b_up, keep, give = net.hidden_back(d_after, w_down, slope, w_up)
    mid_came = net.send(give, net.to_core)
    own = 2 * shard
    after_keep, after_give = call(after_kernel, 2, (((own, width), F32), ((own, width), BF)), (flags, act, w_down))
    after_came = net.send(after_give, net.to_core)
    half = (2, shard, own_feats)
    d_middle, d_branch, keep, give, sums_mid = call(
        middle_back_kernel,
        3,
        ((chunk, F32), ((own, width), BF), (half, BF), (half, BF), ((4, width), F32)),
        (flags, keep, mid_came, middle, both, branch, pj_own, pj_came, vectors),
    )
    heads_came = net.send(give, net.to_core)
    out = ((width, own_feats), BF)
    proj_keep, proj_give = call(proj_grad_kernel, 2, (out, out), (flags, joined, d_branch))
    proj_came = net.send(proj_give, net.to_core)

    d_joints, scores, sums_attn = [], [], []
    for t, (q, k, v, prob) in enumerate(pairs):
        d_joint, ds, sums = call(
            functools.partial(attn_bwd_kernel, t),
            5,
            (((ROW_LEN, 384), BF), (square, BF), ((2, 128), F32)),
            (flags, q, k, v, keep, heads_came, prob),
            scratch=[pltpu.VMEM(row, BF), pltpu.VMEM((128, ROW_LEN), F32), pltpu.VMEM((128, ROW_LEN), F32)],
        )
        d_joints.append(d_joint)
        scores.append(ds)
        sums_attn.append(sums)
        if t == 0:
            up_sum = net.reduce((2 * rows_w, ff // 2 + own_feats), (h2_all, d_before), (proj_keep, proj_came))
            down_sum.next()
        if t == 1:
            mixed, sums_out = call(
                mixed_kernel,
                2,
                ((chunk, BF), ((2, width), F32)),
                (flags, after_keep, after_came, middle, both, d_after, vectors),
            )
    attn_sum = net.reduce((2 * rows_w, 3 * own_feats), *[(h1, d_joint) for d_joint in d_joints])
    keep, give = call(h1_back_kernel, 3, ((chunk, F32), (chunk, BF)), (flags, *d_joints, w_qkv))
    h1_came = net.send(give, net.to_core)
    down_sum.next()
    up_sum.next()
    table = net.table_of(meta, scores)
    attn_sum.next()
    down_sum.next()
    up_sum.next()

    keep, give, smalls = call(
        end_kernel,
        2,
        ((chunk, BF), (chunk, BF), ((16, width), F32)),
        (flags, keep, h1_came, both, d_middle, mixed, vectors, *sums_attn, sums_mid, sums_out, d_b_up),
    )
    smalls_came = net.send(smalls, net.to_core)
    out_came = net.send(give, net.to_x)
    (smalls,) = call(sum_kernel, 0.6, (((16, width), F32),), (flags, smalls, smalls_came))
    total = Total(net, jnp.concatenate([smalls.reshape(-1, 128), table.reshape(-1, 128)]))
    total.next()
    total.next()
    up_sum.next()
    attn_sum.next()
    g_down = down_sum.end()
    mixed, tokens_grad = call(home_kernel, 1, ((chunk, BF), (chunk, BF)), (flags, keep, out_came))
    total.next()
    attn_sum.next()
    g_up = up_sum.end()
    total.next()
    g_attn = attn_sum.end()

    def home(block, groups, cols):
        view = block.reshape(2, rows_w, groups, cols)
        came = net.send(net.pick(view, 1 - core, 0), net.to_core)
        return net.by_core(net.pick(view, core, 0), came, 2).reshape(rows_w, groups * 2 * cols)

    g_proj = home(g_up[:, ff // 2 :], 1, own_feats)
    g_up = home(g_up[:, : ff // 2], chips, rows_f)
    packed = total.sum
    sums = packed[: smalls.size // 128].reshape(smalls.shape)
    table = packed[smalls.size // 128 :].reshape(own_heads, FLAT)
    table = net.by_core(table, net.send(table, net.to_core), 0).reshape(heads, FLAT)[:, : SIDE * SIDE]
    table_grad = jnp.transpose(table.reshape(heads, SIDE, SIDE), (2, 1, 0)).reshape(SIDE * SIDE, heads)
    g_small = lax.dynamic_slice_in_dim(sums[:n_vec], at * rows_w, rows_w, 1)
    g_up_small = net.pick(sums[n_vec : n_vec + 2 * n_up].reshape(2, ff // 2), core, 0)
    g_up_small = lax.dynamic_slice_in_dim(g_up_small, at_chip * rows_f, rows_f)
    smalls = [g_small[j] for j in range(n_vec)] + [g_up_small]

    g_attn = g_attn.reshape(2 * rows_w, 3, 3, 128).transpose(0, 2, 1, 3).reshape(2 * rows_w, 3 * own_feats)
    g_qkv = home(g_attn, 3, own_feats)
    g_query, g_value, g_bproj, g_bdown, g_gain1, g_shift1, g_gain2, g_shift2, g_layer1, g_layer2, g_bup = smalls
    return (
        mixed,
        tokens_grad,
        g_qkv,
        g_query,
        g_value,
        g_proj,
        g_bproj,
        g_up,
        g_bup,
        g_down,
        g_bdown,
        g_gain1,
        g_shift1,
        g_gain2,
        g_shift2,
        g_layer1,
        g_layer2,
        table_grad,
    )


def solution(mesh):
    both = P(BOTH)
    both2 = P(BOTH, None)
    act = P("dp", "seq", None)
    in_specs = (act, P("dp", None), P("dp", None), both2, both, both, both2, both, both2, both, both2)
    in_specs += (both,) * 7 + (P(), act)
    out_specs = (act, act, both2, both, both, both2, both, both2, both, both2) + (both,) * 7 + (P(),)
    body = functools.partial(local, mesh.shape["dp"], mesh.shape["seq"])
    return jax.shard_map(body, mesh=mesh, in_specs=in_specs, out_specs=out_specs, check_vma=False)
```

```python
import functools

import jax
import jax.numpy as jnp
from jax import lax
from jax.experimental import pallas as pl
from jax.experimental.pallas import tpu as pltpu
from jax.sharding import PartitionSpec as P

GRID = 24
SIDE = 2 * GRID - 1
ROW_LEN = 576
IMGS = 4
EPS = 1e-06
STRIP = 640
BLOCKS = 12
DEPTH = 1152
FLAT = 2304
BF = jnp.bfloat16
F32 = jnp.float32
BOTH = ("dp", "seq")
VECS = ("q", "v", "b_proj", "b_down", "gain1", "shift1", "gain2", "shift2", "scale1", "scale2")


def layout(lengths, widths):
    ends = jnp.cumsum(lengths).astype(jnp.int32)
    starts = ends - lengths
    total = ends[-1]
    full = jnp.full((1,), ROW_LEN, jnp.int32)
    meta = jnp.stack(
        [
            jnp.concatenate([starts, total[None]]),
            jnp.concatenate([ends, full]),
            jnp.concatenate([starts, jnp.zeros((1,), jnp.int32)]),
            jnp.concatenate([widths, jnp.full((1,), GRID, jnp.int32)]),
        ]
    ).astype(jnp.int32)
    places = jnp.arange(ROW_LEN, dtype=jnp.int32)
    segment = jnp.sum((places[:, None] >= ends[None, :]).astype(jnp.int32), axis=1)
    return meta, segment


def strip_range(b, e):
    length = e - b
    return (STRIP - length) // 256, jnp.minimum((STRIP + length + GRID) // 256, BLOCKS // 2 - 1)


def strip_onehot(pair, w, depth):
    lane = lax.broadcasted_iota(jnp.int32, (1, 256), 1) + (pair * 256 - STRIP + 80 * w)
    line = jnp.floor((lane.astype(F32) + 0.5) / jnp.full((1, 256), w, jnp.int32).astype(F32)).astype(jnp.int32)
    column = lane - line * w
    level = jnp.clip(80 - line, 1 - GRID, GRID - 1) + (GRID - 1)
    code = (GRID - 1 - column) * SIDE + level
    return (lax.broadcasted_iota(jnp.int32, (depth, 256), 0) == code).astype(F32).astype(BF)


def segment_loops(meta, g):
    b, e, s, w = meta[0, g], meta[1, g], meta[2, g], meta[3, g]
    low, high = strip_range(b, e)
    stop = jnp.where(e > b, high + 1, low)
    first, last = (b - s) // w, jnp.where(e > b, (e - 1 - s) // w + 1, 0)
    return b, e, s, w, low, stop, first, last, (w + 7) // 8


def bias_kernel(meta, flat, seg_col, seg_row, *refs):
    outs, (tab, strip, bias) = refs[:-3], refs[-3:]
    heads = bias.shape[0]
    depth = tab.shape[1]
    lane = lax.broadcasted_iota(jnp.int32, (1, 128), 1)
    for c in range(GRID):
        moved = flat[:, SIDE * c : SIDE * c + depth]
        for h in range(heads):
            row = (c // 8 * heads + h) * 8 + c % 8
            tab[row : row + 1, :] = moved[h : h + 1]
    low_tab = tab[...].astype(BF)
    for g in range(IMGS + 1):
        b, e, s, w, low, stop, first, last, groups = segment_loops(meta, g)

        def build(pair, carry, w=w):
            made = jnp.dot(low_tab, strip_onehot(pair, w, depth), preferred_element_type=F32)
            for n in range(3):
                rows_n = slice(n * heads * 8, (n + 1) * heads * 8)
                strip[n, 2 * pair] = made[rows_n, :128]
                strip[n, 2 * pair + 1] = made[rows_n, 128:]
            return carry

        lax.fori_loop(low, stop, build, 0)

        for size in range(1, 4):

            def lines(turn, carry, b=b, s=s, w=w, g=g, size=size, first=first, last=last):
                found = []
                for y in (first + 2 * turn, jnp.minimum(first + 2 * turn + 1, last - 1)):
                    p0 = s + y * w
                    off = STRIP - p0
                    j0 = off // 128
                    r = off - j0 * 128
                    for n in range(size):
                        parts = [strip[n, j0 + kb] for kb in range(6)]
                        for kb in range(5):
                            moved = pltpu.roll(jnp.where(lane >= r, parts[kb], parts[kb + 1]), (128 - r) % 128, 1)
                            found.append((kb, pl.ds(p0 + 8 * n, 8), moved))
                for kb, here, moved in found:
                    for h in range(heads):
                        piece = moved[h * 8 : (h + 1) * 8]
                        if g == IMGS:
                            piece = jnp.where(lane + kb * 128 >= b, piece, bias[h, kb, here, :])
                        bias[h, kb, here, :] = piece
                return carry

            lax.fori_loop(0, jnp.where(groups == size, (last - first + 1) // 2, 0), lines, 0)

    rows = 144

    def mask(i, carry):
        here = pl.ds(pl.multiple_of(i * rows, 16), rows)
        allowed = seg_col[here, :] == seg_row[...]
        for h in range(heads):
            offs = jnp.concatenate([bias[h, kb, here, :] for kb in range(5)], axis=1)[:, :ROW_LEN]
            outs[h // 2][h % 2, here, :] = jnp.where(allowed, offs, -1e30).astype(BF)
        return carry

    lax.fori_loop(0, ROW_LEN // rows, mask, 0)


def norm_parts(x):
    center = x - jnp.mean(x, axis=-1, keepdims=True)
    inverse = lax.rsqrt(jnp.mean(center * center, axis=-1, keepdims=True) + EPS)
    return center * inverse, inverse


def norm_back(normed, inverse, grad, gain):
    pulled = grad * gain
    mean = jnp.mean(pulled, axis=-1, keepdims=True)
    along = jnp.mean(pulled * normed, axis=-1, keepdims=True)
    return (pulled - mean - normed * along) * inverse


def vec(vecs, name):
    return vecs[VECS.index(name) : VECS.index(name) + 1, :].astype(F32)


def own_half(core, row):
    n = row.shape[1] // 2
    return jnp.where(core == 0, row[:, :n], row[:, n:])


def split_kernel(flags, w, keep, give):
    core = flags[0]
    n = w.shape[1] // 6
    for j in range(3):
        low, high = w[:, 2 * n * j : 2 * n * j + n], w[:, 2 * n * j + n : 2 * n * j + 2 * n]
        keep[:, n * j : n * j + n] = jnp.where(core == 0, low, high)
        give[:, n * j : n * j + n] = jnp.where(core == 0, high, low)


def stack_kernel(flags, own, came, out):
    core = flags[0]
    rows = own.shape[0]
    first = core == 0
    out[:rows] = jnp.where(first, own[...], came[...])
    out[rows:] = jnp.where(first, came[...], own[...])


def start_kernel(flags, tokens, out_grad, came, both):
    x = flags[1]
    both[0, x] = tokens[x]
    both[1, x] = out_grad[x]
    both[0, 1 - x] = came[0]
    both[1, 1 - x] = came[1]


def attn_fwd_kernel(first, t, flags, *refs):
    core = flags[0]
    if first:
        own, came, w, vecs, bias, qkv, b_up, p_out, keep, give, h1, joined = refs
        shard = own.shape[2]
        ups = vecs[len(VECS) : len(VECS) + 4, :]
        pairs = [jnp.concatenate([ups[2 * c : 2 * c + 1], ups[2 * c + 1 : 2 * c + 2]], axis=1) for c in range(2)]
        b_up[...] = jnp.where(core == 0, pairs[0], pairs[1])
        for a in range(2):
            for side, part in ((core, own), (1 - core, came)):
                normed, _ = norm_parts(part[0, a].astype(F32))
                normed = normed * vec(vecs, "gain1") + vec(vecs, "shift1")
                h1[pl.ds(pl.multiple_of((2 * a + side) * shard, 16), shard), :] = normed.astype(BF)
    else:
        h1, w, vecs, bias, qkv, p_out, keep, give, joined = refs
        shard = keep.shape[1]
    feats = w.shape[2] // 3
    cols = slice(128 * t, 128 * t + 128)

    def weight(j):
        return w[:, :, feats * j + 128 * t : feats * j + 128 * t + 128].reshape(h1.shape[1], 128)

    q_row, v_row = own_half(core, vec(vecs, "q"))[:, cols], own_half(core, vec(vecs, "v"))[:, cols]
    q, k, v = slice(0, 128), slice(128, 256), slice(256, 384)
    qkv[:, q] = ((jnp.dot(h1[...], weight(0), preferred_element_type=F32) + q_row) * 64**-0.5).astype(BF)
    qkv[:, k] = jnp.dot(h1[...], weight(1), preferred_element_type=F32).astype(BF)
    qkv[:, v] = (jnp.dot(h1[...], weight(2), preferred_element_type=F32) + v_row).astype(BF)
    rows = 144
    half = lax.broadcasted_iota(jnp.int32, (1, 128), 1) < 64

    def chunk(i, carry):
        here = pl.ds(pl.multiple_of(i * rows, 16), rows)
        q_tile = qkv[here, q]
        outs = []
        for sub in range(2):
            q_own = jnp.where(half if sub == 0 else ~half, q_tile, jnp.zeros_like(q_tile))
            score = lax.dot_general(q_own, qkv[:, k], (((1,), (1,)), ((), ())), preferred_element_type=F32)
            score = score + bias[sub, here, :].astype(F32)
            raised = jnp.exp(score - jnp.max(score, axis=1, keepdims=True))
            prob = (raised * (1.0 / jnp.sum(raised, axis=1, keepdims=True))).astype(BF)
            p_out[sub, here, :] = prob
            outs.append(jnp.dot(prob, qkv[:, v], preferred_element_type=F32))
        joined[here, :] = jnp.where(half, outs[0], outs[1]).astype(BF)
        return carry

    lax.fori_loop(0, ROW_LEN // rows, chunk, 0)
    for a in range(2):
        keep[a] = joined[pl.ds(pl.multiple_of((2 * a + core) * shard, 16), shard), :]
        give[a] = joined[pl.ds(pl.multiple_of((2 * a + 1 - core) * shard, 16), shard), :]


def by_core_in(core, own, came):
    return jnp.concatenate([jnp.where(core == 0, own, came), jnp.where(core == 0, came, own)], axis=-1)


def proj_kernel(flags, *refs):
    keeps, cames = refs[:3], refs[3:6]
    w_own, w_came, own, grads_came, vecs, joined, branch, middle, h2, d_after = refs[6:]
    core = flags[0]
    width = own.shape[-1]
    shard = own.shape[2]
    feats = width // 2
    for a in range(2):
        keep = jnp.concatenate([part[a] for part in keeps], axis=-1)
        came = jnp.concatenate([part[a] for part in cames], axis=-1)
        joined[a] = by_core_in(core, keep, came)
    weight = by_core_in(core, w_own[...].reshape(width, feats), w_came[...].reshape(width, feats))
    for a in range(2):
        out = jnp.dot(joined[a], weight, preferred_element_type=F32) + vec(vecs, "b_proj")
        branch[a] = out.astype(BF)
        mid = own[0, a].astype(F32) + vec(vecs, "scale1") * out
        middle[a] = mid
        for j, part in enumerate((own, grads_came)):
            here = slice((2 * j + a) * shard, (2 * j + a + 1) * shard)
            d_after[here, :] = (vec(vecs, "scale2") * part[1, a].astype(F32)).astype(BF)
        normed, _ = norm_parts(mid)
        h2[a] = (normed * vec(vecs, "gain2") + vec(vecs, "shift2")).astype(BF)


def after_kernel(flags, act, w, keep, give):
    n = keep.shape[0]
    keep[...] = jnp.dot(act[:n], w[...], preferred_element_type=F32)
    give[...] = jnp.dot(act[n:], w[...], preferred_element_type=F32).astype(BF)


def mixed_kernel(flags, keep, came, middle, own, d_after, vecs, mixed, sums):
    rows = middle.shape[0] * middle.shape[1]
    width = middle.shape[2]
    out = keep[...] + came[...].astype(F32) + vec(vecs, "b_down")
    mid = middle[...].reshape(rows, width)
    mixed[...] = (mid + vec(vecs, "scale2") * out).astype(BF).reshape(mixed.shape)
    g = own[1].reshape(rows, width).astype(F32)
    sums[0:1, :] = jnp.sum(g * out, axis=0, keepdims=True)
    sums[1:2, :] = jnp.sum(d_after[:rows].astype(F32), axis=0, keepdims=True)


def hidden_back_kernel(flags, d_after, w_down, slope, w_up, d_before, b_sum, keep, give, total):
    i = pl.program_id(0)
    width = w_up.shape[0]
    d_act = lax.dot_general(d_after[...], w_down[...], (((1,), (1,)), ((), ())), preferred_element_type=F32)
    low = (d_act * slope[...].astype(F32)).astype(BF)
    d_before[...] = low
    b_sum[...] = jnp.sum(low.astype(F32), axis=0, keepdims=True)
    d_h2 = lax.dot_general(low, w_up[...], (((1,), (1,)), ((), ())), preferred_element_type=F32)

    @pl.when(i == 0)
    def _():
        total[...] = d_h2

    @pl.when(i > 0)
    def _():
        total[...] += d_h2

    @pl.when(i == pl.num_programs(0) - 1)
    def _():
        n = keep.shape[0]
        keep[...] = total[:n]
        give[...] = total[n:].astype(BF)


def middle_back_kernel(flags, keep_in, came, middle, own, branch, w_own, w_came, vecs, d_middle, d_branch, keep, give, sums):
    core = flags[0]
    width = middle.shape[-1]
    shard = middle.shape[1]
    weight = by_core_in(core, w_own[...].reshape(width, width // 2), w_came[...].reshape(width, width // 2))
    total = [jnp.zeros((1, width), F32)] * 4
    for a in range(2):
        here = slice(a * shard, a * shard + shard)
        normed, inverse = norm_parts(middle[a])
        d_h2 = keep_in[here, :] + came[here, :].astype(F32)
        d_mid = own[1, a].astype(F32) + norm_back(normed, inverse, d_h2, vec(vecs, "gain2"))
        d_middle[a] = d_mid
        low = (vec(vecs, "scale1") * d_mid).astype(BF)
        d_branch[here, :] = low
        back = lax.dot_general(low, weight, (((1,), (1,)), ((), ())), preferred_element_type=F32).astype(BF)
        feats = width // 2
        keep[a] = jnp.where(core == 0, back[:, :feats], back[:, feats:])
        give[a] = jnp.where(core == 0, back[:, feats:], back[:, :feats])
        parts = (d_h2 * normed, d_h2, d_mid * branch[a].astype(F32), low.astype(F32))
        total = [t + jnp.sum(p, axis=0, keepdims=True) for t, p in zip(total, parts)]
    for j in range(4):
        sums[j : j + 1, :] = total[j]


def attn_bwd_kernel(t, flags, qkv, keep, came, p, d_joint, ds_out, sums, do, dkt, dvt):
    core = flags[0]
    shard = keep.shape[1]
    cols = slice(128 * t, 128 * t + 128)
    for a in range(2):
        do[pl.ds(pl.multiple_of((2 * a + core) * shard, 16), shard), :] = keep[a, :, cols]
        do[pl.ds(pl.multiple_of((2 * a + 1 - core) * shard, 16), shard), :] = came[a, :, cols]
    rows = 144
    half = lax.broadcasted_iota(jnp.int32, (1, 128), 1) < 64
    q, k, v = slice(0, 128), slice(128, 256), slice(256, 384)
    q_turn = jnp.transpose(qkv[:, q].astype(F32)).astype(BF)
    do_turn = jnp.transpose(do[...].astype(F32)).astype(BF)

    def chunk(i, carry):
        here = pl.ds(pl.multiple_of(i * rows, 16), rows)
        do_tile = do[here, :]
        outs = []
        for sub in range(2):
            do_own = jnp.where(half if sub == 0 else ~half, do_tile, jnp.zeros_like(do_tile))
            d_prob = lax.dot_general(do_own, qkv[:, v], (((1,), (1,)), ((), ())), preferred_element_type=F32)
            prob = p[sub, here, :].astype(F32)
            weighted = prob * d_prob
            delta = jnp.sum(weighted, axis=1, keepdims=True)
            low = (weighted - prob * delta).astype(BF)
            ds_out[sub, here, :] = low
            outs.append(jnp.dot(low, qkv[:, k], preferred_element_type=F32))
        dq = jnp.where(half, outs[0], outs[1]).astype(BF).astype(F32) * 64**-0.5
        d_joint[here, 0:128] = dq.astype(BF)
        return carry + jnp.sum(dq, axis=0, keepdims=True)

    sums[0:1, :] = lax.fori_loop(0, ROW_LEN // rows, chunk, jnp.zeros((1, 128), F32))
    for sub in range(2):
        part = slice(64 * sub, 64 * sub + 64)
        dkt[part, :] = jnp.dot(q_turn[part], ds_out[sub], preferred_element_type=F32)
        dvt[part, :] = jnp.dot(do_turn[part], p[sub], preferred_element_type=F32)
    dv = jnp.transpose(dvt[...]).astype(BF)
    d_joint[:, 128:256] = jnp.transpose(dkt[...]).astype(BF)
    d_joint[:, 256:384] = dv
    sums[1:2, :] = jnp.sum(dv.astype(F32), axis=0, keepdims=True)


def h1_back_kernel(flags, first, second, third, w, keep, give):
    core = flags[0]
    width = keep.shape[-1]
    shard = keep.shape[1]
    feats = w.shape[2] // 3
    parts = []
    for t in range(3):
        for j in range(3):
            parts.append(w[:, :, feats * j + 128 * t : feats * j + 128 * t + 128])
    weight = jnp.concatenate(parts, axis=2).reshape(width, 3 * feats)
    for a in range(2):
        for mine in range(2):
            side = core if mine else 1 - core
            here = pl.ds(pl.multiple_of((2 * a + side) * shard, 16), shard)
            part = jnp.concatenate([d_joint[here, :] for d_joint in (first, second, third)], axis=1)
            out = lax.dot_general(part, weight, (((1,), (1,)), ((), ())), preferred_element_type=F32)
            if mine:
                keep[a] = out
            else:
                give[a] = out.astype(BF)


def end_kernel(flags, keep_in, came, own, d_middle, mixed, vecs, *refs):
    sums_attn, (sums_mid, sums_out, d_b_up, keep, give, sums) = refs[:-6], refs[-6:]
    core, x = flags[0], flags[1]
    width = own.shape[-1]
    total = [jnp.zeros((1, width), F32)] * 2
    for a in range(2):
        side = x if a == 0 else 1 - x
        d_h1 = keep_in[side] + came[side].astype(F32)
        normed, inverse = norm_parts(own[0, side].astype(F32))
        out = d_middle[side] + norm_back(normed, inverse, d_h1, vec(vecs, "gain1"))
        to = keep if a == 0 else give
        to[0] = mixed[side]
        to[1] = out.astype(BF)
        parts = (d_h1 * normed, d_h1)
        total = [t + jnp.sum(p, axis=0, keepdims=True) for t, p in zip(total, parts)]
    attn = jnp.concatenate([part[...] for part in sums_attn], axis=1)
    none = jnp.zeros_like(attn)
    attn = jnp.concatenate([jnp.where(core == 0, attn, none), jnp.where(core == 0, none, attn)], axis=1)
    mid, out = sums_mid[...], sums_out[...]
    rows = [attn, mid[3:4], out[1:2], *total, mid[0:3], out[0:1]]
    n_up = d_b_up.shape[1] // width
    for c in range(2):
        for j in range(n_up):
            rows.append(jnp.where(core == c, d_b_up[:, j * width : (j + 1) * width], 0.0))
    rows = jnp.concatenate(rows, axis=0)
    sums[: rows.shape[0], :] = rows
    sums[rows.shape[0] :, :] = jnp.zeros((sums.shape[0] - rows.shape[0], width), F32)


def home_kernel(flags, keep, came, mixed, d_tokens):
    x = flags[1]
    for j, out in enumerate((mixed, d_tokens)):
        out[x] = keep[j]
        out[1 - x] = came[j]


def table_kernel(meta, *refs):
    scores, (out, grid_out, strip, wide_ds) = refs[:-4], refs[-4:]
    heads = wide_ds.shape[0]
    depth = grid_out.shape[1]
    rows = 144
    lane = lax.broadcasted_iota(jnp.int32, (1, 128), 1)
    column = lax.broadcasted_iota(jnp.int32, (8, 128), 0)
    wide_ds[:, :, ROW_LEN:, :] = jnp.zeros(wide_ds.shape[:2] + (wide_ds.shape[2] - ROW_LEN, 128), F32)

    def widen(i, carry):
        here = pl.ds(pl.multiple_of(i * rows, 16), rows)
        for h in range(heads):
            part = scores[h // 2][h % 2, here, :].astype(F32)
            for kb in range(4):
                wide_ds[h, kb, here, :] = part[:, 128 * kb : 128 * kb + 128]
            wide_ds[h, 4, here, 0:64] = part[:, 512:576]
        return carry

    lax.fori_loop(0, ROW_LEN // rows, widen, 0)
    grid_out[...] = jnp.zeros_like(grid_out)
    for g in range(IMGS + 1):
        b, e, s, w, low, stop, first, last, groups = segment_loops(meta, g)

        def clear(pair, carry):
            for n in range(3):
                strip[n, 2 * pair] = jnp.zeros(strip.shape[2:], F32)
                strip[n, 2 * pair + 1] = jnp.zeros(strip.shape[2:], F32)
            return carry

        lax.fori_loop(low, stop, clear, 0)

        for size in range(1, 4):

            def lines(turn, carry, b=b, e=e, s=s, w=w, size=size, first=first, last=last):
                found = []
                for extra in range(2):
                    y = first + 2 * turn + extra
                    stop_column = jnp.where(y < last, w, 0)
                    p0 = s + jnp.minimum(y, last - 1) * w
                    off = STRIP - p0
                    j0 = off // 128
                    r = off - j0 * 128
                    for n in range(size):
                        here = pl.ds(p0 + 8 * n, 8)
                        inside = column < stop_column - 8 * n
                        moved = []
                        for kb in range(5):
                            place = lane + kb * 128
                            keep = inside & (place >= b) & (place < e)
                            piece = [jnp.where(keep, wide_ds[h, kb, here, :], 0.0) for h in range(heads)]
                            moved.append(pltpu.roll(jnp.concatenate(piece, axis=0), r, 1))
                        zero = jnp.zeros_like(moved[0])
                        moved = [zero] + moved + [zero]
                        for kb in range(6):
                            found.append((n, j0 + kb, jnp.where(lane >= r, moved[kb + 1], moved[kb])))
                for n, block, part in found:
                    strip[n, block] += part
                return carry

            lax.fori_loop(0, jnp.where(groups == size, (last - first + 1) // 2, 0), lines, 0)

        def fold(pair, carry, w=w):
            sides = [jnp.concatenate([strip[n, 2 * pair + j] for n in range(3)], axis=0) for j in range(2)]
            whole = jnp.concatenate(sides, axis=1)
            grid_out[...] += lax.dot_general(
                whole.astype(BF), strip_onehot(pair, w, depth), (((1,), (1,)), ((), ())), preferred_element_type=F32
            )
            return carry

        lax.fori_loop(low, stop, fold, 0)

    total = jnp.zeros((heads, FLAT), F32)
    for c in range(GRID):
        rows_c = [(c // 8 * heads + h) * 8 + c % 8 for h in range(heads)]
        part = jnp.concatenate([grid_out[i : i + 1, :] for i in rows_c], axis=0)
        pieces = [part, jnp.zeros((heads, FLAT - depth - SIDE * c), F32)]
        if c:
            pieces.insert(0, jnp.zeros((heads, SIDE * c), F32))
        total = total + jnp.concatenate(pieces, axis=1)
    out[...] = total


def vmem():
    return pl.BlockSpec(memory_space=pltpu.VMEM)


def smem():
    return pl.BlockSpec(memory_space=pltpu.SMEM)


def params(mib):
    return pltpu.CompilerParams(vmem_limit_bytes=mib * 1024 * 1024)


def cost(us):
    return pl.CostEstimate(flops=int(us * 600_000_000), bytes_accessed=1_000, transcendentals=0)


def strip_scratch(heads):
    return [
        pltpu.VMEM((3, BLOCKS, heads * 8, 128), F32),
        pltpu.VMEM((heads, 5, ROW_LEN + 32, 128), F32),
    ]


def hidden_kernel(flags, own, came, w, b, act, slope, h2):
    width = w.shape[0]
    n = h2.shape[0] // 2

    @pl.when(pl.program_id(0) == 0)
    def _():
        h2[:n] = own[...].reshape(n, width)
        h2[n:] = came[...].reshape(n, width)

    x = jnp.dot(h2[...], w[...], preferred_element_type=F32) + b[...].astype(F32)
    size = jnp.abs(x)
    t = 1.0 / (1.0 + (0.3275911 * 0.7071067811865476) * size)
    bell = jnp.exp(-0.5 * x * x)
    tail = t * (0.254829592 + t * (-0.284496736 + t * (1.421413741 + t * (-1.453152027 + t * 1.061405429))))
    tail = 0.5 * tail * bell
    phi = jnp.where(x >= 0, 1.0 - tail, tail)
    act[...] = (x * phi).astype(BF)
    slope[...] = (phi + x * (bell * 0.3989422804014327)).astype(BF)


def fixed(array, part=None):
    if part is None:
        return pl.BlockSpec(array.shape, lambda i: (0,) * array.ndim)
    return pl.BlockSpec((1,) + array.shape[1:], lambda i: (part,) + (0,) * (array.ndim - 1))


def join_kernel(at, places, own, came, *outs):
    n = own.shape[0]
    rows = own.shape[1]
    for out in outs:
        for high in range(out.shape[1] // rows):
            cols = slice(at, at + out.shape[2])
            at += out.shape[2]
            for i in range(n):
                out[places[i], high * rows : (high + 1) * rows, :] = own[i, :, cols]
                out[places[n + i], high * rows : (high + 1) * rows, :] = came[i, :, cols]


def first_join_kernel(places, own, came, w, vecs):
    n = own.shape[0]
    cols = w.shape[2]
    total = jnp.zeros((own.shape[1], own.shape[2] - cols), F32)
    for i in range(n):
        w[places[i]] = own[i, :, :cols]
        w[places[n + i]] = came[i, :, :cols]
        total = total + own[i, :, cols:].astype(F32) + came[i, :, cols:].astype(F32)
    for v in range(vecs.shape[0]):
        vecs[v : v + 1, :] = jnp.concatenate([total[3 * v + j : 3 * v + j + 1] for j in range(3)], axis=1)


def cat_kernel(flags, *refs):
    out, at = refs[-1], 0
    for part in refs[:-1]:
        out[at : at + part.shape[0]] = part[...]
        at += part.shape[0]


def add_kernel(flags, a, b, *outs):
    at = 0
    for out in outs:
        n = out.shape[0]
        out[...] = (a[at : at + n].astype(F32) + b[at : at + n].astype(F32)).astype(BF)
        at += n


def sum_kernel(flags, *refs):
    total = refs[0][...].astype(F32)
    for part in refs[1:-1]:
        total = total + part[...].astype(F32)
    refs[-1][...] = total.astype(refs[-1].dtype)


def grad_kernel(places, *refs):
    keep, give, full = refs[-3:]
    at = 0
    for a, b in zip(refs[:-3:2], refs[1:-3:2]):
        cols = slice(at, at + b.shape[1])
        at += b.shape[1]
        if a.shape[0] == full.shape[0]:
            full[:, cols] = (a[...].astype(F32) + b[...].astype(F32)).astype(BF)
            continue
        step = 256
        for t in range(full.shape[0] // step):
            here = slice(t * step, t * step + step)
            made = lax.dot_general(a[:, here], b[...], (((0,), (0,)), ((), ())), preferred_element_type=F32)
            full[here, cols] = made.astype(BF)
    n, rows, _ = keep.shape
    width = full.shape[1]
    block = full.shape[0] // (2 * n)
    for high in range(block // rows):
        there = slice(high * width, (high + 1) * width)
        for i in range(n):
            for out, j in ((keep, places[i]), (give, places[n + i])):
                out[i, :, there] = full[pl.ds(pl.multiple_of(j * block + high * rows, 16), rows), :]


def attn_end_kernel(flags, a, b, own, give):
    core = flags[0]
    rows = own.shape[0]
    total = a[0].astype(F32) + b[0].astype(F32)
    for t in range(3):
        for j in range(3):
            src, dst = slice((3 * t + j) * 128, (3 * t + j + 1) * 128), slice((3 * j + t) * 128, (3 * j + t + 1) * 128)
            low, high = total[:rows, src], total[rows:, src]
            own[:, dst] = jnp.where(core == 0, low, high)
            give[:, dst] = jnp.where(core == 0, high, low)


def attn_home_kernel(flags, own, came, out):
    core = flags[0]
    n = own.shape[1] // 3
    for j in range(3):
        mine, other = own[:, n * j : n * j + n], came[:, n * j : n * j + n]
        out[:, 2 * n * j : 2 * n * j + n] = jnp.where(core == 0, mine, other)
        out[:, 2 * n * j + n : 2 * n * (j + 1)] = jnp.where(core == 0, other, mine)


def proj_grad_kernel(flags, joined, d_branch, keep, give):
    core = flags[0]
    n = keep.shape[1]
    width = joined.shape[-1]
    made = lax.dot_general(
        joined[...].reshape(-1, width), d_branch[...], (((0,), (0,)), ((), ())), preferred_element_type=F32
    )
    low, high = made[:, :n], made[:, n:]
    keep[...] = jnp.where(core == 0, low, high).astype(BF)
    give[...] = jnp.where(core == 0, high, low).astype(BF)


def after(array, *others):
    others = tuple(other for other in others if other is not None)
    return lax.optimization_barrier((array,) + others)[0] if others else array


class Net:
    def __init__(self, dp, seq):
        self.dp, self.seq = dp, seq
        self.fast = dp == 8
        self.last, self.waits = None, ()
        at_seq = lax.axis_index("seq")
        self.core = at_seq % 2
        self.x = at_seq // 2
        at_dp = lax.axis_index("dp")

        def table(fn):
            pairs = []
            for d in range(dp):
                for s in range(seq):
                    d2, s2 = fn(d, s)
                    pairs.append((d * seq + s, d2 * seq + s2))
            return pairs

        self.to_core = table(lambda d, s: (d, s ^ 1))
        self.to_x = table(lambda d, s: (d, s ^ 2))
        self.flags = jnp.stack([self.core, self.x]).astype(jnp.int32)
        if self.fast:
            self.phases = (
                table(lambda d, s: (d ^ 4, s)),
                table(lambda d, s: (d ^ 2, s)),
                table(lambda d, s: (d, s ^ 2) if s % 2 == 0 else (d ^ 1, s)),
                table(lambda d, s: (d ^ 1, s) if s % 2 == 0 else (d, s ^ 2)),
            )
            rel = jnp.arange(16, dtype=jnp.int32)
            d1, d2, d3, d4 = rel % 2, (rel // 2) % 2, (rel // 4) % 2, rel // 8
            by_x = jnp.where(self.core == 0, d3, d4)
            by_y = jnp.where(self.core == 0, d4, d3)
            self.places = ((at_dp * 2 + self.x) ^ (d1 * 8 + d2 * 4 + by_y * 2 + by_x)).astype(jnp.int32)

    def pin(self, array):
        waits, self.waits = self.waits, ()
        return array if self.last is None else after(array, self.last, *waits)

    def call(self, kernel, us, outs, args, scratch=(), mib=8, aliases=()):
        got = pl.pallas_call(
            kernel,
            out_shape=tuple(jax.ShapeDtypeStruct(shape, kind) for shape, kind in outs),
            in_specs=[smem()] + [vmem()] * (len(args) - 1),
            out_specs=(vmem(),) * len(outs),
            scratch_shapes=list(scratch),
            compiler_params=params(mib),
            cost_estimate=cost(us),
            name=getattr(kernel, "func", kernel).__name__,
            input_output_aliases=dict(aliases),
        )(self.pin(args[0]), *args[1:])
        self.last = got[0]
        return got

    def send(self, array, pairs):
        return lax.ppermute(array, BOTH, pairs)

    def by_core(self, own, other, axis):
        first = self.core == 0
        return jnp.stack([jnp.where(first, own, other), jnp.where(first, other, own)], axis=axis)

    def pick(self, array, index, axis):
        return lax.dynamic_index_in_dim(array, index, axis, keepdims=False)

    def bias_of(self, meta, flat, segment):
        heads = flat.shape[0]
        return self.call(
            bias_kernel,
            12,
            (((2, ROW_LEN, ROW_LEN), BF),) * (heads // 2),
            (meta, flat, segment[:, None], segment[None, :]),
            scratch=[pltpu.VMEM((heads * GRID, DEPTH), F32)] + strip_scratch(heads),
            mib=16,
        )

    def table_of(self, meta, scores):
        heads = 2 * len(scores)
        return self.call(
            table_kernel,
            12,
            (((heads, FLAT), F32),),
            (meta, *scores),
            scratch=[pltpu.VMEM((heads * GRID, DEPTH), F32)] + strip_scratch(heads),
            mib=16,
        )[0]

    def hidden(self, own, came, w, b):
        rows = 2 * own.size // w.shape[0]
        depth, cols = w.shape
        tile = 256
        out = jax.ShapeDtypeStruct((rows, cols), BF)
        got = pl.pallas_call(
            hidden_kernel,
            grid=(cols // tile,),
            out_shape=(out, out, jax.ShapeDtypeStruct((rows, depth), BF)),
            in_specs=[
                smem(),
                fixed(own),
                fixed(came),
                pl.BlockSpec((depth, tile), lambda i: (0, i)),
                pl.BlockSpec((1, tile), lambda i: (0, i)),
            ],
            out_specs=(pl.BlockSpec((rows, tile), lambda i: (0, i)),) * 2 + (pl.BlockSpec((rows, depth), lambda i: (0, 0)),),
            compiler_params=params(8),
            cost_estimate=cost(6),
            name="hidden",
        )(self.pin(self.flags), own, came, w, b)
        self.last = got[0]
        return got

    def hidden_back(self, d_after, w_down, slope, w_up):
        rows, cols = slope.shape
        width = w_up.shape[0]
        tile = cols // 2
        got = pl.pallas_call(
            hidden_back_kernel,
            grid=(cols // tile,),
            out_shape=(
                jax.ShapeDtypeStruct((rows, cols), BF),
                jax.ShapeDtypeStruct((1, cols), F32),
                jax.ShapeDtypeStruct((rows // 2, width), F32),
                jax.ShapeDtypeStruct((rows // 2, width), BF),
            ),
            in_specs=[
                smem(),
                fixed(d_after),
                pl.BlockSpec((tile, width), lambda i: (i, 0)),
                pl.BlockSpec((rows, tile), lambda i: (0, i)),
                pl.BlockSpec((width, tile), lambda i: (0, i)),
            ],
            out_specs=(
                pl.BlockSpec((rows, tile), lambda i: (0, i)),
                pl.BlockSpec((1, tile), lambda i: (0, i)),
                pl.BlockSpec((rows // 2, width), lambda i: (0, 0)),
                pl.BlockSpec((rows // 2, width), lambda i: (0, 0)),
            ),
            scratch_shapes=[pltpu.VMEM((rows, width), F32)],
            compiler_params=params(14),
            cost_estimate=cost(5),
            name="hidden_back",
        )(self.pin(self.flags), d_after, w_down, slope, w_up)
        self.last = got[0]
        return got

    def gather(self, block):
        return Gather(self, block) if self.fast else WholeGather(self, block)

    def library_gather(self, block):
        if not self.fast:
            return WholeGather(self, block).got
        groups = [[(d * 2 + x) * 2 + c for d in range(self.dp) for x in range(2)] for c in range(2)]
        return lax.all_gather(block, BOTH, axis=0, axis_index_groups=groups)

    def reduce(self, shape, *pairs):
        if self.fast:
            return Reduce(self, shape, pairs)
        made = []
        for a, b in pairs:
            made.append((wide(a) + wide(b) if a.shape == b.shape else dot_t(a, b)).astype(BF))
        return WholeReduce(self, jnp.concatenate(made, axis=1))


class Gather:
    def __init__(self, net, block):
        self.net, self.got, self.step = net, block[None], 0
        self.go()

    def go(self):
        self.came = self.net.send(self.got, self.net.phases[self.step])

    def next(self):
        out = ((2 * self.got.shape[0],) + self.got.shape[1:], BF)
        self.got = self.net.call(cat_kernel, 0.6, (out,), (self.net.flags, self.got, self.came))[0]
        self.step += 1
        self.go()

    def join(self, *shapes, at=0):
        outs = [((2 * self.got.shape[0],) + shape, BF) for shape in shapes]
        kernel = functools.partial(join_kernel, at)
        return self.net.call(kernel, 0.7, outs, (self.net.places, self.got, self.came))

    def first_join(self, cols):
        _, rows, width = self.got.shape
        outs = (((2 * self.got.shape[0], rows, cols), BF), ((rows // 3, 3 * (width - cols)), F32))
        return self.net.call(first_join_kernel, 0.7, outs, (self.net.places, self.got, self.came))


class WholeGather:
    def __init__(self, net, block):
        block = lax.all_gather(block, "dp", axis=0)
        other = net.send(block, net.to_x)
        first = net.x == 0
        block = jnp.stack([jnp.where(first, block, other), jnp.where(first, other, block)], axis=1)
        self.got = block.reshape((2 * net.dp,) + block.shape[2:])

    def next(self):
        pass

    def join(self, *shapes, at=0):
        return (self.got[:, :, at : at + shapes[0][1]],)


class Reduce:
    def __init__(self, net, shape, pairs):
        self.net, self.step = net, 3
        arrays = [array for pair in pairs for array in pair]
        depth = pairs[0][0].shape[0] if pairs[0][0].shape == pairs[0][1].shape else pairs[0][0].shape[1]
        width = sum(b.shape[1] for _, b in pairs)
        out = ((8,) + shape, BF)
        self.keep, self.give = net.call(
            grad_kernel, 3, (out, out), (net.places, *arrays), scratch=[pltpu.VMEM((depth, width), BF)]
        )
        self.go()

    def go(self):
        self.came = self.net.send(self.give, self.net.phases[self.step])

    def next(self):
        out = ((self.keep.shape[0] // 2,) + self.keep.shape[1:], BF)
        self.keep, self.give = self.net.call(add_kernel, 1, (out, out), (self.net.flags, self.keep, self.came))
        self.step -= 1
        self.go()

    def end(self):
        out = ((1,) + self.keep.shape[1:], F32)
        return self.net.call(sum_kernel, 0.6, (out,), (self.net.flags, self.keep, self.came))[0][0]


class WholeReduce:
    def __init__(self, net, full):
        blocks = full.reshape((net.dp, 2, -1) + full.shape[1:])
        came = net.send(net.pick(blocks, 1 - net.x, 1), net.to_x)
        summed = net.pick(blocks, net.x, 1).astype(F32) + came.astype(F32)
        self.sum = lax.psum_scatter(summed, "dp", scatter_dimension=0, tiled=False)

    def next(self):
        pass

    def end(self):
        return self.sum


class Total:
    def __init__(self, net, array):
        self.net, self.sum, self.step = net, array, 0
        if net.fast:
            self.came = net.send(array, net.phases[0])
        else:
            self.sum = lax.psum(array + net.send(array, net.to_x), "dp")

    def next(self):
        if self.net.fast:
            out = (self.sum.shape, F32)
            self.sum = self.net.call(sum_kernel, 0.6, (out,), (self.net.flags, self.sum, self.came))[0]
            self.step += 1
            if self.step < 4:
                self.came = self.net.send(self.sum, self.net.phases[self.step])


def wide(array):
    return array.astype(F32)


def dot(a, b):
    return jnp.dot(a, b, preferred_element_type=F32)


def dot_t(a, b):
    return lax.dot_general(a, b, (((0,), (0,)), ((), ())), preferred_element_type=F32)


def local(
    dp,
    seq,
    tokens,
    image_lengths,
    grid_widths,
    qkv_weight,
    q_bias,
    v_bias,
    proj_weight,
    proj_bias,
    fc1_weight,
    fc1_bias,
    fc2_weight,
    fc2_bias,
    norm1_gain,
    norm1_bias,
    norm2_gain,
    norm2_bias,
    scale1,
    scale2,
    bias_table,
    out_grad,
):
    net = Net(dp, seq)
    call, flags, core, at_x = net.call, net.flags, net.core, net.x
    row_count, shard, width = tokens.shape
    heads = bias_table.shape[1]
    own_heads = heads // 2
    own_feats = width // 2
    n_dev = dp * seq
    chips = n_dev // 2
    rows_w = width // n_dev
    ff = fc2_weight.shape[0] * n_dev
    rows_f = ff // n_dev
    at = lax.axis_index("dp") * seq + lax.axis_index("seq")
    at_chip = lax.axis_index("dp") * 2 + at_x

    lanes = jnp.arange(width, dtype=jnp.int32)
    spots = (lanes[None] // rows_w == at) & (lanes[None] % rows_w == jnp.arange(rows_w, dtype=jnp.int32)[:, None])
    vecs = [q_bias, v_bias, proj_bias, fc2_bias, norm1_gain, norm1_bias, norm2_gain, norm2_bias, scale1, scale2]
    n_vec = len(vecs)
    placed = dot(jnp.stack(vecs), spots.astype(BF)).astype(BF)
    n_up = ff // 2 // width
    lanes_up = jnp.arange(ff // 2, dtype=jnp.int32)
    spots_up = (lanes_up[None] // rows_f == at_chip) & (lanes_up[None] % rows_f == jnp.arange(rows_f, dtype=jnp.int32)[:, None])
    placed_up = dot(fc1_bias[None], spots_up.astype(BF)).astype(BF).reshape(n_up, width)
    mine = (jnp.arange(2) == core)[:, None, None]
    placed_up = jnp.where(mine, placed_up[None], jnp.zeros((), BF)).reshape(2 * n_up, width)
    placed = jnp.concatenate([placed, placed_up, jnp.zeros((16 - n_vec - 2 * n_up, width), BF)])

    low = ((rows_w, 3 * own_feats), BF)
    keep, give = call(split_kernel, 0.5, (low, low), (flags, qkv_weight))
    attn_block = net.by_core(keep, net.send(give, net.to_core), 0).reshape(2 * rows_w, 3 * own_feats)
    placed = placed + net.send(placed, net.to_core)
    if net.fast:
        attn_block = jnp.concatenate([attn_block, placed.reshape(48, 256)], axis=1)
    attn_chain = net.gather(attn_block)

    first_came = getattr(attn_chain, "came", None)
    their_tokens, their_grad = after(tokens, attn_block), after(out_grad, attn_block)
    theirs = jnp.stack([net.pick(their_tokens, 1 - at_x, 0), net.pick(their_grad, 1 - at_x, 0)])
    token_came = net.send(theirs, net.to_x)
    proj_view = after(proj_weight, first_came).reshape(rows_w, 2, own_feats)
    fc1_view = after(fc1_weight, first_came).reshape(rows_w, chips, 2, rows_f)
    views = []
    for index in (core, 1 - core):
        up = net.pick(fc1_view, index, 2).reshape(rows_w, ff // 2)
        views.append(jnp.concatenate([up, net.pick(proj_view, index, 1)], axis=1))
    up_came = net.send(views[1], net.to_core)

    lengths = net.pick(image_lengths, at_x, 0)
    widths = net.pick(grid_widths, at_x, 0)
    meta, segment = layout(after(lengths, attn_block), after(widths, attn_block))
    flat = jnp.transpose(after(bias_table, attn_block).reshape(SIDE, SIDE, heads), (2, 1, 0)).reshape(heads, SIDE * SIDE)
    flat = jnp.pad(wide(lax.dynamic_slice_in_dim(flat, core * own_heads, own_heads)), ((0, 0), (0, FLAT - SIDE * SIDE)))

    chunk = (2, shard, width)
    attn_chain.next()
    (up_block,) = call(stack_kernel, 0.5, (((2 * rows_w, ff // 2 + own_feats), BF),), (flags, views[0], up_came))
    up_chain = net.gather(up_block)
    attn_chain.next()
    (both,) = call(start_kernel, 0.5, (((2,) + chunk, BF),), (flags, tokens, out_grad, token_came))
    both_came = net.send(both, net.to_core)
    attn_chain.next()
    up_chain.next()
    down_block = fc2_weight if not net.fast else jnp.concatenate([fc2_weight[: 2 * rows_w], fc2_weight[2 * rows_w :]], axis=1)
    down_chain = net.gather(net.pin(down_block))
    biases = net.bias_of(meta, flat, segment)
    down_chain.next()
    up_chain.next()
    if net.fast:
        w_qkv, vectors = attn_chain.first_join(3 * own_feats)
    else:
        (w_qkv,) = attn_chain.join((2 * rows_w, 3 * own_feats))
        vectors = Total(net, wide(placed)).sum

    row = (ROW_LEN, 128)
    part_heads = (2, shard, 128)
    square = (2, ROW_LEN, ROW_LEN)
    pairs, keeps, cames = [], [], []
    for t, bias in enumerate(biases):
        outs = ((square, BF), (part_heads, BF), (part_heads, BF))
        outs = (((ROW_LEN, 384), BF),) + ((((1, ff // 2), F32),) if t == 0 else ()) + outs
        if t == 0:
            outs = outs + (((ROW_LEN, width), BF),)
            args = (flags, both, both_came, w_qkv, vectors, bias)
        else:
            args = (flags, h1, w_qkv, vectors, bias)
        alias = {len(args) - 1: 2 if t == 0 else 1}
        got = call(functools.partial(attn_fwd_kernel, t == 0, t), 5, outs, args, scratch=[pltpu.VMEM(row, BF)], aliases=alias)
        if t == 0:
            b_up, h1 = got[1], got[5]
            got = got[:1] + got[2:]
        pairs.append(got[:2])
        keeps.append(got[2])
        cames.append(net.send(got[3], net.to_core))
        if t == 0:
            down_chain.next()
            up_chain.next()
    down_chain.next()
    (pj_own,) = up_chain.join((2 * rows_w, own_feats), at=ff // 2)
    pj_came = net.send(pj_own, net.to_core)
    (fc1_all,) = up_chain.join((2 * rows_w, ff // 2))
    joined, branch, middle, h2, d_after = call(
        proj_kernel,
        3,
        ((chunk, BF), (chunk, BF), (chunk, F32), (chunk, BF), ((ROW_LEN, width), BF)),
        (flags, *keeps, *cames, pj_own, pj_came, both, both_came, vectors),
    )
    h2_came = net.send(h2, net.to_core)
    w_up = fc1_all.reshape(width, ff // 2)
    act, slope, h2_all = net.hidden(h2, h2_came, w_up, b_up)
    down_sum = net.reduce((rows_f, width), (act, d_after))
    w_down = down_chain.join((rows_f, width))[0].reshape(ff // 2, width)
    d_before, d_b_up, keep, give = net.hidden_back(d_after, w_down, slope, w_up)
    mid_came = net.send(give, net.to_core)
    own = 2 * shard
    after_keep, after_give = call(after_kernel, 2, (((own, width), F32), ((own, width), BF)), (flags, act, w_down))
    after_came = net.send(after_give, net.to_core)
    half = (2, shard, own_feats)
    d_middle, d_branch, keep, give, sums_mid = call(
        middle_back_kernel,
        3,
        ((chunk, F32), ((own, width), BF), (half, BF), (half, BF), ((4, width), F32)),
        (flags, keep, mid_came, middle, both, branch, pj_own, pj_came, vectors),
    )
    heads_came = net.send(give, net.to_core)
    out = ((width, own_feats), BF)
    proj_keep, proj_give = call(proj_grad_kernel, 2, (out, out), (flags, joined, d_branch))
    proj_came = net.send(proj_give, net.to_core)

    d_joints, scores, sums_attn = [], [], []
    for t, (qkv, prob) in enumerate(pairs):
        d_joint, ds, sums = call(
            functools.partial(attn_bwd_kernel, t),
            5,
            (((ROW_LEN, 384), BF), (square, BF), ((2, 128), F32)),
            (flags, qkv, keep, heads_came, prob),
            scratch=[pltpu.VMEM(row, BF), pltpu.VMEM((128, ROW_LEN), F32), pltpu.VMEM((128, ROW_LEN), F32)],
        )
        d_joints.append(d_joint)
        scores.append(ds)
        sums_attn.append(sums)
        if t == 0:
            up_sum = net.reduce((2 * rows_w, ff // 2 + own_feats), (h2_all, d_before), (proj_keep, proj_came))
            down_sum.next()
        if t == 1:
            mixed, sums_out = call(
                mixed_kernel,
                2,
                ((chunk, BF), ((2, width), F32)),
                (flags, after_keep, after_came, middle, both, d_after, vectors),
            )
    attn_sum = net.reduce((2 * rows_w, 3 * own_feats), *[(h1, d_joint) for d_joint in d_joints])
    keep, give = call(h1_back_kernel, 3, ((chunk, F32), (chunk, BF)), (flags, *d_joints, w_qkv))
    h1_came = net.send(give, net.to_core)
    down_sum.next()
    up_sum.next()
    table = net.table_of(meta, scores)
    attn_sum.next()
    down_sum.next()
    up_sum.next()

    keep, give, smalls = call(
        end_kernel,
        2,
        ((chunk, BF), (chunk, BF), ((16, width), F32)),
        (flags, keep, h1_came, both, d_middle, mixed, vectors, *sums_attn, sums_mid, sums_out, d_b_up),
    )
    smalls_came = net.send(smalls, net.to_core)
    out_came = net.send(give, net.to_x)
    (smalls,) = call(sum_kernel, 0.6, (((16, width), F32),), (flags, smalls, smalls_came))
    total = Total(net, jnp.concatenate([smalls.reshape(-1, 128), table.reshape(-1, 128)]))
    total.next()
    total.next()
    up_sum.next()
    attn_sum.next()
    g_down = down_sum.end()
    mixed, tokens_grad = call(home_kernel, 1, ((chunk, BF), (chunk, BF)), (flags, keep, out_came))
    total.next()
    attn_sum.next()
    g_up = up_sum.end()
    total.next()

    def home(block, groups, cols):
        view = block.reshape(2, rows_w, groups, cols)
        came = net.send(net.pick(view, 1 - core, 0), net.to_core)
        return net.by_core(net.pick(view, core, 0), came, 2).reshape(rows_w, groups * 2 * cols)

    g_proj = home(g_up[:, ff // 2 :], 1, own_feats)
    g_up = home(g_up[:, : ff // 2], chips, rows_f)
    packed = total.sum
    sums = packed[: smalls.size // 128].reshape(smalls.shape)
    table = packed[smalls.size // 128 :].reshape(own_heads, FLAT)
    table = net.by_core(table, net.send(table, net.to_core), 0).reshape(heads, FLAT)[:, : SIDE * SIDE]
    table_grad = jnp.transpose(table.reshape(heads, SIDE, SIDE), (2, 1, 0)).reshape(SIDE * SIDE, heads)
    g_small = lax.dynamic_slice_in_dim(sums[:n_vec], at * rows_w, rows_w, 1)
    g_up_small = net.pick(sums[n_vec : n_vec + 2 * n_up].reshape(2, ff // 2), core, 0)
    g_up_small = lax.dynamic_slice_in_dim(g_up_small, at_chip * rows_f, rows_f)
    smalls = [g_small[j] for j in range(n_vec)] + [g_up_small]

    if net.fast:
        net.waits = (g_proj, g_up, table_grad, g_small, g_up_small)
        rows = ((rows_w, 3 * own_feats), F32)
        own_rows, give = call(attn_end_kernel, 0.5, (rows, rows), (flags, attn_sum.keep, attn_sum.came))
        came = net.send(give, net.to_core)
        (g_qkv,) = call(attn_home_kernel, 0.5, (((rows_w, 3 * width), F32),), (flags, own_rows, came))
    else:
        g_attn = attn_sum.end().reshape(2 * rows_w, 3, 3, 128).transpose(0, 2, 1, 3)
        g_qkv = home(g_attn.reshape(2 * rows_w, 3 * own_feats), 3, own_feats)
    g_query, g_value, g_bproj, g_bdown, g_gain1, g_shift1, g_gain2, g_shift2, g_layer1, g_layer2, g_bup = smalls
    return (
        mixed,
        tokens_grad,
        g_qkv,
        g_query,
        g_value,
        g_proj,
        g_bproj,
        g_up,
        g_bup,
        g_down,
        g_bdown,
        g_gain1,
        g_shift1,
        g_gain2,
        g_shift2,
        g_layer1,
        g_layer2,
        table_grad,
    )


def solution(mesh):
    both = P(BOTH)
    both2 = P(BOTH, None)
    act = P("dp", "seq", None)
    in_specs = (act, P("dp", None), P("dp", None), both2, both, both, both2, both, both2, both, both2)
    in_specs += (both,) * 7 + (P(), act)
    out_specs = (act, act, both2, both, both, both2, both, both2, both, both2) + (both,) * 7 + (P(),)
    body = functools.partial(local, mesh.shape["dp"], mesh.shape["seq"])
    return jax.shard_map(body, mesh=mesh, in_specs=in_specs, out_specs=out_specs, check_vma=False)
```

```python
import functools

import jax
import jax.numpy as jnp
from jax import lax
from jax.experimental import pallas as pl
from jax.experimental.pallas import tpu as pltpu
from jax.sharding import PartitionSpec as P

GRID = 24
SIDE = 2 * GRID - 1
ROW_LEN = 576
IMGS = 4
EPS = 1e-06
STRIP = 640
BLOCKS = 12
DEPTH = 1152
FLAT = 2304
BF = jnp.bfloat16
F32 = jnp.float32
BOTH = ("dp", "seq")
VECS = ("q", "v", "b_proj", "b_down", "gain1", "shift1", "gain2", "shift2", "scale1", "scale2")


def layout(lengths, widths):
    ends = jnp.cumsum(lengths).astype(jnp.int32)
    starts = ends - lengths
    total = ends[-1]
    full = jnp.full((1,), ROW_LEN, jnp.int32)
    meta = jnp.stack(
        [
            jnp.concatenate([starts, total[None]]),
            jnp.concatenate([ends, full]),
            jnp.concatenate([starts, jnp.zeros((1,), jnp.int32)]),
            jnp.concatenate([widths, jnp.full((1,), GRID, jnp.int32)]),
        ]
    ).astype(jnp.int32)
    places = jnp.arange(ROW_LEN, dtype=jnp.int32)
    segment = jnp.sum((places[:, None] >= ends[None, :]).astype(jnp.int32), axis=1)
    return meta, segment


def strip_range(b, e):
    length = e - b
    return (STRIP - length) // 256, jnp.minimum((STRIP + length + GRID) // 256, BLOCKS // 2 - 1)


def strip_onehot(pair, w, depth):
    lane = lax.broadcasted_iota(jnp.int32, (1, 256), 1) + (pair * 256 - STRIP + 80 * w)
    line = jnp.floor((lane.astype(F32) + 0.5) / jnp.full((1, 256), w, jnp.int32).astype(F32)).astype(jnp.int32)
    column = lane - line * w
    level = jnp.clip(80 - line, 1 - GRID, GRID - 1) + (GRID - 1)
    code = (GRID - 1 - column) * SIDE + level
    return (lax.broadcasted_iota(jnp.int32, (depth, 256), 0) == code).astype(F32).astype(BF)


def segment_loops(meta, g):
    b, e, s, w = meta[0, g], meta[1, g], meta[2, g], meta[3, g]
    low, high = strip_range(b, e)
    stop = jnp.where(e > b, high + 1, low)
    first, last = (b - s) // w, jnp.where(e > b, (e - 1 - s) // w + 1, 0)
    return b, e, s, w, low, stop, first, last, (w + 7) // 8


def bias_kernel(meta, flat, seg_col, seg_row, *refs):
    outs, (tab, strip, bias) = refs[:-3], refs[-3:]
    heads = bias.shape[0]
    depth = tab.shape[1]
    lane = lax.broadcasted_iota(jnp.int32, (1, 128), 1)
    for c in range(GRID):
        moved = flat[:, SIDE * c : SIDE * c + depth]
        for h in range(heads):
            row = (c // 8 * heads + h) * 8 + c % 8
            tab[row : row + 1, :] = moved[h : h + 1]
    low_tab = tab[...].astype(BF)
    for g in range(IMGS + 1):
        b, e, s, w, low, stop, first, last, groups = segment_loops(meta, g)

        def build(pair, carry, w=w):
            made = jnp.dot(low_tab, strip_onehot(pair, w, depth), preferred_element_type=F32)
            for n in range(3):
                rows_n = slice(n * heads * 8, (n + 1) * heads * 8)
                strip[n, 2 * pair] = made[rows_n, :128]
                strip[n, 2 * pair + 1] = made[rows_n, 128:]
            return carry

        lax.fori_loop(low, stop, build, 0)

        for size in range(1, 4):

            def lines(turn, carry, b=b, s=s, w=w, g=g, size=size, first=first, last=last):
                found = []
                for y in (first + 2 * turn, jnp.minimum(first + 2 * turn + 1, last - 1)):
                    p0 = s + y * w
                    off = STRIP - p0
                    j0 = off // 128
                    r = off - j0 * 128
                    for n in range(size):
                        parts = [strip[n, j0 + kb] for kb in range(6)]
                        for kb in range(5):
                            moved = pltpu.roll(jnp.where(lane >= r, parts[kb], parts[kb + 1]), (128 - r) % 128, 1)
                            found.append((kb, pl.ds(p0 + 8 * n, 8), moved))
                for kb, here, moved in found:
                    for h in range(heads):
                        piece = moved[h * 8 : (h + 1) * 8]
                        if g == IMGS:
                            piece = jnp.where(lane + kb * 128 >= b, piece, bias[h, kb, here, :])
                        bias[h, kb, here, :] = piece
                return carry

            lax.fori_loop(0, jnp.where(groups == size, (last - first + 1) // 2, 0), lines, 0)

    rows = 144

    def mask(i, carry):
        here = pl.ds(pl.multiple_of(i * rows, 16), rows)
        allowed = seg_col[here, :] == seg_row[...]
        for h in range(heads):
            offs = jnp.concatenate([bias[h, kb, here, :] for kb in range(5)], axis=1)[:, :ROW_LEN]
            outs[h // 2][h % 2, here, :] = jnp.where(allowed, offs, -1e30).astype(BF)
        return carry

    lax.fori_loop(0, ROW_LEN // rows, mask, 0)


def norm_parts(x):
    center = x - jnp.mean(x, axis=-1, keepdims=True)
    inverse = lax.rsqrt(jnp.mean(center * center, axis=-1, keepdims=True) + EPS)
    return center * inverse, inverse


def norm_back(normed, inverse, grad, gain):
    pulled = grad * gain
    mean = jnp.mean(pulled, axis=-1, keepdims=True)
    along = jnp.mean(pulled * normed, axis=-1, keepdims=True)
    return (pulled - mean - normed * along) * inverse


def vec(vecs, name):
    return vecs[VECS.index(name) : VECS.index(name) + 1, :].astype(F32)


def own_half(core, row):
    n = row.shape[1] // 2
    return jnp.where(core == 0, row[:, :n], row[:, n:])


def split_kernel(flags, w, keep, give):
    core = flags[0]
    n = w.shape[1] // 6
    for j in range(3):
        low, high = w[:, 2 * n * j : 2 * n * j + n], w[:, 2 * n * j + n : 2 * n * j + 2 * n]
        keep[:, n * j : n * j + n] = jnp.where(core == 0, low, high)
        give[:, n * j : n * j + n] = jnp.where(core == 0, high, low)


def stack_kernel(flags, own, came, out):
    mine, other = own[...].astype(F32), came[...].astype(F32)
    low, high = jnp.concatenate([mine, other], axis=0), jnp.concatenate([other, mine], axis=0)
    out[...] = jnp.where(flags[0] == 0, low, high).astype(BF)


def start_kernel(flags, tokens, out_grad, came, both):
    x = flags[1]
    both[0, x] = tokens[x]
    both[1, x] = out_grad[x]
    both[0, 1 - x] = came[0]
    both[1, 1 - x] = came[1]


def attn_fwd_kernel(first, t, flags, *refs):
    core = flags[0]
    if first:
        own, came, w, vecs, bias, qkv, b_up, p_out, keep, give, h1, joined = refs
        shard = own.shape[2]
        ups = vecs[len(VECS) : len(VECS) + 4, :]
        pairs = [jnp.concatenate([ups[2 * c : 2 * c + 1], ups[2 * c + 1 : 2 * c + 2]], axis=1) for c in range(2)]
        b_up[...] = jnp.where(core == 0, pairs[0], pairs[1])
        for a in range(2):
            for side, part in ((core, own), (1 - core, came)):
                normed, _ = norm_parts(part[0, a].astype(F32))
                normed = normed * vec(vecs, "gain1") + vec(vecs, "shift1")
                h1[pl.ds(pl.multiple_of((2 * a + side) * shard, 16), shard), :] = normed.astype(BF)
    else:
        h1, w, vecs, bias, qkv, p_out, keep, give, joined = refs
        shard = keep.shape[1]
    feats = w.shape[2] // 3
    cols = slice(128 * t, 128 * t + 128)

    def weight(j):
        return w[:, :, feats * j + 128 * t : feats * j + 128 * t + 128].reshape(h1.shape[1], 128)

    q_row, v_row = own_half(core, vec(vecs, "q"))[:, cols], own_half(core, vec(vecs, "v"))[:, cols]
    q, k, v = slice(0, 128), slice(128, 256), slice(256, 384)
    qkv[:, q] = ((jnp.dot(h1[...], weight(0), preferred_element_type=F32) + q_row) * 64**-0.5).astype(BF)
    qkv[:, k] = jnp.dot(h1[...], weight(1), preferred_element_type=F32).astype(BF)
    qkv[:, v] = (jnp.dot(h1[...], weight(2), preferred_element_type=F32) + v_row).astype(BF)
    rows = 144
    half = lax.broadcasted_iota(jnp.int32, (1, 128), 1) < 64

    def chunk(i, carry):
        here = pl.ds(pl.multiple_of(i * rows, 16), rows)
        q_tile = qkv[here, q]
        outs = []
        for sub in range(2):
            q_own = jnp.where(half if sub == 0 else ~half, q_tile, jnp.zeros_like(q_tile))
            score = lax.dot_general(q_own, qkv[:, k], (((1,), (1,)), ((), ())), preferred_element_type=F32)
            score = score + bias[sub, here, :].astype(F32)
            raised = jnp.exp(score - jnp.max(score, axis=1, keepdims=True))
            prob = (raised * (1.0 / jnp.sum(raised, axis=1, keepdims=True))).astype(BF)
            p_out[sub, here, :] = prob
            outs.append(jnp.dot(prob, qkv[:, v], preferred_element_type=F32))
        joined[here, :] = jnp.where(half, outs[0], outs[1]).astype(BF)
        return carry

    lax.fori_loop(0, ROW_LEN // rows, chunk, 0)
    for a in range(2):
        keep[a] = joined[pl.ds(pl.multiple_of((2 * a + core) * shard, 16), shard), :]
        give[a] = joined[pl.ds(pl.multiple_of((2 * a + 1 - core) * shard, 16), shard), :]


def by_core_in(core, own, came):
    return jnp.concatenate([jnp.where(core == 0, own, came), jnp.where(core == 0, came, own)], axis=-1)


def proj_kernel(flags, *refs):
    keeps, cames = refs[:3], refs[3:6]
    w_own, w_came, own, grads_came, vecs, joined, branch, middle, h2, d_after = refs[6:]
    core = flags[0]
    width = own.shape[-1]
    shard = own.shape[2]
    feats = width // 2
    for a in range(2):
        keep = jnp.concatenate([part[a] for part in keeps], axis=-1)
        came = jnp.concatenate([part[a] for part in cames], axis=-1)
        joined[a] = by_core_in(core, keep, came)
    weight = by_core_in(core, w_own[...].reshape(width, feats), w_came[...].reshape(width, feats))
    for a in range(2):
        out = jnp.dot(joined[a], weight, preferred_element_type=F32) + vec(vecs, "b_proj")
        branch[a] = out.astype(BF)
        mid = own[0, a].astype(F32) + vec(vecs, "scale1") * out
        middle[a] = mid
        for j, part in enumerate((own, grads_came)):
            here = slice((2 * j + a) * shard, (2 * j + a + 1) * shard)
            d_after[here, :] = (vec(vecs, "scale2") * part[1, a].astype(F32)).astype(BF)
        normed, _ = norm_parts(mid)
        h2[a] = (normed * vec(vecs, "gain2") + vec(vecs, "shift2")).astype(BF)


def after_kernel(flags, act, w, keep, give):
    n = keep.shape[0]
    keep[...] = jnp.dot(act[:n], w[...], preferred_element_type=F32)
    give[...] = jnp.dot(act[n:], w[...], preferred_element_type=F32).astype(BF)


def mixed_kernel(flags, keep, came, middle, own, d_after, vecs, mixed, sums):
    rows = middle.shape[0] * middle.shape[1]
    width = middle.shape[2]
    out = keep[...] + came[...].astype(F32) + vec(vecs, "b_down")
    mid = middle[...].reshape(rows, width)
    mixed[...] = (mid + vec(vecs, "scale2") * out).astype(BF).reshape(mixed.shape)
    g = own[1].reshape(rows, width).astype(F32)
    sums[0:1, :] = jnp.sum(g * out, axis=0, keepdims=True)
    sums[1:2, :] = jnp.sum(d_after[:rows].astype(F32), axis=0, keepdims=True)


def hidden_back_kernel(flags, d_after, w_down, slope, w_up, d_before, b_sum, keep, give, total):
    i = pl.program_id(0)
    width = w_up.shape[0]
    d_act = lax.dot_general(d_after[...], w_down[...], (((1,), (1,)), ((), ())), preferred_element_type=F32)
    low = (d_act * slope[...].astype(F32)).astype(BF)
    d_before[...] = low
    b_sum[...] = jnp.sum(low.astype(F32), axis=0, keepdims=True)
    d_h2 = lax.dot_general(low, w_up[...], (((1,), (1,)), ((), ())), preferred_element_type=F32)

    @pl.when(i == 0)
    def _():
        total[...] = d_h2

    @pl.when(i > 0)
    def _():
        total[...] += d_h2

    @pl.when(i == pl.num_programs(0) - 1)
    def _():
        n = keep.shape[0]
        keep[...] = total[:n]
        give[...] = total[n:].astype(BF)


def middle_back_kernel(flags, keep_in, came, middle, own, branch, w_own, w_came, vecs, d_middle, d_branch, keep, give, sums):
    core = flags[0]
    width = middle.shape[-1]
    shard = middle.shape[1]
    weight = by_core_in(core, w_own[...].reshape(width, width // 2), w_came[...].reshape(width, width // 2))
    total = [jnp.zeros((1, width), F32)] * 4
    for a in range(2):
        here = slice(a * shard, a * shard + shard)
        normed, inverse = norm_parts(middle[a])
        d_h2 = keep_in[here, :] + came[here, :].astype(F32)
        d_mid = own[1, a].astype(F32) + norm_back(normed, inverse, d_h2, vec(vecs, "gain2"))
        d_middle[a] = d_mid
        low = (vec(vecs, "scale1") * d_mid).astype(BF)
        d_branch[here, :] = low
        back = lax.dot_general(low, weight, (((1,), (1,)), ((), ())), preferred_element_type=F32).astype(BF)
        feats = width // 2
        keep[a] = jnp.where(core == 0, back[:, :feats], back[:, feats:])
        give[a] = jnp.where(core == 0, back[:, feats:], back[:, :feats])
        parts = (d_h2 * normed, d_h2, d_mid * branch[a].astype(F32), low.astype(F32))
        total = [t + jnp.sum(p, axis=0, keepdims=True) for t, p in zip(total, parts)]
    for j in range(4):
        sums[j : j + 1, :] = total[j]


def attn_bwd_kernel(t, flags, qkv, keep, came, p, d_joint, ds_out, sums, do, dkt, dvt):
    core = flags[0]
    shard = keep.shape[1]
    cols = slice(128 * t, 128 * t + 128)
    for a in range(2):
        do[pl.ds(pl.multiple_of((2 * a + core) * shard, 16), shard), :] = keep[a, :, cols]
        do[pl.ds(pl.multiple_of((2 * a + 1 - core) * shard, 16), shard), :] = came[a, :, cols]
    rows = 144
    half = lax.broadcasted_iota(jnp.int32, (1, 128), 1) < 64
    q, k, v = slice(0, 128), slice(128, 256), slice(256, 384)
    q_turn = jnp.transpose(qkv[:, q].astype(F32)).astype(BF)
    do_turn = jnp.transpose(do[...].astype(F32)).astype(BF)

    def chunk(i, carry):
        here = pl.ds(pl.multiple_of(i * rows, 16), rows)
        do_tile = do[here, :]
        outs = []
        for sub in range(2):
            do_own = jnp.where(half if sub == 0 else ~half, do_tile, jnp.zeros_like(do_tile))
            d_prob = lax.dot_general(do_own, qkv[:, v], (((1,), (1,)), ((), ())), preferred_element_type=F32)
            prob = p[sub, here, :].astype(F32)
            weighted = prob * d_prob
            delta = jnp.sum(weighted, axis=1, keepdims=True)
            low = (weighted - prob * delta).astype(BF)
            ds_out[sub, here, :] = low
            outs.append(jnp.dot(low, qkv[:, k], preferred_element_type=F32))
        dq = jnp.where(half, outs[0], outs[1]).astype(BF).astype(F32) * 64**-0.5
        d_joint[here, 0:128] = dq.astype(BF)
        return carry + jnp.sum(dq, axis=0, keepdims=True)

    sums[0:1, :] = lax.fori_loop(0, ROW_LEN // rows, chunk, jnp.zeros((1, 128), F32))
    for sub in range(2):
        part = slice(64 * sub, 64 * sub + 64)
        dkt[part, :] = jnp.dot(q_turn[part], ds_out[sub], preferred_element_type=F32)
        dvt[part, :] = jnp.dot(do_turn[part], p[sub], preferred_element_type=F32)
    dv = jnp.transpose(dvt[...]).astype(BF)
    d_joint[:, 128:256] = jnp.transpose(dkt[...]).astype(BF)
    d_joint[:, 256:384] = dv
    sums[1:2, :] = jnp.sum(dv.astype(F32), axis=0, keepdims=True)


def h1_back_kernel(flags, first, second, third, w, keep, give):
    core = flags[0]
    width = keep.shape[-1]
    shard = keep.shape[1]
    feats = w.shape[2] // 3
    parts = []
    for t in range(3):
        for j in range(3):
            parts.append(w[:, :, feats * j + 128 * t : feats * j + 128 * t + 128])
    weight = jnp.concatenate(parts, axis=2).reshape(width, 3 * feats)
    for a in range(2):
        for mine in range(2):
            side = core if mine else 1 - core
            here = pl.ds(pl.multiple_of((2 * a + side) * shard, 16), shard)
            part = jnp.concatenate([d_joint[here, :] for d_joint in (first, second, third)], axis=1)
            out = lax.dot_general(part, weight, (((1,), (1,)), ((), ())), preferred_element_type=F32)
            if mine:
                keep[a] = out
            else:
                give[a] = out.astype(BF)


def end_kernel(flags, keep_in, came, own, d_middle, mixed, vecs, *refs):
    sums_attn, (sums_mid, sums_out, d_b_up, keep, give, sums) = refs[:-6], refs[-6:]
    core, x = flags[0], flags[1]
    width = own.shape[-1]
    total = [jnp.zeros((1, width), F32)] * 2
    for a in range(2):
        side = x if a == 0 else 1 - x
        d_h1 = keep_in[side] + came[side].astype(F32)
        normed, inverse = norm_parts(own[0, side].astype(F32))
        out = d_middle[side] + norm_back(normed, inverse, d_h1, vec(vecs, "gain1"))
        to = keep if a == 0 else give
        to[0] = mixed[side]
        to[1] = out.astype(BF)
        parts = (d_h1 * normed, d_h1)
        total = [t + jnp.sum(p, axis=0, keepdims=True) for t, p in zip(total, parts)]
    attn = jnp.concatenate([part[...] for part in sums_attn], axis=1)
    none = jnp.zeros_like(attn)
    attn = jnp.concatenate([jnp.where(core == 0, attn, none), jnp.where(core == 0, none, attn)], axis=1)
    mid, out = sums_mid[...], sums_out[...]
    rows = [attn, mid[3:4], out[1:2], *total, mid[0:3], out[0:1]]
    n_up = d_b_up.shape[1] // width
    for c in range(2):
        for j in range(n_up):
            rows.append(jnp.where(core == c, d_b_up[:, j * width : (j + 1) * width], 0.0))
    rows = jnp.concatenate(rows, axis=0)
    sums[: rows.shape[0], :] = rows
    sums[rows.shape[0] :, :] = jnp.zeros((sums.shape[0] - rows.shape[0], width), F32)


def home_kernel(flags, keep, came, mixed, d_tokens):
    x = flags[1]
    for j, out in enumerate((mixed, d_tokens)):
        out[x] = keep[j]
        out[1 - x] = came[j]


def table_kernel(meta, *refs):
    scores, (out, grid_out, strip, wide_ds) = refs[:-4], refs[-4:]
    heads = wide_ds.shape[0]
    depth = grid_out.shape[1]
    rows = 144
    lane = lax.broadcasted_iota(jnp.int32, (1, 128), 1)
    column = lax.broadcasted_iota(jnp.int32, (8, 128), 0)
    wide_ds[:, :, ROW_LEN:, :] = jnp.zeros(wide_ds.shape[:2] + (wide_ds.shape[2] - ROW_LEN, 128), F32)

    def widen(i, carry):
        here = pl.ds(pl.multiple_of(i * rows, 16), rows)
        for h in range(heads):
            part = scores[h // 2][h % 2, here, :].astype(F32)
            for kb in range(4):
                wide_ds[h, kb, here, :] = part[:, 128 * kb : 128 * kb + 128]
            wide_ds[h, 4, here, 0:64] = part[:, 512:576]
        return carry

    lax.fori_loop(0, ROW_LEN // rows, widen, 0)
    grid_out[...] = jnp.zeros_like(grid_out)
    for g in range(IMGS + 1):
        b, e, s, w, low, stop, first, last, groups = segment_loops(meta, g)

        def clear(pair, carry):
            for n in range(3):
                strip[n, 2 * pair] = jnp.zeros(strip.shape[2:], F32)
                strip[n, 2 * pair + 1] = jnp.zeros(strip.shape[2:], F32)
            return carry

        lax.fori_loop(low, stop, clear, 0)

        for size in range(1, 4):

            def lines(turn, carry, b=b, e=e, s=s, w=w, size=size, first=first, last=last):
                found = []
                for extra in range(2):
                    y = first + 2 * turn + extra
                    stop_column = jnp.where(y < last, w, 0)
                    p0 = s + jnp.minimum(y, last - 1) * w
                    off = STRIP - p0
                    j0 = off // 128
                    r = off - j0 * 128
                    for n in range(size):
                        here = pl.ds(p0 + 8 * n, 8)
                        inside = column < stop_column - 8 * n
                        moved = []
                        for kb in range(5):
                            place = lane + kb * 128
                            keep = inside & (place >= b) & (place < e)
                            piece = [jnp.where(keep, wide_ds[h, kb, here, :], 0.0) for h in range(heads)]
                            moved.append(pltpu.roll(jnp.concatenate(piece, axis=0), r, 1))
                        zero = jnp.zeros_like(moved[0])
                        moved = [zero] + moved + [zero]
                        for kb in range(6):
                            found.append((n, j0 + kb, jnp.where(lane >= r, moved[kb + 1], moved[kb])))
                for n, block, part in found:
                    strip[n, block] += part
                return carry

            lax.fori_loop(0, jnp.where(groups == size, (last - first + 1) // 2, 0), lines, 0)

        def fold(pair, carry, w=w):
            sides = [jnp.concatenate([strip[n, 2 * pair + j] for n in range(3)], axis=0) for j in range(2)]
            whole = jnp.concatenate(sides, axis=1)
            grid_out[...] += lax.dot_general(
                whole.astype(BF), strip_onehot(pair, w, depth), (((1,), (1,)), ((), ())), preferred_element_type=F32
            )
            return carry

        lax.fori_loop(low, stop, fold, 0)

    total = jnp.zeros((heads, FLAT), F32)
    for c in range(GRID):
        rows_c = [(c // 8 * heads + h) * 8 + c % 8 for h in range(heads)]
        part = jnp.concatenate([grid_out[i : i + 1, :] for i in rows_c], axis=0)
        pieces = [part, jnp.zeros((heads, FLAT - depth - SIDE * c), F32)]
        if c:
            pieces.insert(0, jnp.zeros((heads, SIDE * c), F32))
        total = total + jnp.concatenate(pieces, axis=1)
    out[...] = total


def vmem():
    return pl.BlockSpec(memory_space=pltpu.VMEM)


def smem():
    return pl.BlockSpec(memory_space=pltpu.SMEM)


def params(mib):
    return pltpu.CompilerParams(vmem_limit_bytes=mib * 1024 * 1024)


def cost(us):
    return pl.CostEstimate(flops=int(us * 600_000_000), bytes_accessed=1_000, transcendentals=0)


def strip_scratch(heads):
    return [
        pltpu.VMEM((3, BLOCKS, heads * 8, 128), F32),
        pltpu.VMEM((heads, 5, ROW_LEN + 32, 128), F32),
    ]


def hidden_kernel(flags, own, came, w, b, act, slope, h2):
    width = w.shape[0]
    n = h2.shape[0] // 2

    @pl.when(pl.program_id(0) == 0)
    def _():
        h2[:n] = own[...].reshape(n, width)
        h2[n:] = came[...].reshape(n, width)

    x = jnp.dot(h2[...], w[...], preferred_element_type=F32) + b[...].astype(F32)
    size = jnp.abs(x)
    t = 1.0 / (1.0 + (0.3275911 * 0.7071067811865476) * size)
    bell = jnp.exp(-0.5 * x * x)
    tail = t * (0.254829592 + t * (-0.284496736 + t * (1.421413741 + t * (-1.453152027 + t * 1.061405429))))
    tail = 0.5 * tail * bell
    phi = jnp.where(x >= 0, 1.0 - tail, tail)
    act[...] = (x * phi).astype(BF)
    slope[...] = (phi + x * (bell * 0.3989422804014327)).astype(BF)


def fixed(array, part=None):
    if part is None:
        return pl.BlockSpec(array.shape, lambda i: (0,) * array.ndim)
    return pl.BlockSpec((1,) + array.shape[1:], lambda i: (part,) + (0,) * (array.ndim - 1))


def join_kernel(at, places, own, came, *outs):
    n = own.shape[0]
    rows = own.shape[1]
    for out in outs:
        for high in range(out.shape[1] // rows):
            cols = slice(at, at + out.shape[2])
            at += out.shape[2]
            for i in range(n):
                out[places[i], high * rows : (high + 1) * rows, :] = own[i, :, cols]
                out[places[n + i], high * rows : (high + 1) * rows, :] = came[i, :, cols]


def first_join_kernel(places, own, came, w, vecs):
    n = own.shape[0]
    cols = w.shape[2]
    total = jnp.zeros((own.shape[1], own.shape[2] - cols), F32)
    for i in range(n):
        w[places[i]] = own[i, :, :cols]
        w[places[n + i]] = came[i, :, :cols]
        total = total + own[i, :, cols:].astype(F32) + came[i, :, cols:].astype(F32)
    for v in range(vecs.shape[0]):
        vecs[v : v + 1, :] = jnp.concatenate([total[3 * v + j : 3 * v + j + 1] for j in range(3)], axis=1)


def cat_kernel(flags, *refs):
    out, at = refs[-1], 0
    for part in refs[:-1]:
        out[at : at + part.shape[0]] = part[...]
        at += part.shape[0]


def add_kernel(flags, a, b, *outs):
    at = 0
    for out in outs:
        n = out.shape[0]
        out[...] = (a[at : at + n].astype(F32) + b[at : at + n].astype(F32)).astype(BF)
        at += n


def sum_kernel(flags, *refs):
    total = refs[0][...].astype(F32)
    for part in refs[1:-1]:
        total = total + part[...].astype(F32)
    refs[-1][...] = total.astype(refs[-1].dtype)


def grad_kernel(places, *refs):
    keep, give, full = refs[-3:]
    at = 0
    for a, b in zip(refs[:-3:2], refs[1:-3:2]):
        cols = slice(at, at + b.shape[1])
        at += b.shape[1]
        if a.shape[0] == full.shape[0]:
            full[:, cols] = (a[...].astype(F32) + b[...].astype(F32)).astype(BF)
            continue
        step = 256
        for t in range(full.shape[0] // step):
            here = slice(t * step, t * step + step)
            made = lax.dot_general(a[:, here], b[...], (((0,), (0,)), ((), ())), preferred_element_type=F32)
            full[here, cols] = made.astype(BF)
    n, rows, _ = keep.shape
    width = full.shape[1]
    block = full.shape[0] // (2 * n)
    for high in range(block // rows):
        there = slice(high * width, (high + 1) * width)
        for i in range(n):
            for out, j in ((keep, places[i]), (give, places[n + i])):
                out[i, :, there] = full[pl.ds(pl.multiple_of(j * block + high * rows, 16), rows), :]


def attn_end_kernel(flags, a, b, own, give):
    core = flags[0]
    rows = own.shape[0]
    total = a[0].astype(F32) + b[0].astype(F32)
    for t in range(3):
        for j in range(3):
            src, dst = slice((3 * t + j) * 128, (3 * t + j + 1) * 128), slice((3 * j + t) * 128, (3 * j + t + 1) * 128)
            low, high = total[:rows, src], total[rows:, src]
            own[:, dst] = jnp.where(core == 0, low, high)
            give[:, dst] = jnp.where(core == 0, high, low)


def attn_home_kernel(flags, own, came, out):
    core = flags[0]
    n = own.shape[1] // 3
    for j in range(3):
        mine, other = own[:, n * j : n * j + n], came[:, n * j : n * j + n]
        out[:, 2 * n * j : 2 * n * j + n] = jnp.where(core == 0, mine, other)
        out[:, 2 * n * j + n : 2 * n * (j + 1)] = jnp.where(core == 0, other, mine)


def proj_grad_kernel(flags, joined, d_branch, keep, give):
    core = flags[0]
    n = keep.shape[1]
    width = joined.shape[-1]
    made = lax.dot_general(
        joined[...].reshape(-1, width), d_branch[...], (((0,), (0,)), ((), ())), preferred_element_type=F32
    )
    low, high = made[:, :n], made[:, n:]
    keep[...] = jnp.where(core == 0, low, high).astype(BF)
    give[...] = jnp.where(core == 0, high, low).astype(BF)


def after(array, *others):
    others = tuple(other for other in others if other is not None)
    return lax.optimization_barrier((array,) + others)[0] if others else array


class Net:
    def __init__(self, dp, seq):
        self.dp, self.seq = dp, seq
        self.fast = dp == 8
        self.last, self.waits = None, ()
        at_seq = lax.axis_index("seq")
        self.core = at_seq % 2
        self.x = at_seq // 2
        at_dp = lax.axis_index("dp")

        def table(fn):
            pairs = []
            for d in range(dp):
                for s in range(seq):
                    d2, s2 = fn(d, s)
                    pairs.append((d * seq + s, d2 * seq + s2))
            return pairs

        self.to_core = table(lambda d, s: (d, s ^ 1))
        self.to_x = table(lambda d, s: (d, s ^ 2))
        self.flags = jnp.stack([self.core, self.x]).astype(jnp.int32)
        if self.fast:
            self.phases = (
                table(lambda d, s: (d ^ 4, s)),
                table(lambda d, s: (d ^ 2, s)),
                table(lambda d, s: (d, s ^ 2) if s % 2 == 0 else (d ^ 1, s)),
                table(lambda d, s: (d ^ 1, s) if s % 2 == 0 else (d, s ^ 2)),
            )
            rel = jnp.arange(16, dtype=jnp.int32)
            d1, d2, d3, d4 = rel % 2, (rel // 2) % 2, (rel // 4) % 2, rel // 8
            by_x = jnp.where(self.core == 0, d3, d4)
            by_y = jnp.where(self.core == 0, d4, d3)
            self.places = ((at_dp * 2 + self.x) ^ (d1 * 8 + d2 * 4 + by_y * 2 + by_x)).astype(jnp.int32)
            by_x = jnp.where(self.core == 0, d1, d4)
            by_y = jnp.where(self.core == 0, d4, d1)
            self.other_places = ((at_dp * 2 + self.x) ^ (d2 * 8 + d3 * 4 + by_y * 2 + by_x)).astype(jnp.int32)
            self.other_phases = (self.phases[2], self.phases[0], self.phases[1], self.phases[3])

    def pin(self, array):
        waits, self.waits = self.waits, ()
        return array if self.last is None else after(array, self.last, *waits)

    def call(self, kernel, us, outs, args, scratch=(), mib=8, aliases=()):
        got = pl.pallas_call(
            kernel,
            out_shape=tuple(jax.ShapeDtypeStruct(shape, kind) for shape, kind in outs),
            in_specs=[smem()] + [vmem()] * (len(args) - 1),
            out_specs=(vmem(),) * len(outs),
            scratch_shapes=list(scratch),
            compiler_params=params(mib),
            cost_estimate=cost(us),
            name=getattr(kernel, "func", kernel).__name__,
            input_output_aliases=dict(aliases),
        )(self.pin(args[0]), *args[1:])
        self.last = got[0]
        return got

    def send(self, array, pairs):
        return lax.ppermute(array, BOTH, pairs)

    def by_core(self, own, other, axis):
        first = self.core == 0
        return jnp.stack([jnp.where(first, own, other), jnp.where(first, other, own)], axis=axis)

    def pick(self, array, index, axis):
        return lax.dynamic_index_in_dim(array, index, axis, keepdims=False)

    def bias_of(self, meta, flat, segment):
        heads = flat.shape[0]
        return self.call(
            bias_kernel,
            12,
            (((2, ROW_LEN, ROW_LEN), BF),) * (heads // 2),
            (meta, flat, segment[:, None], segment[None, :]),
            scratch=[pltpu.VMEM((heads * GRID, DEPTH), F32)] + strip_scratch(heads),
            mib=16,
        )

    def table_of(self, meta, scores):
        heads = 2 * len(scores)
        return self.call(
            table_kernel,
            12,
            (((heads, FLAT), F32),),
            (meta, *scores),
            scratch=[pltpu.VMEM((heads * GRID, DEPTH), F32)] + strip_scratch(heads),
            mib=16,
        )[0]

    def hidden(self, own, came, w, b):
        rows = 2 * own.size // w.shape[0]
        depth, cols = w.shape
        tile = 256
        out = jax.ShapeDtypeStruct((rows, cols), BF)
        got = pl.pallas_call(
            hidden_kernel,
            grid=(cols // tile,),
            out_shape=(out, out, jax.ShapeDtypeStruct((rows, depth), BF)),
            in_specs=[
                smem(),
                fixed(own),
                fixed(came),
                pl.BlockSpec((depth, tile), lambda i: (0, i)),
                pl.BlockSpec((1, tile), lambda i: (0, i)),
            ],
            out_specs=(pl.BlockSpec((rows, tile), lambda i: (0, i)),) * 2 + (pl.BlockSpec((rows, depth), lambda i: (0, 0)),),
            compiler_params=params(8),
            cost_estimate=cost(6),
            name="hidden",
        )(self.pin(self.flags), own, came, w, b)
        self.last = got[0]
        return got

    def hidden_back(self, d_after, w_down, slope, w_up):
        rows, cols = slope.shape
        width = w_up.shape[0]
        tile = cols // 2
        got = pl.pallas_call(
            hidden_back_kernel,
            grid=(cols // tile,),
            out_shape=(
                jax.ShapeDtypeStruct((rows, cols), BF),
                jax.ShapeDtypeStruct((1, cols), F32),
                jax.ShapeDtypeStruct((rows // 2, width), F32),
                jax.ShapeDtypeStruct((rows // 2, width), BF),
            ),
            in_specs=[
                smem(),
                fixed(d_after),
                pl.BlockSpec((tile, width), lambda i: (i, 0)),
                pl.BlockSpec((rows, tile), lambda i: (0, i)),
                pl.BlockSpec((width, tile), lambda i: (0, i)),
            ],
            out_specs=(
                pl.BlockSpec((rows, tile), lambda i: (0, i)),
                pl.BlockSpec((1, tile), lambda i: (0, i)),
                pl.BlockSpec((rows // 2, width), lambda i: (0, 0)),
                pl.BlockSpec((rows // 2, width), lambda i: (0, 0)),
            ),
            scratch_shapes=[pltpu.VMEM((rows, width), F32)],
            compiler_params=params(14),
            cost_estimate=cost(5),
            name="hidden_back",
        )(self.pin(self.flags), d_after, w_down, slope, w_up)
        self.last = got[0]
        return got

    def gather(self, block, other=False):
        return Gather(self, block, other) if self.fast else WholeGather(self, block)

    def library_gather(self, block):
        if not self.fast:
            return WholeGather(self, block).got
        groups = [[(d * 2 + x) * 2 + c for d in range(self.dp) for x in range(2)] for c in range(2)]
        return lax.all_gather(block, BOTH, axis=0, axis_index_groups=groups)

    def reduce(self, shape, *pairs):
        if self.fast:
            return Reduce(self, shape, pairs)
        made = []
        for a, b in pairs:
            made.append((wide(a) + wide(b) if a.shape == b.shape else dot_t(a, b)).astype(BF))
        return WholeReduce(self, jnp.concatenate(made, axis=1))


class Gather:
    def __init__(self, net, block, other):
        self.net, self.got, self.step = net, block[None], 0
        if other:
            self.phases, self.places = net.other_phases, net.other_places
        else:
            self.phases, self.places = net.phases, net.places
        self.go()

    def go(self):
        self.came = self.net.send(self.got, self.phases[self.step])

    def next(self):
        out = ((2 * self.got.shape[0],) + self.got.shape[1:], BF)
        self.got = self.net.call(cat_kernel, 0.6, (out,), (self.net.flags, self.got, self.came))[0]
        self.step += 1
        self.go()

    def join(self, *shapes, at=0):
        outs = [((2 * self.got.shape[0],) + shape, BF) for shape in shapes]
        kernel = functools.partial(join_kernel, at)
        return self.net.call(kernel, 0.7, outs, (self.places, self.got, self.came))

    def first_join(self, cols):
        _, rows, width = self.got.shape
        outs = (((2 * self.got.shape[0], rows, cols), BF), ((rows // 3, 3 * (width - cols)), F32))
        return self.net.call(first_join_kernel, 0.7, outs, (self.places, self.got, self.came))


class WholeGather:
    def __init__(self, net, block):
        block = lax.all_gather(block, "dp", axis=0)
        other = net.send(block, net.to_x)
        first = net.x == 0
        block = jnp.stack([jnp.where(first, block, other), jnp.where(first, other, block)], axis=1)
        self.got = block.reshape((2 * net.dp,) + block.shape[2:])

    def next(self):
        pass

    def join(self, *shapes, at=0):
        return (self.got[:, :, at : at + shapes[0][1]],)


class Reduce:
    def __init__(self, net, shape, pairs):
        self.net, self.step = net, 3
        arrays = [array for pair in pairs for array in pair]
        depth = pairs[0][0].shape[0] if pairs[0][0].shape == pairs[0][1].shape else pairs[0][0].shape[1]
        width = sum(b.shape[1] for _, b in pairs)
        out = ((8,) + shape, BF)
        self.keep, self.give = net.call(
            grad_kernel, 3, (out, out), (net.places, *arrays), scratch=[pltpu.VMEM((depth, width), BF)]
        )
        self.go()

    def go(self):
        self.came = self.net.send(self.give, self.net.phases[self.step])

    def next(self):
        out = ((self.keep.shape[0] // 2,) + self.keep.shape[1:], BF)
        self.keep, self.give = self.net.call(add_kernel, 1, (out, out), (self.net.flags, self.keep, self.came))
        self.step -= 1
        self.go()

    def end(self):
        out = ((1,) + self.keep.shape[1:], F32)
        return self.net.call(sum_kernel, 0.6, (out,), (self.net.flags, self.keep, self.came))[0][0]


class WholeReduce:
    def __init__(self, net, full):
        blocks = full.reshape((net.dp, 2, -1) + full.shape[1:])
        came = net.send(net.pick(blocks, 1 - net.x, 1), net.to_x)
        summed = net.pick(blocks, net.x, 1).astype(F32) + came.astype(F32)
        self.sum = lax.psum_scatter(summed, "dp", scatter_dimension=0, tiled=False)

    def next(self):
        pass

    def end(self):
        return self.sum


class Total:
    def __init__(self, net, array):
        self.net, self.sum, self.step = net, array, 0
        if net.fast:
            self.came = net.send(array, net.phases[0])
        else:
            self.sum = lax.psum(array + net.send(array, net.to_x), "dp")

    def next(self):
        if self.net.fast:
            out = (self.sum.shape, F32)
            self.sum = self.net.call(sum_kernel, 0.6, (out,), (self.net.flags, self.sum, self.came))[0]
            self.step += 1
            if self.step < 4:
                self.came = self.net.send(self.sum, self.net.phases[self.step])


def wide(array):
    return array.astype(F32)


def dot(a, b):
    return jnp.dot(a, b, preferred_element_type=F32)


def dot_t(a, b):
    return lax.dot_general(a, b, (((0,), (0,)), ((), ())), preferred_element_type=F32)


def local(
    dp,
    seq,
    tokens,
    image_lengths,
    grid_widths,
    qkv_weight,
    q_bias,
    v_bias,
    proj_weight,
    proj_bias,
    fc1_weight,
    fc1_bias,
    fc2_weight,
    fc2_bias,
    norm1_gain,
    norm1_bias,
    norm2_gain,
    norm2_bias,
    scale1,
    scale2,
    bias_table,
    out_grad,
):
    net = Net(dp, seq)
    call, flags, core, at_x = net.call, net.flags, net.core, net.x
    row_count, shard, width = tokens.shape
    heads = bias_table.shape[1]
    own_heads = heads // 2
    own_feats = width // 2
    n_dev = dp * seq
    chips = n_dev // 2
    rows_w = width // n_dev
    ff = fc2_weight.shape[0] * n_dev
    rows_f = ff // n_dev
    at = lax.axis_index("dp") * seq + lax.axis_index("seq")
    at_chip = lax.axis_index("dp") * 2 + at_x

    lanes = jnp.arange(width, dtype=jnp.int32)
    spots = (lanes[None] // rows_w == at) & (lanes[None] % rows_w == jnp.arange(rows_w, dtype=jnp.int32)[:, None])
    vecs = [q_bias, v_bias, proj_bias, fc2_bias, norm1_gain, norm1_bias, norm2_gain, norm2_bias, scale1, scale2]
    n_vec = len(vecs)
    placed = dot(jnp.stack(vecs), spots.astype(BF)).astype(BF)
    n_up = ff // 2 // width
    lanes_up = jnp.arange(ff // 2, dtype=jnp.int32)
    spots_up = (lanes_up[None] // rows_f == at_chip) & (lanes_up[None] % rows_f == jnp.arange(rows_f, dtype=jnp.int32)[:, None])
    placed_up = dot(fc1_bias[None], spots_up.astype(BF)).astype(BF).reshape(n_up, width)
    mine = (jnp.arange(2) == core)[:, None, None]
    placed_up = jnp.where(mine, placed_up[None], jnp.zeros((), BF)).reshape(2 * n_up, width)
    placed = jnp.concatenate([placed, placed_up, jnp.zeros((16 - n_vec - 2 * n_up, width), BF)])

    low = ((rows_w, 3 * own_feats), BF)
    keep, give = call(split_kernel, 0.5, (low, low), (flags, qkv_weight))
    attn_block = net.by_core(keep, net.send(give, net.to_core), 0).reshape(2 * rows_w, 3 * own_feats)
    placed = placed + net.send(placed, net.to_core)
    if net.fast:
        attn_block = jnp.concatenate([attn_block, placed.reshape(48, 256)], axis=1)
    attn_chain = net.gather(attn_block)
    down_block = fc2_weight if not net.fast else jnp.concatenate([fc2_weight[: 2 * rows_w], fc2_weight[2 * rows_w :]], axis=1)
    down_chain = net.gather(after(down_block, attn_block), True)

    first_came = getattr(attn_chain, "came", None)
    their_tokens, their_grad = after(tokens, attn_block), after(out_grad, attn_block)
    theirs = jnp.stack([net.pick(their_tokens, 1 - at_x, 0), net.pick(their_grad, 1 - at_x, 0)])
    token_came = net.send(theirs, net.to_x)
    proj_view = after(proj_weight, first_came).reshape(rows_w, 2, own_feats)
    fc1_view = after(fc1_weight, first_came).reshape(rows_w, chips, 2, rows_f)
    views = []
    for index in (core, 1 - core):
        up = net.pick(fc1_view, index, 2).reshape(rows_w, ff // 2)
        views.append(jnp.concatenate([up, net.pick(proj_view, index, 1)], axis=1))
    up_came = net.send(views[1], net.to_core)

    lengths = net.pick(image_lengths, at_x, 0)
    widths = net.pick(grid_widths, at_x, 0)
    meta, segment = layout(after(lengths, attn_block), after(widths, attn_block))
    flat = jnp.transpose(after(bias_table, attn_block).reshape(SIDE, SIDE, heads), (2, 1, 0)).reshape(heads, SIDE * SIDE)
    flat = jnp.pad(wide(lax.dynamic_slice_in_dim(flat, core * own_heads, own_heads)), ((0, 0), (0, FLAT - SIDE * SIDE)))

    chunk = (2, shard, width)
    attn_chain.next()
    (up_block,) = call(stack_kernel, 0.5, (((2 * rows_w, ff // 2 + own_feats), BF),), (flags, views[0], up_came))
    up_chain = net.gather(up_block)
    attn_chain.next()
    (both,) = call(start_kernel, 0.5, (((2,) + chunk, BF),), (flags, tokens, out_grad, token_came))
    both_came = net.send(both, net.to_core)
    attn_chain.next()
    up_chain.next()
    down_chain.next()
    biases = net.bias_of(meta, flat, segment)
    down_chain.next()
    up_chain.next()
    if net.fast:
        w_qkv, vectors = attn_chain.first_join(3 * own_feats)
    else:
        (w_qkv,) = attn_chain.join((2 * rows_w, 3 * own_feats))
        vectors = Total(net, wide(placed)).sum

    row = (ROW_LEN, 128)
    part_heads = (2, shard, 128)
    square = (2, ROW_LEN, ROW_LEN)
    pairs, keeps, cames = [], [], []
    for t, bias in enumerate(biases):
        outs = ((square, BF), (part_heads, BF), (part_heads, BF))
        outs = (((ROW_LEN, 384), BF),) + ((((1, ff // 2), F32),) if t == 0 else ()) + outs
        if t == 0:
            outs = outs + (((ROW_LEN, width), BF),)
            args = (flags, both, both_came, w_qkv, vectors, bias)
        else:
            args = (flags, h1, w_qkv, vectors, bias)
        alias = {len(args) - 1: 2 if t == 0 else 1}
        got = call(functools.partial(attn_fwd_kernel, t == 0, t), 5, outs, args, scratch=[pltpu.VMEM(row, BF)], aliases=alias)
        if t == 0:
            b_up, h1 = got[1], got[5]
            got = got[:1] + got[2:]
        pairs.append(got[:2])
        keeps.append(got[2])
        cames.append(net.send(got[3], net.to_core))
        if t == 0:
            up_chain.next()
    down_chain.next()
    (pj_own,) = up_chain.join((2 * rows_w, own_feats), at=ff // 2)
    pj_came = net.send(pj_own, net.to_core)
    (fc1_all,) = up_chain.join((2 * rows_w, ff // 2))
    joined, branch, middle, h2, d_after = call(
        proj_kernel,
        3,
        ((chunk, BF), (chunk, BF), (chunk, F32), (chunk, BF), ((ROW_LEN, width), BF)),
        (flags, *keeps, *cames, pj_own, pj_came, both, both_came, vectors),
    )
    h2_came = net.send(h2, net.to_core)
    w_up = fc1_all.reshape(width, ff // 2)
    act, slope, h2_all = net.hidden(h2, h2_came, w_up, b_up)
    down_sum = net.reduce((rows_f, width), (act, d_after))
    w_down = down_chain.join((rows_f, width))[0].reshape(ff // 2, width)
    d_before, d_b_up, keep, give = net.hidden_back(d_after, w_down, slope, w_up)
    mid_came = net.send(give, net.to_core)
    own = 2 * shard
    after_keep, after_give = call(after_kernel, 2, (((own, width), F32), ((own, width), BF)), (flags, act, w_down))
    after_came = net.send(after_give, net.to_core)
    half = (2, shard, own_feats)
    d_middle, d_branch, keep, give, sums_mid = call(
        middle_back_kernel,
        3,
        ((chunk, F32), ((own, width), BF), (half, BF), (half, BF), ((4, width), F32)),
        (flags, keep, mid_came, middle, both, branch, pj_own, pj_came, vectors),
    )
    heads_came = net.send(give, net.to_core)
    out = ((width, own_feats), BF)
    proj_keep, proj_give = call(proj_grad_kernel, 2, (out, out), (flags, joined, d_branch))
    proj_came = net.send(proj_give, net.to_core)

    d_joints, scores, sums_attn = [], [], []
    for t, (qkv, prob) in enumerate(pairs):
        d_joint, ds, sums = call(
            functools.partial(attn_bwd_kernel, t),
            5,
            (((ROW_LEN, 384), BF), (square, BF), ((2, 128), F32)),
            (flags, qkv, keep, heads_came, prob),
            scratch=[pltpu.VMEM(row, BF), pltpu.VMEM((128, ROW_LEN), F32), pltpu.VMEM((128, ROW_LEN), F32)],
        )
        d_joints.append(d_joint)
        scores.append(ds)
        sums_attn.append(sums)
        if t == 0:
            up_sum = net.reduce((2 * rows_w, ff // 2 + own_feats), (h2_all, d_before), (proj_keep, proj_came))
            down_sum.next()
        if t == 1:
            mixed, sums_out = call(
                mixed_kernel,
                2,
                ((chunk, BF), ((2, width), F32)),
                (flags, after_keep, after_came, middle, both, d_after, vectors),
            )
    attn_sum = net.reduce((2 * rows_w, 3 * own_feats), *[(h1, d_joint) for d_joint in d_joints])
    keep, give = call(h1_back_kernel, 3, ((chunk, F32), (chunk, BF)), (flags, *d_joints, w_qkv))
    h1_came = net.send(give, net.to_core)
    down_sum.next()
    up_sum.next()
    table = net.table_of(meta, scores)
    attn_sum.next()
    down_sum.next()
    up_sum.next()

    keep, give, smalls = call(
        end_kernel,
        2,
        ((chunk, BF), (chunk, BF), ((16, width), F32)),
        (flags, keep, h1_came, both, d_middle, mixed, vectors, *sums_attn, sums_mid, sums_out, d_b_up),
    )
    smalls_came = net.send(smalls, net.to_core)
    out_came = net.send(give, net.to_x)
    (smalls,) = call(sum_kernel, 0.6, (((16, width), F32),), (flags, smalls, smalls_came))
    total = Total(net, jnp.concatenate([smalls.reshape(-1, 128), table.reshape(-1, 128)]))
    total.next()
    total.next()
    up_sum.next()
    attn_sum.next()
    g_down = down_sum.end()
    mixed, tokens_grad = call(home_kernel, 1, ((chunk, BF), (chunk, BF)), (flags, keep, out_came))
    total.next()
    attn_sum.next()
    g_up = up_sum.end()
    total.next()

    def home(block, groups, cols):
        view = block.reshape(2, rows_w, groups, cols)
        came = net.send(net.pick(view, 1 - core, 0), net.to_core)
        return net.by_core(net.pick(view, core, 0), came, 2).reshape(rows_w, groups * 2 * cols)

    g_proj = home(g_up[:, ff // 2 :], 1, own_feats)
    g_up = home(g_up[:, : ff // 2], chips, rows_f)
    packed = total.sum
    sums = packed[: smalls.size // 128].reshape(smalls.shape)
    table = packed[smalls.size // 128 :].reshape(own_heads, FLAT)
    table = net.by_core(table, net.send(table, net.to_core), 0).reshape(heads, FLAT)[:, : SIDE * SIDE]
    table_grad = jnp.transpose(table.reshape(heads, SIDE, SIDE), (2, 1, 0)).reshape(SIDE * SIDE, heads)
    g_small = lax.dynamic_slice_in_dim(sums[:n_vec], at * rows_w, rows_w, 1)
    g_up_small = net.pick(sums[n_vec : n_vec + 2 * n_up].reshape(2, ff // 2), core, 0)
    g_up_small = lax.dynamic_slice_in_dim(g_up_small, at_chip * rows_f, rows_f)
    smalls = [g_small[j] for j in range(n_vec)] + [g_up_small]

    if net.fast:
        net.waits = (g_proj, g_up, table_grad, g_small, g_up_small)
        rows = ((rows_w, 3 * own_feats), F32)
        own_rows, give = call(attn_end_kernel, 0.5, (rows, rows), (flags, attn_sum.keep, attn_sum.came))
        came = net.send(give, net.to_core)
        (g_qkv,) = call(attn_home_kernel, 0.5, (((rows_w, 3 * width), F32),), (flags, own_rows, came))
    else:
        g_attn = attn_sum.end().reshape(2 * rows_w, 3, 3, 128).transpose(0, 2, 1, 3)
        g_qkv = home(g_attn.reshape(2 * rows_w, 3 * own_feats), 3, own_feats)
    g_query, g_value, g_bproj, g_bdown, g_gain1, g_shift1, g_gain2, g_shift2, g_layer1, g_layer2, g_bup = smalls
    return (
        mixed,
        tokens_grad,
        g_qkv,
        g_query,
        g_value,
        g_proj,
        g_bproj,
        g_up,
        g_bup,
        g_down,
        g_bdown,
        g_gain1,
        g_shift1,
        g_gain2,
        g_shift2,
        g_layer1,
        g_layer2,
        table_grad,
    )


def solution(mesh):
    both = P(BOTH)
    both2 = P(BOTH, None)
    act = P("dp", "seq", None)
    in_specs = (act, P("dp", None), P("dp", None), both2, both, both, both2, both, both2, both, both2)
    in_specs += (both,) * 7 + (P(), act)
    out_specs = (act, act, both2, both, both, both2, both, both2, both, both2) + (both,) * 7 + (P(),)
    body = functools.partial(local, mesh.shape["dp"], mesh.shape["seq"])
    return jax.shard_map(body, mesh=mesh, in_specs=in_specs, out_specs=out_specs, check_vma=False)
```
